32 devices in a mesh: dp: 8 (over z, x), tensor: 4 (over y, core).
Axes of the slice: x: 2, y: 2, z: 4, core: 2. Of those that a mesh axis runs over, the one named last changes fastest.
Arguments:
- tokens: bfloat16 [32768, 768], P(('dp', 'tensor')), may hold values from -6 to 6
- segment_ids: int32 [64, 512], P(('dp', 'tensor')), may hold values from 0 to 3, never falling along the last dimension, each value on 1 to 256 neighbouring positions
- w_qkv: bfloat16 [768, 2304], replicated, may hold values from -0.21875 to 0.21875
- b_qkv: float32 [2304], replicated, may hold values from -3 to 3
- conv_kernel: float32 [12, 35], replicated, may hold values from -0.125 to 0.125
- w_out: bfloat16 [768, 768], replicated, may hold values from -1.75 to 1.75
- b_out: float32 [768], replicated, may hold values from -3 to 3
- norm1_gain: float32 [768], replicated, may hold values from 0.5 to 1.5
- norm1_bias: float32 [768], replicated, may hold values from -3 to 3
- w_up: bfloat16 [768, 3072], P(None, 'tensor'), may hold values from -0.21875 to 0.21875
- b_up: bfloat16 [3072], P('tensor'), may hold values from -3 to 3
- w_down: bfloat16 [3072, 768], P('tensor'), may hold values from -0.109375 to 0.109375
- b_down: float32 [768], replicated, may hold values from -3 to 3
- norm2_gain: float32 [768], replicated, may hold values from 0.5 to 1.5
- norm2_bias: float32 [768], replicated, may hold values from -3 to 3
- cotangent: bfloat16 [32768, 768], P(('dp', 'tensor')), may hold values from -6 to 6
Outputs:
- output: bfloat16 [32768, 768], P(('dp', 'tensor'))
- grad_tokens: bfloat16 [32768, 768], P(('dp', 'tensor'))
- grad_w_qkv: float32 [768, 2304], replicated
- grad_b_qkv: float32 [2304], replicated
- grad_conv: float32 [12, 35], replicated
- grad_w_out: float32 [768, 768], replicated
- grad_b_out: float32 [768], replicated
- grad_norm1_gain: float32 [768], replicated
- grad_norm1_bias: float32 [768], replicated
- grad_w_up: float32 [768, 3072], P(None, 'tensor')
- grad_b_up: float32 [3072], P('tensor')
- grad_w_down: float32 [3072, 768], P('tensor')
- grad_b_down: float32 [768], replicated
- grad_norm2_gain: float32 [768], replicated
- grad_norm2_bias: float32 [768], replicated
The draws below stay inside these ranges and needn't reach their ends.
Inputs may be any that keep to these rules, and one draw needn't show every extreme that they name: `segment_ids`: within a packed row segment ids never fall; attention and the convolution connect only tokens of equal id in the same packed row.
All inputs are finite; a program needn't handle non-finite values.
Results may differ from the reference program's by a relative error of at most 0.015.
Values may be sent and summed in bfloat16 or wider, within the bound.
A program may use at most 320 MiB of HBM per device.

```python
import math
import jax
import jax.numpy as jnp
import numpy as np
from jax import lax

D = 768
H = 12
FF = 3072
LEN = 512
KW = 35
TAU = 8
SEQS = 64
TOKENS = 32768


def level_of(stream_key, shape, shards, low, largest):
    loudness = 1.0
    for position, shards_of in shards:
        draws = jax.random.uniform(jax.random.fold_in(jax.random.fold_in(stream_key, 6), position), (shards_of,), jnp.float32, low / len(shards), largest / len(shards))
        loudness = loudness * jnp.repeat(jnp.exp(draws), shape[position] // shards_of).reshape((-1,) + (1,) * (len(shape) - 1 - position))
    return loudness


def length_profile(number_of, total, most, slope):
    portions = [(1 << 20) // math.isqrt(grade ** slope) + 1 for grade in range(2, number_of + 1)]
    spare, counts = total - most - (number_of - 1), [1] * (number_of - 1)
    while spare > 0:
        free = [i for i in range(number_of - 1) if counts[i] < most]
        whole, remaining = sum([portions[i] for i in free]), spare
        for i in free:
            addition = min(most - counts[i], max(1, remaining * portions[i] // whole), spare)
            counts[i] = counts[i] + addition
            spare = spare - addition
    return np.array([most] + counts)


def uneven(rng, count, total, bound, slope):
    if count == 2:
        one = jax.random.randint(rng, (), max(1, total - bound), min(bound, total - 1) + 1)
        return jnp.stack([one, total - one])
    sizes = jnp.asarray(length_profile(count, total, bound, slope), jnp.int32)
    couples = (count - 1) // 2
    giver, receiver = sizes[1:1 + 2 * couples:2], sizes[2:2 + 2 * couples:2]
    slack = jnp.minimum(giver - 1, bound - receiver)
    shifted = jax.random.randint(jax.random.fold_in(rng, 1), (couples,), 0, 1 << 20) % (slack + 1)
    sizes = sizes.at[1:1 + 2 * couples:2].set(giver - shifted).at[2:2 + 2 * couples:2].set(receiver + shifted)
    return sizes[jax.random.permutation(jax.random.fold_in(rng, 2), count)]


def normal_values(stream_key, shape, deviation, reach, split=(), kind=jnp.bfloat16):
    entries = deviation * jax.random.normal(stream_key, shape, jnp.float32)
    if split:
        entries = entries * level_of(stream_key, shape, split, -0.22, 0.18)
    return jnp.clip(entries, -reach, reach).astype(kind)


def setup_inputs(seed: int = 0) -> dict:
    key_of = jax.random.split(jax.random.key(seed), 17)
    return {
        "tokens": normal_values(key_of[0], (TOKENS, D), 1.0, 6.0, ((0, 32),)),
        "segment_ids": jax.vmap(lambda own: jnp.searchsorted(jnp.cumsum(uneven(own, 4, LEN, LEN // 2, 0)), jnp.arange(LEN), side="right"))(jax.random.split(key_of[1], SEQS)).reshape((SEQS, LEN)).astype(jnp.int32),
        "w_qkv": normal_values(key_of[2], (D, 3 * D), D ** -0.5, 0.21875),
        "b_qkv": normal_values(key_of[3], (3 * D,), 0.5, 3.0, (), jnp.float32),
        "conv_kernel": normal_values(key_of[4], (H, KW), 0.02, 0.125, (), jnp.float32),
        "w_out": normal_values(key_of[5], (D, D), (D // 64) ** -0.5, 1.75),
        "b_out": normal_values(key_of[6], (D,), 0.5, 3.0, (), jnp.float32),
        "norm1_gain": jnp.clip(1.0 + 0.1 * jax.random.normal(key_of[7], (D,), jnp.float32), 0.5, 1.5),
        "norm1_bias": normal_values(key_of[8], (D,), 0.5, 3.0, (), jnp.float32),
        "w_up": normal_values(key_of[9], (D, FF), D ** -0.5, 0.21875, ((1, 4),)),
        "b_up": normal_values(key_of[10], (FF,), 0.5, 3.0, ((0, 4),)),
        "w_down": normal_values(key_of[11], (FF, D), FF ** -0.5, 0.109375, ((0, 4),)),
        "b_down": normal_values(key_of[12], (D,), 0.5, 3.0, (), jnp.float32),
        "norm2_gain": jnp.clip(1.0 + 0.1 * jax.random.normal(key_of[13], (D,), jnp.float32), 0.5, 1.5),
        "norm2_bias": normal_values(key_of[14], (D,), 0.5, 3.0, (), jnp.float32),
        "cotangent": normal_values(key_of[15], (TOKENS, D), 1.0, 6.0, ((0, 32),)),
    }


eps_norm = 1e-05
eps_unit = 1e-06
shrink = 0.95

@jax.custom_vjp
def low(v):
    return lax.optimization_barrier(v.astype(jnp.bfloat16)).astype(jnp.float32)

@jax.custom_vjp
def low_back(v):
    return v

def low_keep(v):
    return (low(v), None)

def low_pass(kept, grad):
    return (grad,)

def back_keep(v):
    return (v, None)

def back_low(kept, grad):
    return (low(grad),)
low.defvjp(low_keep, low_pass)
low_back.defvjp(back_keep, back_low)

def dot_exact(left, right):
    return jnp.dot(left, right, precision=lax.Precision.HIGHEST, preferred_element_type=jnp.float32)

def norm_forward(rows_in, norm_gain, norm_shift):
    centred = rows_in - lax.optimization_barrier(jnp.mean(rows_in, -1, keepdims=True))
    scaling = lax.rsqrt(lax.optimization_barrier(jnp.mean(centred * centred, -1, keepdims=True)) + eps_norm)
    return centred * scaling * norm_gain + norm_shift

def unit_rows(vectors):
    return vectors * lax.rsqrt(lax.optimization_barrier(jnp.sum(vectors * vectors, -1, keepdims=True)) + eps_unit)

def conv_forward(values, seg_ids, kernel):
    radius = kernel.shape[1] // 2
    length = values.shape[1]
    padded = jnp.pad(values, ((0, 0), (radius, radius), (0, 0), (0, 0)))
    padded_ids = jnp.pad(seg_ids, ((0, 0), (radius, radius)), constant_values=-1)
    summed = jnp.zeros_like(values)
    for offset in range(kernel.shape[1]):
        matched = (padded_ids[:, offset:offset + length] == seg_ids)[:, :, None, None]
        summed = summed + jnp.where(matched, padded[:, offset:offset + length], 0.0) * kernel[:, offset][:, None]
    return summed

def attend_exact(pieces):
    q_unit, k_unit, v_low, seg_ids = pieces
    cosine = low_back(shrink * jnp.einsum('qhd,khd->hqk', q_unit, k_unit, precision=lax.Precision.HIGHEST))
    matched = (seg_ids[:, None] == seg_ids[None, :])[None]
    weight = jnp.where(matched, (1.0 - jnp.arccos(cosine) / math.pi) ** TAU, 0.0)
    totals = 1.0 + lax.optimization_barrier(jnp.sum(weight, -1))
    summed = low_back(jnp.einsum('hqk,khd->qhd', low(weight), v_low, precision=lax.Precision.HIGHEST))
    return (summed, totals.T)

def block_forward(rows_in, seg_ids, w_qkv, b_qkv, conv_kernel, w_out, b_out, gain_one, shift_one, w_up, b_up, w_down, b_down, gain_two, shift_two):
    seq_count = seg_ids.shape[0]
    projected = low_back(dot_exact(rows_in, w_qkv) + b_qkv)
    split_parts = projected.reshape(seq_count, LEN, 3, H, D // H)
    queries = unit_rows(split_parts[:, :, 0])
    keys_unit = unit_rows(split_parts[:, :, 1])
    values = split_parts[:, :, 2]
    summed, totals = lax.map(jax.checkpoint(attend_exact), (low(queries), low(keys_unit), low(values), seg_ids))
    context = summed / totals[..., None] + conv_forward(values, seg_ids, conv_kernel)
    context = low(context.reshape(rows_in.shape))
    first = norm_forward(rows_in + low_back(dot_exact(context, w_out) + b_out), gain_one, shift_one)
    preact = low_back(dot_exact(low(first), w_up) + b_up)
    ffn_out = low_back(dot_exact(low(jax.nn.gelu(preact, approximate=True)), w_down) + b_down)
    return norm_forward(first + ffn_out, gain_two, shift_two)

def reference(tokens, segment_ids, w_qkv, b_qkv, conv_kernel, w_out, b_out, norm1_gain, norm1_bias, w_up, b_up, w_down, b_down, norm2_gain, norm2_bias, cotangent):
    params = tuple((weight_arg.astype(jnp.float32) for weight_arg in (w_qkv, b_qkv, conv_kernel, w_out, b_out, norm1_gain, norm1_bias, w_up, b_up, w_down, b_down, norm2_gain, norm2_bias)))
    group_count = SEQS // 8
    rows_all = tokens.astype(jnp.float32).reshape(group_count, 8 * LEN, D)
    ids_all = segment_ids.reshape(group_count, 8, LEN)
    cot_all = cotangent.astype(jnp.float32).reshape(group_count, 8 * LEN, D)

    def one_group(running, stacked):
        rows_in, seg_ids, grad_rows = stacked

        def forward(rows_arg, *weights):
            return block_forward(rows_arg, seg_ids, *weights)
        result, pullback = jax.vjp(forward, rows_in, *params)
        grads = pullback(grad_rows)
        running = tuple((total_grad + piece_grad for total_grad, piece_grad in zip(running, grads[1:])))
        return (running, (result.astype(jnp.bfloat16), grads[0].astype(jnp.bfloat16)))
    start_sums = tuple((jnp.zeros_like(weight_arg) for weight_arg in params))
    running, (outputs, grad_all) = lax.scan(one_group, start_sums, (rows_all, ids_all, cot_all))
    return (outputs.reshape(TOKENS, D), grad_all.reshape(TOKENS, D), running[0], running[1], running[2], running[3], running[4], running[5], running[6], running[7], running[8], running[9], running[10], running[11], running[12])
```

```python
import functools
import math

import jax
import jax.numpy as jnp
from jax import lax
from jax.experimental import pallas as pl
from jax.experimental.pallas import tpu as pltpu
from jax.sharding import PartitionSpec as P

F32 = jnp.float32
BF16 = jnp.bfloat16
EPS_NORM = 1e-5
EPS_UNIT = 1e-6
SHRINK = 0.95
TAU = 8
SLOPE = TAU / math.pi
ARC = (0.49999996, -0.06830509, 0.02825875, -0.01557005, 0.00864352, -0.00363107, 0.00076235)
QUAD = 256
PAIR = 128
HEAD = 64
BLK = 128
HALO = 64


def dot_nn(a, b):
    return lax.dot_general(a, b, (((1,), (0,)), ((), ())), preferred_element_type=F32)


def dot_nt(a, b):
    return lax.dot_general(a, b, (((1,), (1,)), ((), ())), preferred_element_type=F32)


def dot_tn(a, b):
    return lax.dot_general(a, b, (((0,), (0,)), ((), ())), preferred_element_type=F32)


def lanes(shape):
    return lax.broadcasted_iota(jnp.int32, shape, len(shape) - 1)


def rows(shape):
    return lax.broadcasted_iota(jnp.int32, shape, len(shape) - 2)


def head_sum(values):
    width = values.shape[-1]
    ones = (rows((width, width)) // HEAD == lanes((width, width)) // HEAD).astype(BF16)
    high = values.astype(BF16)
    low = (values - high.astype(F32)).astype(BF16)
    return dot_nn(high, ones) + dot_nn(low, ones)


def closeness_terms(cosine):
    size = jnp.abs(cosine)
    room = 1.0 - size
    inverse = lax.rsqrt(room)
    poly = jnp.full_like(size, ARC[-1])
    for coefficient in ARC[-2::-1]:
        poly = poly * size + coefficient
    small = room * inverse * poly
    close = jnp.where(cosine >= 0.0, 1.0 - small, small)
    two = close * close
    four = two * two
    slope = (four * two) * (close * inverse) * lax.rsqrt(1.0 + size)
    return four * four, slope


def head_mask(half, shape):
    return (lanes(shape) // HEAD == half).astype(BF16)


def window_of(block, blocks):
    low = max(0, block * BLK - 256)
    high = min(blocks * BLK, block * BLK + BLK + 256)
    return low, high


def band(taps, count):
    spread = jnp.broadcast_to(taps, (count, taps.shape[1]))
    return pltpu.roll(spread, 0, 1, stride=1, stride_axis=0)


def norm_stats(values):
    centred = values - jnp.mean(values, -1, keepdims=True)
    scaling = lax.rsqrt(jnp.mean(centred * centred, -1, keepdims=True) + EPS_NORM)
    return centred * scaling, scaling


def build_masks(seg_col, seg_pad, same_ref, near_ref):
    length = seg_col.shape[0]
    for start in range(0, length, BLK):
        own = seg_col[start : start + BLK]
        same_ref[start : start + BLK, :] = jnp.where(
            own == seg_pad[:, HALO : HALO + length], 1.0, 0.0
        ).astype(BF16)
        near_ref[start // BLK] = jnp.where(
            own == seg_pad[:, start : start + 2 * BLK], 1.0, 0.0
        ).astype(BF16)


def build_near(seg_col, seg_pad, near_ref):
    length = seg_col.shape[0]
    for start in range(0, length, BLK):
        own = seg_col[start : start + BLK]
        near_ref[start // BLK] = jnp.where(
            own == seg_pad[:, start : start + 2 * BLK], 1.0, 0.0
        ).astype(BF16)


def attend_kernel(
    x_ref, col_ref, pad_ref, wq_ref, wk_ref, wv_ref, bq_ref, bk_ref, bv_ref, tap_ref, wo_ref, bo_ref,
    q_ref, k_ref, v_ref, sq_ref, sk_ref, w_ref, s_ref, att_ref, inv_ref, ctx_ref, res_ref,
    same_ref, near_ref, vv_ref,
):
    quad = pl.program_id(1)
    length = x_ref.shape[0]
    blocks = length // BLK

    @pl.when(quad == 0)
    def _():
        build_masks(col_ref[...], pad_ref[0], same_ref, near_ref)
        for half in range(2):
            edge = jnp.zeros((HALO, 2 * PAIR), BF16)
            vv_ref[half, :HALO] = edge
            vv_ref[half, HALO + length :] = edge
            vv_ref[half, HALO : HALO + length, PAIR:] = head_mask(half, (length, PAIR))

    for start in range(0, length, BLK):
        here = slice(start, start + BLK)
        x = x_ref[here]
        for w, b, unit, scale, factor in (
            (wq_ref, bq_ref, q_ref, sq_ref, SHRINK),
            (wk_ref, bk_ref, k_ref, sk_ref, 1.0),
        ):
            part = dot_nn(x, w[...]) + b[...]
            scaling = lax.rsqrt(head_sum(part * part) + EPS_UNIT)
            unit[here] = (part * (scaling * factor)).astype(BF16)
            scale[here] = scaling.astype(BF16)
        v_ref[here] = (dot_nn(x, wv_ref[...]) + bv_ref[...]).astype(BF16)

    def one_pair(pair, carry):
        at = pl.ds(pl.multiple_of(pair * PAIR, PAIR), PAIR)
        v = v_ref[:, at]
        for half in range(2):
            vv_ref[half, HALO : HALO + length, :PAIR] = v * head_mask(half, (length, PAIR))
        for block in range(blocks):
            here = slice(block * BLK, block * BLK + BLK)
            low, high = window_of(block, blocks)
            q = q_ref[here, at]
            total = jnp.zeros((BLK, 2 * PAIR), F32)
            near = jnp.zeros((BLK, PAIR), F32)
            for half in range(2):
                head = pair * 2 + half
                q_half = q * head_mask(half, (BLK, PAIR))
                for start in range(low, high, KCH):
                    stop = min(start + KCH, high)
                    cosine = dot_nt(q_half, k_ref[start:stop, at])
                    weight, slope = closeness_terms(cosine)
                    same = same_ref[here, start:stop]
                    weight = weight.astype(BF16) * same
                    w_ref[0, head, here, start:stop] = weight
                    s_ref[0, head, here, start:stop] = slope.astype(BF16) * same
                    total += dot_nn(weight, vv_ref[half, HALO + start : HALO + stop])
                if low > 0:
                    w_ref[0, head, here, :low] = jnp.zeros((BLK, low), BF16)
                if high < length:
                    w_ref[0, head, here, high:] = jnp.zeros((BLK, length - high), BF16)
                taps = band(tap_ref[0, pl.ds(head, 1)], BLK).astype(BF16) * near_ref[block]
                near += dot_nn(taps, vv_ref[half, block * BLK : block * BLK + 2 * BLK, :PAIR])
            inverse = 1.0 / (1.0 + total[:, PAIR:])
            attended = total[:, :PAIR] * inverse
            att_ref[here, at] = attended.astype(BF16)
            inv_ref[here, at] = inverse.astype(BF16)
            ctx_ref[here, at] = (attended + near).astype(BF16)
        return carry

    lax.fori_loop(0, QUAD // PAIR, one_pair, 0)

    for start in range(0, length, BLK):
        here = slice(start, start + BLK)
        grown = dot_nn(ctx_ref[here], wo_ref[...])

        @pl.when(quad == 0)
        def _():
            res_ref[here] = grown + x_ref[here].astype(F32) + bo_ref[...]

        @pl.when(quad > 0)
        def _():
            res_ref[here] += grown


KCH = 256


def attend(tokens, seg_col, seg_pad, w_qkv, b_qkv, taps, w_out, b_out, length):
    count, width = tokens.shape
    seqs = count // length
    quads = width // QUAD
    heads = width // HEAD
    per = QUAD // HEAD
    blocks = length // BLK
    own = pl.BlockSpec((length, QUAD), lambda r, p: (r, p))
    act = jax.ShapeDtypeStruct((count, width), BF16)
    big = jax.ShapeDtypeStruct((seqs, heads, length, length), BF16)
    big_spec = pl.BlockSpec((1, per, length, length), lambda r, p: (r, p, 0, 0))

    def part(rows_of, k):
        return pl.BlockSpec((rows_of, QUAD), lambda r, p, k=k: (0, p + k * quads))

    return pl.pallas_call(
        attend_kernel,
        grid=(seqs, quads),
        in_specs=[
            pl.BlockSpec((length, width), lambda r, p: (r, 0)),
            pl.BlockSpec((length, 1), lambda r, p: (r, 0)),
            pl.BlockSpec((1, 1, length + 2 * HALO), lambda r, p: (r, 0, 0)),
            part(width, 0), part(width, 1), part(width, 2),
            part(1, 0), part(1, 1), part(1, 2),
            pl.BlockSpec((1, per, 2 * BLK), lambda r, p: (p, 0, 0)),
            pl.BlockSpec((QUAD, width), lambda r, p: (p, 0)),
            pl.BlockSpec((1, width), lambda r, p: (0, 0)),
        ],
        out_specs=[own] * 5 + [big_spec] * 2 + [own] * 3 + [pl.BlockSpec((length, width), lambda r, p: (r, 0))],
        out_shape=[act] * 5 + [big] * 2 + [act] * 3 + [jax.ShapeDtypeStruct((count, width), F32)],
        scratch_shapes=[
            pltpu.VMEM((length, length), BF16),
            pltpu.VMEM((blocks, BLK, 2 * BLK), BF16),
            pltpu.VMEM((2, length + 2 * HALO, 2 * PAIR), BF16),
        ],
        compiler_params=pltpu.CompilerParams(vmem_limit_bytes=56 * 2**20),
        name="attend_forward",
    )(tokens, seg_col, seg_pad, w_qkv, w_qkv, w_qkv, b_qkv, b_qkv, b_qkv, taps, w_out, b_out)

GELU_A = math.sqrt(2.0 / math.pi)
GELU_B = 0.044715
TILE = 256


def gelu_terms(pre):
    square = pre * pre
    swing = jnp.tanh(pre * (GELU_A + GELU_A * GELU_B * square))
    gate = 0.5 + 0.5 * swing
    steep = GELU_A + 3.0 * GELU_A * GELU_B * square
    return pre * gate, gate + 0.5 * pre * (1.0 - swing * swing) * steep


def norm_backward(grad_out, unit, scaling, gain):
    grad_unit = grad_out * gain
    return scaling * (
        grad_unit
        - jnp.mean(grad_unit, -1, keepdims=True)
        - unit * jnp.mean(grad_unit * unit, -1, keepdims=True)
    )


def column_sum(values):
    return jnp.sum(values, 0, keepdims=True)


def ffn_kernel(
    res_ref, cot_ref, ctx_ref, wo_ref, gain1_ref, shift1_ref, gain2_ref, shift2_ref, bd_ref, bu_ref, wu_ref, wd_ref,
    out_ref, dproj_ref, dctx_ref, gwo_ref, gu_ref, gd_ref, gbu_ref, gbd_ref, gg2_ref, gs2_ref, gg1_ref, gs1_ref, gbo_ref,
    low_ref, acc_ref, hid_ref, slope_ref, dffn_ref, dpre_ref,
):
    parts = pl.num_programs(0) // 2
    step = pl.program_id(0)
    count, width = res_ref.shape
    tiles = count // TILE
    f = lax.rem(step, parts)

    def at(t):
        return pl.ds(pl.multiple_of(t * TILE, TILE), TILE)

    @pl.when(step == 0)
    def _():
        def one(t, carry):
            unit, _ = norm_stats(res_ref[at(t)])
            low_ref[at(t)] = (unit * gain1_ref[...] + shift1_ref[...]).astype(BF16)
            return carry

        lax.fori_loop(0, tiles, one, 0)

    @pl.when(step < parts)
    def _():
        def one(t, carry):
            pre = dot_nn(low_ref[at(t)], wu_ref[0]) + bu_ref[0].astype(F32)
            hidden, slope = gelu_terms(pre)
            hidden = hidden.astype(BF16)
            hid_ref[f, at(t)] = hidden
            slope_ref[f, at(t)] = slope.astype(BF16)
            grown = dot_nn(hidden, wd_ref[0])

            @pl.when(step == 0)
            def _():
                acc_ref[at(t)] = grown

            @pl.when(step > 0)
            def _():
                acc_ref[at(t)] += grown

            return carry

        lax.fori_loop(0, tiles, one, 0)

    @pl.when(step == parts)
    def _():
        def one(t, sums):
            unit, _ = norm_stats(res_ref[at(t)])
            first = unit * gain1_ref[...] + shift1_ref[...]
            unit, scaling = norm_stats(first + acc_ref[at(t)] + bd_ref[...])
            out_ref[at(t)] = (unit * gain2_ref[...] + shift2_ref[...]).astype(BF16)
            grad = cot_ref[at(t)].astype(F32)
            d_res = norm_backward(grad, unit, scaling, gain2_ref[...])
            d_ffn = d_res.astype(BF16)
            acc_ref[at(t)] = d_res
            dffn_ref[at(t)] = d_ffn
            return (
                sums[0] + column_sum(grad * unit),
                sums[1] + column_sum(grad),
                sums[2] + column_sum(d_ffn.astype(F32)),
            )

        zero = jnp.zeros((1, width), F32)
        gg2_ref[...], gs2_ref[...], gbd_ref[...] = lax.fori_loop(0, tiles, one, (zero, zero, zero))

    @pl.when(step >= parts)
    def _():
        def one(t, total):
            d_hidden = dot_nt(dffn_ref[at(t)], wd_ref[0])
            d_pre = (d_hidden * slope_ref[f, at(t)].astype(F32)).astype(BF16)
            dpre_ref[at(t)] = d_pre
            acc_ref[at(t)] += dot_nt(d_pre, wu_ref[0])
            return total + column_sum(d_pre.astype(F32))

        share = dpre_ref.shape[1]
        gbu_ref[0] = lax.fori_loop(0, tiles, one, jnp.zeros((1, share), F32))
        for start in range(0, width, TILE):
            cut = slice(start, start + TILE)
            gu_ref[0, cut] = dot_tn(low_ref[:, cut], dpre_ref[...]).astype(BF16)
        piece = min(TILE, share)
        for start in range(0, share, piece):
            cut = slice(start, start + piece)
            gd_ref[0, cut] = dot_tn(hid_ref[f, :, cut], dffn_ref[...]).astype(BF16)

    @pl.when(step == 2 * parts - 1)
    def _():
        def one(t, sums):
            unit, scaling = norm_stats(res_ref[at(t)])
            grad = acc_ref[at(t)]
            d_proj = norm_backward(grad, unit, scaling, gain1_ref[...]).astype(BF16)
            dproj_ref[at(t)] = d_proj
            dctx_ref[at(t)] = dot_nt(d_proj, wo_ref[...]).astype(BF16)
            return (
                sums[0] + column_sum(grad * unit),
                sums[1] + column_sum(grad),
                sums[2] + column_sum(d_proj.astype(F32)),
            )

        zero = jnp.zeros((1, width), F32)
        gg1_ref[...], gs1_ref[...], gbo_ref[...] = lax.fori_loop(0, tiles, one, (zero, zero, zero))
        for start in range(0, width, TILE):
            cut = slice(start, start + TILE)
            gwo_ref[cut] = dot_tn(ctx_ref[:, cut], dproj_ref[...]).astype(BF16)


def feed_forward(res, cot, ctx, w_out, gain1, shift1, gain2, shift2, b_down, b_up, w_up, w_down):
    count, width = res.shape
    parts, _, share = w_up.shape

    def whole(*shape):
        return pl.BlockSpec(shape, lambda s: (0,) * len(shape), pipeline_mode=pl.Buffered(1))

    def per_part(*shape):
        return pl.BlockSpec((1,) + shape, lambda s: (lax.rem(s, parts),) + (0,) * len(shape))

    def late_part(*shape):
        return pl.BlockSpec((1,) + shape, lambda s: (jnp.maximum(s - parts, 0),) + (0,) * len(shape))

    act = jax.ShapeDtypeStruct((count, width), BF16)
    row = jax.ShapeDtypeStruct((1, width), F32)
    return pl.pallas_call(
        ffn_kernel,
        grid=(2 * parts,),
        in_specs=[whole(count, width)] * 3
        + [whole(width, width)]
        + [whole(1, width)] * 5
        + [per_part(1, share), per_part(width, share), per_part(share, width)],
        out_specs=[whole(count, width)] * 3
        + [whole(width, width), late_part(width, share), late_part(share, width), late_part(1, share)]
        + [whole(1, width)] * 6,
        out_shape=[act] * 3
        + [
            jax.ShapeDtypeStruct((width, width), BF16),
            jax.ShapeDtypeStruct((parts, width, share), BF16),
            jax.ShapeDtypeStruct((parts, share, width), BF16),
            jax.ShapeDtypeStruct((parts, 1, share), F32),
        ]
        + [row] * 6,
        scratch_shapes=[
            pltpu.VMEM((count, width), BF16),
            pltpu.VMEM((count, width), F32),
            pltpu.VMEM((parts, count, share), BF16),
            pltpu.VMEM((parts, count, share), BF16),
            pltpu.VMEM((count, width), BF16),
            pltpu.VMEM((count, share), BF16),
        ],
        compiler_params=pltpu.CompilerParams(vmem_limit_bytes=60 * 2**20),
        name="feed_forward",
    )(res, cot, ctx, w_out, gain1, shift1, gain2, shift2, b_down, b_up, w_up, w_down)


def attend_back_kernel(
    dctx_ref, att_ref, inv_ref, q_ref, k_ref, v_ref, sq_ref, sk_ref, w_ref, s_ref, x_ref, col_ref, pad_ref,
    wq_ref, wk_ref, wv_ref, tap_ref, flip_ref, dproj_ref,
    gw_ref, gb_ref, gconv_ref, gt_ref,
    near_ref, vv_ref, dpad_ref, dcos_ref, dq_ref, dk_ref, dv_ref, joined_ref, gwacc_ref, gtacc_ref, conv_ref,
):
    quad, row = pl.program_id(0), pl.program_id(1)
    quads, seqs = pl.num_programs(0), pl.num_programs(1)
    length = x_ref.shape[0]
    blocks = length // BLK
    inside = slice(HALO, HALO + length)

    build_near(col_ref[...], pad_ref[0], near_ref)
    for half in range(2):
        edge = jnp.zeros((HALO, PAIR), BF16)
        for ref in (vv_ref, dpad_ref):
            ref[half, :HALO, :PAIR] = edge
            ref[half, HALO + length :, :PAIR] = edge
        vv_ref[half, inside, PAIR:] = head_mask(half, (length, PAIR))

    @pl.when(row == 0)
    def _():
        conv_ref[...] = jnp.zeros_like(conv_ref)
        gwacc_ref[...] = jnp.zeros_like(gwacc_ref)
        gb_ref[...] = jnp.zeros_like(gb_ref)

    def one_pair(pair, carry):
        at = pl.ds(pl.multiple_of(pair * PAIR, PAIR), PAIR)
        inverse = inv_ref[:, at].astype(F32)
        d_ctx = dctx_ref[:, at]
        d_summed = (d_ctx.astype(F32) * inverse).astype(BF16)
        d_total = (-d_summed.astype(F32) * att_ref[:, at].astype(F32)).astype(BF16)
        both = jnp.concatenate([d_summed, d_total], 1)
        dk = jnp.zeros((length, PAIR), F32)
        dv = jnp.zeros((length, PAIR), F32)
        for half in range(2):
            head = pair * 2 + half
            mask = head_mask(half, (length, PAIR))
            vv_ref[half, inside, :PAIR] = v_ref[:, at] * mask
            dpad_ref[half, inside] = d_ctx * mask
            k_half = k_ref[:, at] * mask
            for block in range(blocks):
                here = slice(block * BLK, block * BLK + BLK)
                low, high = window_of(block, blocks)
                d_weight = dot_nt(both[here], vv_ref[half, HALO + low : HALO + high])
                d_cos = d_weight.astype(BF16) * s_ref[0, head, here, low:high]
                dcos_ref[here, low:high] = d_cos
                if low > 0:
                    dcos_ref[here, :low] = jnp.zeros((BLK, low), BF16)
                if high < length:
                    dcos_ref[here, high:] = jnp.zeros((BLK, length - high), BF16)
                grown = dot_nn(d_cos, k_half[low:high])
                if half == 0:
                    dq_ref[here] = grown
                else:
                    dq_ref[here] += grown
                window = slice(block * BLK, block * BLK + 2 * BLK)
                near = near_ref[block]
                taps = band(flip_ref[0, pl.ds(head, 1)], BLK).astype(BF16) * near
                grown = dot_nn(taps, dpad_ref[half, window])
                if half == 0:
                    dv_ref[here] = grown
                else:
                    dv_ref[here] += grown
                conv_ref[head] += near.astype(F32) * dot_nt(d_ctx[here], vv_ref[half, window, :PAIR])
            dk += dot_tn(dcos_ref[...], q_ref[:, at] * mask)
            dv += dot_tn(w_ref[0, head], d_summed * mask)
        dv_ref[...] += dv
        grad = SLOPE * dq_ref[...]
        unit = q_ref[:, at].astype(F32)
        d_query = sq_ref[:, at].astype(F32) * (SHRINK * grad - unit * (head_sum(grad * unit) / SHRINK))
        grad = SLOPE * dk
        unit = k_ref[:, at].astype(F32)
        d_key = sk_ref[:, at].astype(F32) * (grad - unit * head_sum(grad * unit))
        for part, values in enumerate((d_query, d_key, dv_ref[...])):
            joined_ref[:, pl.ds(pl.multiple_of(part * QUAD + pair * PAIR, PAIR), PAIR)] = values.astype(BF16)
        return carry

    lax.fori_loop(0, QUAD // PAIR, one_pair, 0)

    gb_ref[0] += column_sum(joined_ref[...].astype(F32))
    for start in range(0, gwacc_ref.shape[0], TILE):
        cut = slice(start, start + TILE)
        gwacc_ref[cut] += dot_tn(x_ref[:, cut], joined_ref[...])
    for start in range(0, length, TILE):
        here = pl.ds(pl.multiple_of(row * length + start, TILE), TILE)
        cut = slice(start, start + TILE)
        grown = (
            dot_nt(joined_ref[cut, :QUAD], wq_ref[...])
            + dot_nt(joined_ref[cut, QUAD : 2 * QUAD], wk_ref[...])
            + dot_nt(joined_ref[cut, 2 * QUAD :], wv_ref[...])
        )

        @pl.when(quad == 0)
        def _():
            gtacc_ref[here] = grown + dproj_ref[cut].astype(F32)

        @pl.when(quad > 0)
        def _():
            gtacc_ref[here] += grown

    @pl.when(quad == quads - 1)
    def _():
        gt_ref[...] = gtacc_ref[pl.ds(pl.multiple_of(row * length, TILE), length)].astype(BF16)

    @pl.when(row == seqs - 1)
    def _():
        gw_ref[0] = gwacc_ref[...].astype(BF16)
        for head in range(QUAD // HEAD):
            sums = conv_ref[head]
            high = sums.astype(BF16)
            turn = (rows((BLK, BLK)) + lanes((BLK, BLK)) == BLK - 1).astype(BF16)
            turned = dot_nn(turn, high) + dot_nn(turn, (sums - high.astype(F32)).astype(BF16))
            turned = pltpu.roll(turned, 0, 1, stride=1, stride_axis=0)
            gconv_ref[0, head : head + 1] = column_sum(turned)


def attend_back(dctx, att, inv, q, k, v, sq, sk, weight, slope, tokens, seg_col, seg_pad, w_qkv, taps, flipped, dproj, length):
    count, width = tokens.shape
    seqs = count // length
    quads = width // QUAD
    per = QUAD // HEAD
    blocks = length // BLK
    own = pl.BlockSpec((length, QUAD), lambda p, r: (r, p))
    big = pl.BlockSpec((1, per, length, length), lambda p, r: (r, p, 0, 0))
    wide = pl.BlockSpec((length, width), lambda p, r: (r, 0))

    def part(k):
        return pl.BlockSpec((width, QUAD), lambda p, r, k=k: (0, p + k * quads))

    taps_spec = pl.BlockSpec((1, per, 2 * BLK), lambda p, r: (p, 0, 0))
    return pl.pallas_call(
        attend_back_kernel,
        grid=(quads, seqs),
        in_specs=[own] * 8
        + [big] * 2
        + [
            wide,
            pl.BlockSpec((length, 1), lambda p, r: (r, 0)),
            pl.BlockSpec((1, 1, length + 2 * HALO), lambda p, r: (r, 0, 0)),
            part(0), part(1), part(2),
            taps_spec, taps_spec,
            wide,
        ],
        out_specs=[
            pl.BlockSpec((1, width, 3 * QUAD), lambda p, r: (p, 0, 0)),
            pl.BlockSpec((1, 1, 3 * QUAD), lambda p, r: (p, 0, 0)),
            pl.BlockSpec((1, per, 2 * BLK), lambda p, r: (p, 0, 0)),
            pl.BlockSpec((length, width), lambda p, r: (jnp.where(p == quads - 1, r, 0), 0)),
        ],
        out_shape=[
            jax.ShapeDtypeStruct((quads, width, 3 * QUAD), BF16),
            jax.ShapeDtypeStruct((quads, 1, 3 * QUAD), F32),
            jax.ShapeDtypeStruct((quads, per, 2 * BLK), F32),
            jax.ShapeDtypeStruct((count, width), BF16),
        ],
        scratch_shapes=[
            pltpu.VMEM((blocks, BLK, 2 * BLK), BF16),
            pltpu.VMEM((2, length + 2 * HALO, 2 * PAIR), BF16),
            pltpu.VMEM((2, length + 2 * HALO, PAIR), BF16),
            pltpu.VMEM((length, length), BF16),
            pltpu.VMEM((length, PAIR), F32),
            pltpu.VMEM((length, PAIR), F32),
            pltpu.VMEM((length, PAIR), F32),
            pltpu.VMEM((length, 3 * QUAD), BF16),
            pltpu.VMEM((width, 3 * QUAD), F32),
            pltpu.VMEM((count, width), F32),
            pltpu.VMEM((per, BLK, 2 * BLK), F32),
        ],
        compiler_params=pltpu.CompilerParams(vmem_limit_bytes=60 * 2**20),
        name="attend_backward",
    )(dctx, att, inv, q, k, v, sq, sk, weight, slope, tokens, seg_col, seg_pad, w_qkv, w_qkv, w_qkv, taps, flipped, dproj)


def body(
    tokens, segment_ids, w_qkv, b_qkv, conv_kernel, w_out, b_out, norm1_gain, norm1_bias,
    w_up, b_up, w_down, b_down, norm2_gain, norm2_bias, cotangent,
):
    seqs, length = segment_ids.shape
    width = tokens.shape[1]
    heads, span = conv_kernel.shape
    per = QUAD // HEAD
    radius = span // 2
    first_tap = HALO - radius

    def spread(kernel):
        padded = jnp.pad(kernel, ((0, 0), (first_tap, 2 * BLK - first_tap - span)))
        return padded.reshape(heads // per, per, 2 * BLK)

    seg_col = segment_ids.reshape(-1, 1)
    seg_pad = jnp.pad(segment_ids, ((0, 0), (HALO, HALO)), constant_values=-1)[:, None, :]
    taps, flipped = spread(conv_kernel), spread(conv_kernel[:, ::-1])

    up_all = lax.all_gather(w_up, "tensor")
    down_all = lax.all_gather(w_down, "tensor")
    bias_all = lax.all_gather(b_up, "tensor")[:, None, :]

    q, k, v, sq, sk, weight, slope, att, inv, ctx, res = attend(
        tokens, seg_col, seg_pad, w_qkv, b_qkv[None], taps, w_out, b_out[None], length
    )
    out, dproj, dctx, gwo, gu, gd, gbu, gbd, gg2, gs2, gg1, gs1, gbo = feed_forward(
        res, cotangent, ctx, w_out, norm1_gain[None], norm1_bias[None], norm2_gain[None], norm2_bias[None],
        b_down[None], bias_all, up_all, down_all,
    )
    gw, gb, gconv, gt = attend_back(
        dctx, att, inv, q, k, v, sq, sk, weight, slope, tokens, seg_col, seg_pad, w_qkv, taps, flipped, dproj, length
    )
    grad_up = lax.psum(lax.psum_scatter(gu, "tensor"), "dp").astype(F32)
    grad_down = lax.psum(lax.psum_scatter(gd, "tensor"), "dp").astype(F32)
    first_lane = first_tap + BLK - 1
    grad_conv = gconv.reshape(heads, 2 * BLK)[:, first_lane : first_lane + span]
    gw, gwo = lax.psum((gw, gwo), ("dp", "tensor"))
    gb, grad_conv, gbo, gg1, gs1, gbd, gg2, gs2, gbu = lax.psum(
        (gb, grad_conv, gbo, gg1, gs1, gbd, gg2, gs2, gbu), ("dp", "tensor")
    )
    quads = gw.shape[0]
    gw = gw.reshape(quads, width, 3, QUAD).transpose(1, 2, 0, 3).reshape(width, 3 * width).astype(F32)
    gb = gb.reshape(quads, 3, QUAD).transpose(1, 0, 2).reshape(3 * width)
    grad_b_up = lax.dynamic_index_in_dim(gbu, lax.axis_index("tensor"), 0, False)[0]
    return (
        out, gt, gw, gb, grad_conv, gwo.astype(F32), gbo[0], gg1[0], gs1[0],
        grad_up, grad_b_up, grad_down, gbd[0], gg2[0], gs2[0],
    )


def solution(mesh):
    placed = (
        P(("dp", "tensor"), None),
        P(("dp", "tensor"), None),
        P(), P(), P(), P(), P(), P(), P(),
        P(None, "tensor"),
        P("tensor"),
        P("tensor", None),
        P(), P(), P(),
        P(("dp", "tensor"), None),
    )
    return jax.shard_map(
        body,
        mesh=mesh,
        in_specs=placed,
        out_specs=(
            P(("dp", "tensor"), None),
            P(("dp", "tensor"), None),
            P(), P(), P(), P(), P(), P(), P(),
            P(None, "tensor"),
            P("tensor"),
            P("tensor", None),
            P(), P(), P(),
        ),
        check_vma=False,
    )
```

```python
import functools
import math

import jax
import jax.numpy as jnp
from jax import lax
from jax.experimental import pallas as pl
from jax.experimental.pallas import tpu as pltpu
from jax.sharding import PartitionSpec as P

F32 = jnp.float32
BF16 = jnp.bfloat16
EPS_NORM = 1e-5
EPS_UNIT = 1e-6
SHRINK = 0.95
TAU = 8
SLOPE = TAU / math.pi
ARC = (0.49999996, -0.06830509, 0.02825875, -0.01557005, 0.00864352, -0.00363107, 0.00076235)
QUAD = 256
PAIR = 128
HEAD = 64
BLK = 128
HALO = 64


def dot_nn(a, b):
    return lax.dot_general(a, b, (((1,), (0,)), ((), ())), preferred_element_type=F32)


def dot_nt(a, b):
    return lax.dot_general(a, b, (((1,), (1,)), ((), ())), preferred_element_type=F32)


def dot_tn(a, b):
    return lax.dot_general(a, b, (((0,), (0,)), ((), ())), preferred_element_type=F32)


def lanes(shape):
    return lax.broadcasted_iota(jnp.int32, shape, len(shape) - 1)


def rows(shape):
    return lax.broadcasted_iota(jnp.int32, shape, len(shape) - 2)


def head_sum(values):
    width = values.shape[-1]
    ones = (rows((width, width)) // HEAD == lanes((width, width)) // HEAD).astype(BF16)
    high = values.astype(BF16)
    low = (values - high.astype(F32)).astype(BF16)
    return dot_nn(high, ones) + dot_nn(low, ones)


def closeness_terms(cosine):
    size = jnp.abs(cosine)
    room = 1.0 - size
    inverse = lax.rsqrt(room)
    poly = jnp.full_like(size, ARC[-1])
    for coefficient in ARC[-2::-1]:
        poly = poly * size + coefficient
    small = room * inverse * poly
    close = jnp.where(cosine >= 0.0, 1.0 - small, small)
    two = close * close
    four = two * two
    slope = (four * two) * (close * inverse) * lax.rsqrt(1.0 + size)
    return four * four, slope


def head_mask(half, shape):
    return (lanes(shape) // HEAD == half).astype(BF16)


def window_of(block, blocks):
    low = max(0, block * BLK - 256)
    high = min(blocks * BLK, block * BLK + BLK + 256)
    return low, high


def band(taps, count):
    spread = jnp.broadcast_to(taps, (count, taps.shape[1]))
    return pltpu.roll(spread, 0, 1, stride=1, stride_axis=0)


def norm_stats(values):
    centred = values - jnp.mean(values, -1, keepdims=True)
    scaling = lax.rsqrt(jnp.mean(centred * centred, -1, keepdims=True) + EPS_NORM)
    return centred * scaling, scaling


def build_masks(seg_col, seg_pad, same_ref, near_ref):
    length = seg_col.shape[0]
    for start in range(0, length, BLK):
        own = seg_col[start : start + BLK]
        same_ref[start : start + BLK, :] = jnp.where(
            own == seg_pad[:, HALO : HALO + length], 1.0, 0.0
        ).astype(BF16)
        near_ref[start // BLK] = jnp.where(
            own == seg_pad[:, start : start + 2 * BLK], 1.0, 0.0
        ).astype(BF16)


def build_near(seg_col, seg_pad, near_ref):
    length = seg_col.shape[0]
    for start in range(0, length, BLK):
        own = seg_col[start : start + BLK]
        near_ref[start // BLK] = jnp.where(
            own == seg_pad[:, start : start + 2 * BLK], 1.0, 0.0
        ).astype(BF16)


def attend_kernel(
    x_ref, col_ref, pad_ref, wq_ref, wk_ref, wv_ref, bq_ref, bk_ref, bv_ref, tap_ref, wo_ref, bo_ref,
    q_ref, k_ref, v_ref, sq_ref, sk_ref, w_ref, s_ref, att_ref, inv_ref, ctx_ref, res_ref,
    same_ref, near_ref, vv_ref,
):
    quad = pl.program_id(1)
    length = x_ref.shape[0]
    blocks = length // BLK

    @pl.when(quad == 0)
    def _():
        build_masks(col_ref[...], pad_ref[0], same_ref, near_ref)
        for half in range(2):
            edge = jnp.zeros((HALO, 2 * PAIR), BF16)
            vv_ref[half, :HALO] = edge
            vv_ref[half, HALO + length :] = edge
            vv_ref[half, HALO : HALO + length, PAIR:] = head_mask(half, (length, PAIR))

    for start in range(0, length, BLK):
        here = slice(start, start + BLK)
        x = x_ref[here]
        for w, b, unit, scale, factor in (
            (wq_ref, bq_ref, q_ref, sq_ref, SHRINK),
            (wk_ref, bk_ref, k_ref, sk_ref, 1.0),
        ):
            part = dot_nn(x, w[...]) + b[...]
            scaling = lax.rsqrt(head_sum(part * part) + EPS_UNIT)
            unit[here] = (part * (scaling * factor)).astype(BF16)
            scale[here] = scaling.astype(BF16)
        v_ref[here] = (dot_nn(x, wv_ref[...]) + bv_ref[...]).astype(BF16)

    def one_pair(pair, carry):
        at = pl.ds(pl.multiple_of(pair * PAIR, PAIR), PAIR)
        v = v_ref[:, at]
        for half in range(2):
            vv_ref[half, HALO : HALO + length, :PAIR] = v * head_mask(half, (length, PAIR))
        for block in range(blocks):
            here = slice(block * BLK, block * BLK + BLK)
            low, high = window_of(block, blocks)
            q = q_ref[here, at]
            total = jnp.zeros((BLK, 2 * PAIR), F32)
            near = jnp.zeros((BLK, PAIR), F32)
            for half in range(2):
                head = pair * 2 + half
                q_half = q * head_mask(half, (BLK, PAIR))
                for start in range(low, high, KCH):
                    stop = min(start + KCH, high)
                    cosine = dot_nt(q_half, k_ref[start:stop, at])
                    weight, slope = closeness_terms(cosine)
                    same = same_ref[here, start:stop]
                    weight = weight.astype(BF16) * same
                    w_ref[0, head, here, start:stop] = weight
                    s_ref[0, head, here, start:stop] = slope.astype(BF16) * same
                    total += dot_nn(weight, vv_ref[half, HALO + start : HALO + stop])
                if low > 0:
                    w_ref[0, head, here, :low] = jnp.zeros((BLK, low), BF16)
                if high < length:
                    w_ref[0, head, here, high:] = jnp.zeros((BLK, length - high), BF16)
                taps = band(tap_ref[0, pl.ds(head, 1)], BLK).astype(BF16) * near_ref[block]
                near += dot_nn(taps, vv_ref[half, block * BLK : block * BLK + 2 * BLK, :PAIR])
            inverse = 1.0 / (1.0 + total[:, PAIR:])
            attended = total[:, :PAIR] * inverse
            att_ref[here, at] = attended.astype(BF16)
            inv_ref[here, at] = inverse.astype(BF16)
            ctx_ref[here, at] = (attended + near).astype(BF16)
        return carry

    lax.fori_loop(0, QUAD // PAIR, one_pair, 0)

    for start in range(0, length, BLK):
        here = slice(start, start + BLK)
        grown = dot_nn(ctx_ref[here], wo_ref[...])

        @pl.when(quad == 0)
        def _():
            res_ref[here] = grown + x_ref[here].astype(F32) + bo_ref[...]

        @pl.when(quad > 0)
        def _():
            res_ref[here] += grown


KCH = 256


def attend(tokens, seg_col, seg_pad, w_qkv, b_qkv, taps, w_out, b_out, length):
    count, width = tokens.shape
    seqs = count // length
    quads = width // QUAD
    heads = width // HEAD
    per = QUAD // HEAD
    blocks = length // BLK
    own = pl.BlockSpec((length, QUAD), lambda r, p: (r, p))
    act = jax.ShapeDtypeStruct((count, width), BF16)
    big = jax.ShapeDtypeStruct((seqs, heads, length, length), BF16)
    big_spec = pl.BlockSpec((1, per, length, length), lambda r, p: (r, p, 0, 0))

    def part(rows_of, k):
        return pl.BlockSpec((rows_of, QUAD), lambda r, p, k=k: (0, p + k * quads))

    return pl.pallas_call(
        attend_kernel,
        grid=(seqs, quads),
        in_specs=[
            pl.BlockSpec((length, width), lambda r, p: (r, 0)),
            pl.BlockSpec((length, 1), lambda r, p: (r, 0)),
            pl.BlockSpec((1, 1, length + 2 * HALO), lambda r, p: (r, 0, 0)),
            part(width, 0), part(width, 1), part(width, 2),
            part(1, 0), part(1, 1), part(1, 2),
            pl.BlockSpec((1, per, 2 * BLK), lambda r, p: (p, 0, 0)),
            pl.BlockSpec((QUAD, width), lambda r, p: (p, 0)),
            pl.BlockSpec((1, width), lambda r, p: (0, 0)),
        ],
        out_specs=[own] * 5 + [big_spec] * 2 + [own] * 3 + [pl.BlockSpec((length, width), lambda r, p: (r, 0))],
        out_shape=[act] * 5 + [big] * 2 + [act] * 3 + [jax.ShapeDtypeStruct((count, width), F32)],
        scratch_shapes=[
            pltpu.VMEM((length, length), BF16),
            pltpu.VMEM((blocks, BLK, 2 * BLK), BF16),
            pltpu.VMEM((2, length + 2 * HALO, 2 * PAIR), BF16),
        ],
        compiler_params=pltpu.CompilerParams(vmem_limit_bytes=56 * 2**20),
        name="attend_forward",
    )(tokens, seg_col, seg_pad, w_qkv, w_qkv, w_qkv, b_qkv, b_qkv, b_qkv, taps, w_out, b_out)

GELU_A = math.sqrt(2.0 / math.pi)
GELU_B = 0.044715
TILE = 256


def gelu_terms(pre):
    square = pre * pre
    swing = jnp.tanh(pre * (GELU_A + GELU_A * GELU_B * square))
    gate = 0.5 + 0.5 * swing
    steep = GELU_A + 3.0 * GELU_A * GELU_B * square
    return pre * gate, gate + 0.5 * pre * (1.0 - swing * swing) * steep


def norm_backward(grad_out, unit, scaling, gain):
    grad_unit = grad_out * gain
    return scaling * (
        grad_unit
        - jnp.mean(grad_unit, -1, keepdims=True)
        - unit * jnp.mean(grad_unit * unit, -1, keepdims=True)
    )


def column_sum(values):
    return jnp.sum(values, 0, keepdims=True)


def ffn_kernel(
    res_ref, cot_ref, ctx_ref, wo_ref, gain1_ref, shift1_ref, gain2_ref, shift2_ref, bd_ref, bu_ref, wu_ref, wd_ref,
    out_ref, dproj_ref, dctx_ref, gwo_ref, pu_ref, pd_ref, small_ref,
    low_ref, acc_ref, hid_ref, slope_ref, dffn_ref, dpre_ref, sendu_ref, sendd_ref, recvu_ref, recvd_ref,
    send_sem, recv_sem,
):
    parts = pl.num_programs(0) // 2
    step = pl.program_id(0)
    count, width = res_ref.shape
    share = dpre_ref.shape[1]
    tiles = count // TILE
    f = part_order(step, parts)
    late = jnp.maximum(step - parts, 0)
    heights = parts // 2
    slot = lax.rem(late, heights)
    tensor = lax.axis_index("tensor")
    mate = (lax.axis_index("dp"), tensor + 1 - 2 * lax.rem(tensor, 2))

    def to_mate(which):
        return (
            pltpu.make_async_remote_copy(
                src_ref=sendu_ref.at[which], dst_ref=recvu_ref.at[which],
                send_sem=send_sem.at[0, which], recv_sem=recv_sem.at[0, which],
                device_id=mate, device_id_type=pl.DeviceIdType.MESH,
            ),
            pltpu.make_async_remote_copy(
                src_ref=sendd_ref.at[which], dst_ref=recvd_ref.at[which],
                send_sem=send_sem.at[1, which], recv_sem=recv_sem.at[1, which],
                device_id=mate, device_id_type=pl.DeviceIdType.MESH,
            ),
        )

    @pl.when(step == 0)
    def _():
        barrier = pltpu.get_barrier_semaphore()
        pl.semaphore_signal(barrier, inc=1, device_id=mate, device_id_type=pl.DeviceIdType.MESH)
        pl.semaphore_wait(barrier, 1)

    def put_row(row, values):
        for i in range(values.shape[1] // PAIR):
            small_ref[pl.ds(row + i, 1)] = values[:, i * PAIR : (i + 1) * PAIR]

    def at(t):
        return pl.ds(pl.multiple_of(t * TILE, TILE), TILE)

    @pl.when(step == 0)
    def _():
        def one(t, carry):
            unit, _ = norm_stats(res_ref[at(t)])
            low_ref[at(t)] = (unit * gain1_ref[...] + shift1_ref[...]).astype(BF16)
            return carry

        lax.fori_loop(0, tiles, one, 0)

    @pl.when(step < parts)
    def _():
        def one(t, carry):
            pre = dot_nn(low_ref[at(t)], wu_ref[0]) + bu_ref[0].astype(F32)
            hidden, slope = gelu_terms(pre)
            hidden = hidden.astype(BF16)
            hid_ref[f, at(t)] = hidden
            slope_ref[f, at(t)] = slope.astype(BF16)
            grown = dot_nn(hidden, wd_ref[0])

            @pl.when(step == 0)
            def _():
                acc_ref[at(t)] = grown

            @pl.when(step > 0)
            def _():
                acc_ref[at(t)] += grown

            return carry

        lax.fori_loop(0, tiles, one, 0)

    @pl.when(step == parts)
    def _():
        def one(t, sums):
            unit, _ = norm_stats(res_ref[at(t)])
            first = unit * gain1_ref[...] + shift1_ref[...]
            unit, scaling = norm_stats(first + acc_ref[at(t)] + bd_ref[...])
            out_ref[at(t)] = (unit * gain2_ref[...] + shift2_ref[...]).astype(BF16)
            grad = cot_ref[at(t)].astype(F32)
            d_res = norm_backward(grad, unit, scaling, gain2_ref[...])
            d_ffn = d_res.astype(BF16)
            acc_ref[at(t)] = d_res
            dffn_ref[at(t)] = d_ffn
            return (
                sums[0] + column_sum(grad * unit),
                sums[1] + column_sum(grad),
                sums[2] + column_sum(d_ffn.astype(F32)),
            )

        zero = jnp.zeros((1, width), F32)
        sums = lax.fori_loop(0, tiles, one, (zero, zero, zero))
        small_ref[...] = jnp.zeros_like(small_ref)
        for i, values in enumerate(sums):
            put_row(i * (width // PAIR), values)

    @pl.when(step >= parts)
    def _():
        def one(t, total):
            d_hidden = dot_nt(dffn_ref[at(t)], wd_ref[0])
            d_pre = (d_hidden * slope_ref[f, at(t)].astype(F32)).astype(BF16)
            dpre_ref[at(t)] = d_pre
            acc_ref[at(t)] += dot_nt(d_pre, wu_ref[0])
            return total + column_sum(d_pre.astype(F32))

        bias = lax.fori_loop(0, tiles, one, jnp.zeros((1, share), F32))
        put_row(6 * (width // PAIR) + f * (share // PAIR), bias)

        def grads(store_up, store_down):
            for start in range(0, width, TILE):
                cut = slice(start, start + TILE)
                store_up(cut, dot_tn(low_ref[:, cut], dpre_ref[...]))
            piece = math.gcd(TILE, share)
            for start in range(0, share, piece):
                cut = slice(start, start + piece)
                store_down(cut, dot_tn(hid_ref[f, :, cut], dffn_ref[...]))

        @pl.when(late < heights)
        def _():
            def up(cut, values):
                sendu_ref[slot, cut] = values.astype(BF16)

            def down(cut, values):
                sendd_ref[slot, cut] = values.astype(BF16)

            grads(up, down)
            for copy in to_mate(slot):
                copy.start()

        @pl.when(late >= heights)
        def _():
            for copy in to_mate(slot):
                copy.wait()

            def up(cut, values):
                pu_ref[slot, cut] = (values + recvu_ref[slot, cut].astype(F32)).astype(BF16)

            def down(cut, values):
                pd_ref[slot, cut] = (values + recvd_ref[slot, cut].astype(F32)).astype(BF16)

            grads(up, down)

    @pl.when(step == 2 * parts - 1)
    def _():
        def one(t, sums):
            unit, scaling = norm_stats(res_ref[at(t)])
            grad = acc_ref[at(t)]
            d_proj = norm_backward(grad, unit, scaling, gain1_ref[...]).astype(BF16)
            dproj_ref[at(t)] = d_proj
            dctx_ref[at(t)] = dot_nt(d_proj, wo_ref[...]).astype(BF16)
            return (
                sums[0] + column_sum(grad * unit),
                sums[1] + column_sum(grad),
                sums[2] + column_sum(d_proj.astype(F32)),
            )

        zero = jnp.zeros((1, width), F32)
        sums = lax.fori_loop(0, tiles, one, (zero, zero, zero))
        for i, values in enumerate(sums):
            put_row((3 + i) * (width // PAIR), values)
        for start in range(0, width, TILE):
            values = dot_tn(ctx_ref[:, start : start + TILE], dproj_ref[...]).astype(BF16)
            gwo_ref[start : start + TILE] = values[:, : width // 2]
            gwo_ref[width + start : width + start + TILE] = values[:, width // 2 :]


def part_order(step, parts):
    tensor = lax.axis_index("tensor")
    height, core = tensor // 2, lax.rem(tensor, 2)
    heights = parts // 2
    late = jnp.maximum(step - parts, 0)
    there = lax.rem(height + 1 + lax.rem(late, heights), heights)
    whose = jnp.where(late < heights, 1 - core, core)
    return jnp.where(step < parts, step, there * 2 + whose)


def feed_forward(res, cot, ctx, w_out, gain1, shift1, gain2, shift2, b_down, b_up, w_up, w_down):
    count, width = res.shape
    parts, _, share = w_up.shape
    heights = parts // 2
    smalls = 6 * width // PAIR + parts * share // PAIR
    smalls = -(-smalls // 8) * 8

    def whole(*shape):
        return pl.BlockSpec(shape, lambda s: (0,) * len(shape), pipeline_mode=pl.Buffered(1))

    def per_part(*shape):
        return pl.BlockSpec((1,) + shape, lambda s: (part_order(s, parts),) + (0,) * len(shape))

    act = jax.ShapeDtypeStruct((count, width), BF16)
    return pl.pallas_call(
        ffn_kernel,
        grid=(2 * parts,),
        in_specs=[whole(count, width)] * 3
        + [whole(width, width)]
        + [whole(1, width)] * 5
        + [per_part(1, share), per_part(width, share), per_part(share, width)],
        out_specs=[whole(count, width)] * 3
        + [whole(2 * width, width // 2), whole(heights, width, share), whole(heights, share, width), whole(smalls, PAIR)],
        out_shape=[act] * 3
        + [
            jax.ShapeDtypeStruct((2 * width, width // 2), BF16),
            jax.ShapeDtypeStruct((heights, width, share), BF16),
            jax.ShapeDtypeStruct((heights, share, width), BF16),
            jax.ShapeDtypeStruct((smalls, PAIR), F32),
        ],
        scratch_shapes=[
            pltpu.VMEM((count, width), BF16),
            pltpu.VMEM((count, width), F32),
            pltpu.VMEM((parts, count, share), BF16),
            pltpu.VMEM((parts, count, share), BF16),
            pltpu.VMEM((count, width), BF16),
            pltpu.VMEM((count, share), BF16),
            pltpu.VMEM((heights, width, share), BF16),
            pltpu.VMEM((heights, share, width), BF16),
            pltpu.VMEM((heights, width, share), BF16),
            pltpu.VMEM((heights, share, width), BF16),
            pltpu.SemaphoreType.DMA((2, heights)),
            pltpu.SemaphoreType.DMA((2, heights)),
        ],
        compiler_params=pltpu.CompilerParams(vmem_limit_bytes=60 * 2**20, collective_id=0, has_side_effects=True),
        name="feed_forward",
    )(res, cot, ctx, w_out, gain1, shift1, gain2, shift2, b_down, b_up, w_up, w_down)


DEPTH = 4
CORES = 2


class Axis:
    def __init__(self, size, place, device):
        self.size, self.place, self.device = size, place, device

    def ahead(self, j):
        return lax.rem(self.place + j, self.size)


def slice_axes(dp_size, tensor_size):
    dp, tensor = lax.axis_index("dp"), lax.axis_index("tensor")
    across = dp_size // DEPTH
    z, x = dp // across, lax.rem(dp, across)
    y, core = tensor // CORES, lax.rem(tensor, CORES)
    return {
        "core": Axis(CORES, core, lambda p: (dp, y * CORES + p)),
        "y": Axis(tensor_size // CORES, y, lambda p: (dp, p * CORES + core)),
        "x": Axis(across, x, lambda p: (z * across + p, tensor)),
        "z": Axis(DEPTH, z, lambda p: (p * across + x, tensor)),
    }


def greet(axes):
    barrier = pltpu.get_barrier_semaphore()
    count = 0
    for axis in axes.values():
        for j in range(1, axis.size):
            pl.semaphore_signal(
                barrier, inc=1, device_id=axis.device(axis.ahead(j)), device_id_type=pl.DeviceIdType.MESH
            )
            count += 1
    pl.semaphore_wait(barrier, count)


def send(source, target, sems, at, device):
    return pltpu.make_async_remote_copy(
        src_ref=source, dst_ref=target, send_sem=sems[0].at[at], recv_sem=sems[1].at[at],
        device_id=device, device_id_type=pl.DeviceIdType.MESH,
    )


def span(start, size):
    if isinstance(start, int):
        return pl.ds(start, size)
    return pl.ds(pl.multiple_of(start, math.gcd(size, 16)), size)


def add_rows(target, target_at, terms, size):
    tile = next(t for t in (64, 48, 32, 24, 16, 12, 8) if size % t == 0)

    def one(i, carry):
        total = None
        for ref, start in terms:
            rows_of = ref[span(start + i * tile, tile)].astype(F32)
            total = rows_of if total is None else total + rows_of
        target[span(target_at + i * tile, tile)] = total.astype(target.dtype)
        return carry

    lax.fori_loop(0, size // tile, one, 0)


class Reduction:
    def __init__(self, axes, order, back, source, source_at, size, final, final_at, landings, sems, first_sem=0):
        self.axes, self.order, self.back = axes, order, back
        self.source, self.source_at, self.size = source, source_at, size
        self.final, self.final_at = final, final_at
        self.landings, self.sems = landings, sems
        self.first_sem = first_sem

    def plan(self):
        size, at, out = self.size, self.final_at, []
        for name in self.order:
            axis = self.axes[name]
            size //= axis.size
            at = at + axis.place * size
            out.append((axis, size, at))
        return out

    def copies(self, stage):
        stages = self.plan()
        sem = self.first_sem
        for axis, _, _ in stages[:stage]:
            sem += axis.size - 1
        axis, size, _ = stages[stage]
        held, held_at = (self.source, self.source_at) if stage == 0 else (self.landings[stage - 1].at[0], 0)
        return [
            send(
                held.at[span(held_at + axis.ahead(j) * size, size)], self.landings[stage].at[j - 1],
                self.sems, sem + j - 1, axis.device(axis.ahead(j)),
            )
            for j in range(1, axis.size)
        ]

    def settle(self, stage):
        for copy in self.copies(stage):
            copy.wait()
        axis, size, final_at = self.plan()[stage]
        held, held_at = (self.source, self.source_at) if stage == 0 else (self.landings[stage - 1].at[0], 0)
        terms = [(held, held_at + axis.place * size)]
        terms += [(self.landings[stage].at[j - 1], 0) for j in range(1, axis.size)]
        if stage == len(self.order) - 1:
            add_rows(self.final, final_at, terms, size)
        else:
            add_rows(self.landings[stage].at[0], 0, terms, size)

    def gathers(self, which):
        stages = self.plan()
        sem = self.first_sem + sum(axis.size - 1 for axis, _, _ in stages)
        for name in self.back[:which]:
            sem += self.axes[name].size - 1
        depth = self.order.index(self.back[which])
        axis, size, at = stages[depth]
        block = self.final.at[span(at, size)]
        return [send(block, block, self.sems, sem + j - 1, axis.device(axis.ahead(j))) for j in range(1, axis.size)]

    def events(self):
        out = []
        count = len(self.order)

        def begin(copies):
            for copy in copies:
                copy.start()

        for stage in range(count):
            def event(stage=stage):
                if stage > 0:
                    self.settle(stage - 1)
                begin(self.copies(stage))

            out.append(event)
        for which in range(len(self.back)):
            def event(which=which):
                if which == 0:
                    self.settle(count - 1)
                else:
                    for copy in self.gathers(which - 1):
                        copy.wait()
                begin(self.gathers(which))

            out.append(event)

        def last():
            for copy in self.gathers(len(self.back) - 1):
                copy.wait()

        out.append(last)
        return out


def landing_shapes(order, sizes, size, columns, dtype):
    shapes = []
    for name in order:
        size //= sizes[name]
        shapes.append(pltpu.VMEM((sizes[name] - 1, size, columns), dtype))
    return shapes


def copies_of(order, back, sizes):
    return sum(sizes[name] - 1 for name in order) + sum(sizes[name] - 1 for name in back)


def attend_back_kernel(
    dctx_ref, att_ref, inv_ref, q_ref, k_ref, v_ref, sq_ref, sk_ref, w_ref, s_ref, x_ref, col_ref, pad_ref,
    wq_ref, wk_ref, wv_ref, flip_ref, dproj_ref, gwo_ref, pu_ref, pd_ref, small_ref,
    gt_ref, all_out, up_out, down_out, few_out,
    near_ref, vv_ref, dpad_ref, dcos_ref, dq_ref, dk_ref, dv_ref, joined_ref, gwacc_ref, gtacc_ref, conv_ref,
    gwlow_ref, gb_ref, mini_ref, all_ref, up_ref, down_ref, few_ref, out_sem, *links,
    plan, quads, seqs,
):
    quad, row = pl.program_id(0), pl.program_id(1)
    length = x_ref.shape[0]
    blocks = length // BLK
    inside = slice(HALO, HALO + length)

    _, sizes, dp_size, tensor_size = plan
    axes = slice_axes(dp_size, tensor_size)
    ticks = schedule(axes, sizes, quads, seqs, gwo_ref, pu_ref, pd_ref, gwlow_ref, mini_ref, all_ref, up_ref, down_ref, few_ref, links,
        (all_out, up_out, down_out, few_out, out_sem))
    calls = quads * seqs * (QUAD // PAIR)

    build_near(col_ref[...], pad_ref[0], near_ref)
    for half in range(2):
        edge = jnp.zeros((HALO, PAIR), BF16)
        for ref in (vv_ref, dpad_ref):
            ref[half, :HALO, :PAIR] = edge
            ref[half, HALO + length :, :PAIR] = edge
        vv_ref[half, inside, PAIR:] = head_mask(half, (length, PAIR))

    @pl.when(row == 0)
    def _():
        conv_ref[...] = jnp.zeros_like(conv_ref)
        gwacc_ref[...] = jnp.zeros_like(gwacc_ref)

    @pl.when((quad == 0) & (row == 0))
    def _():
        gb_ref[...] = jnp.zeros_like(gb_ref)
        mini_ref[...] = jnp.zeros_like(mini_ref)
        mini_ref[: small_ref.shape[0]] = small_ref[...]
        filled = 2 * gwacc_ref.shape[0]
        if gwlow_ref.shape[1] > filled:
            gwlow_ref[:, filled:] = jnp.zeros((quads, gwlow_ref.shape[1] - filled, gwlow_ref.shape[2]), BF16)

    def one_pair(pair, carry):
        tick = (quad * seqs + row) * (QUAD // PAIR) + pair
        for when in range(calls):
            if ticks.get(when):

                @pl.when(tick == when)
                def _(when=when):
                    for event in ticks[when]:
                        event()

        at = pl.ds(pl.multiple_of(pair * PAIR, PAIR), PAIR)
        inverse = inv_ref[:, at].astype(F32)
        d_ctx = dctx_ref[:, at]
        d_summed = (d_ctx.astype(F32) * inverse).astype(BF16)
        d_total = (-d_summed.astype(F32) * att_ref[:, at].astype(F32)).astype(BF16)
        both = jnp.concatenate([d_summed, d_total], 1)
        dk = jnp.zeros((length, PAIR), F32)
        dv = jnp.zeros((length, PAIR), F32)
        for half in range(2):
            head = pair * 2 + half
            mask = head_mask(half, (length, PAIR))
            vv_ref[half, inside, :PAIR] = v_ref[:, at] * mask
            dpad_ref[half, inside] = d_ctx * mask
            k_half = k_ref[:, at] * mask
            for block in range(blocks):
                here = slice(block * BLK, block * BLK + BLK)
                low, high = window_of(block, blocks)
                d_weight = dot_nt(both[here], vv_ref[half, HALO + low : HALO + high])
                d_cos = d_weight.astype(BF16) * s_ref[0, head, here, low:high]
                dcos_ref[here, low:high] = d_cos
                if low > 0:
                    dcos_ref[here, :low] = jnp.zeros((BLK, low), BF16)
                if high < length:
                    dcos_ref[here, high:] = jnp.zeros((BLK, length - high), BF16)
                grown = dot_nn(d_cos, k_half[low:high])
                if half == 0:
                    dq_ref[here] = grown
                else:
                    dq_ref[here] += grown
                window = slice(block * BLK, block * BLK + 2 * BLK)
                near = near_ref[block]
                taps = band(flip_ref[0, pl.ds(head, 1)], BLK).astype(BF16) * near
                grown = dot_nn(taps, dpad_ref[half, window])
                if half == 0:
                    dv_ref[here] = grown
                else:
                    dv_ref[here] += grown
                conv_ref[head] += near.astype(F32) * dot_nt(d_ctx[here], vv_ref[half, window, :PAIR])
            dk += dot_tn(dcos_ref[...], q_ref[:, at] * mask)
            dv += dot_tn(w_ref[0, head], d_summed * mask)
        dv_ref[...] += dv
        grad = SLOPE * dq_ref[...]
        unit = q_ref[:, at].astype(F32)
        d_query = sq_ref[:, at].astype(F32) * (SHRINK * grad - unit * (head_sum(grad * unit) / SHRINK))
        grad = SLOPE * dk
        unit = k_ref[:, at].astype(F32)
        d_key = sk_ref[:, at].astype(F32) * (grad - unit * head_sum(grad * unit))
        for part, values in enumerate((d_query, d_key, dv_ref[...])):
            joined_ref[:, pl.ds(pl.multiple_of(part * QUAD + pair * PAIR, PAIR), PAIR)] = values.astype(BF16)
        return carry

    lax.fori_loop(0, QUAD // PAIR, one_pair, 0)

    gb_ref[quad, :1] += column_sum(joined_ref[...].astype(F32))
    width = gwacc_ref.shape[0]
    for start in range(0, width, TILE):
        cut = slice(start, start + TILE)
        gwacc_ref[cut] += dot_tn(x_ref[:, cut], joined_ref[...])

    @pl.when(row == seqs - 1)
    def _():
        half = gwacc_ref.shape[1] // 2
        for start in range(0, width, TILE):
            for side in range(2):
                values = gwacc_ref[start : start + TILE, side * half : (side + 1) * half]
                gwlow_ref[quad, side * width + start : side * width + start + TILE] = values.astype(BF16)
        base = small_ref.shape[0]
        lines = gb_ref.shape[2] // PAIR
        for i in range(lines):
            mini_ref[pl.ds(base + quad * lines + i, 1)] = gb_ref[quad, :1, i * PAIR : (i + 1) * PAIR]
        base += quads * lines
        for head in range(QUAD // HEAD):
            sums = conv_ref[head]
            high = sums.astype(BF16)
            turn = (rows((BLK, BLK)) + lanes((BLK, BLK)) == BLK - 1).astype(BF16)
            turned = dot_nn(turn, high) + dot_nn(turn, (sums - high.astype(F32)).astype(BF16))
            turned = pltpu.roll(turned, BLK, 1, stride=1, stride_axis=0)
            mini_ref[pl.ds(base + quad * (QUAD // HEAD) + head, 1)] = column_sum(turned)[:, :PAIR]

    last = (quad == quads - 1) & (row == seqs - 1)

    @pl.when(last)
    def _():
        for event in ticks[calls]:
            event()

    for start in range(0, length, TILE):
        here = pl.ds(pl.multiple_of(row * length + start, TILE), TILE)
        cut = slice(start, start + TILE)
        grown = (
            dot_nt(joined_ref[cut, :QUAD], wq_ref[...])
            + dot_nt(joined_ref[cut, QUAD : 2 * QUAD], wk_ref[...])
            + dot_nt(joined_ref[cut, 2 * QUAD :], wv_ref[...])
        )

        @pl.when(quad == 0)
        def _():
            gtacc_ref[here] = grown + dproj_ref[cut].astype(F32)

        @pl.when(quad > 0)
        def _():
            gtacc_ref[here] += grown

    @pl.when(quad == quads - 1)
    def _():
        gt_ref[...] = gtacc_ref[pl.ds(pl.multiple_of(row * length, TILE), length)].astype(BF16)

    @pl.when(last)
    def _():
        for when in sorted(ticks):
            if when > calls:
                for event in ticks[when]:
                    event()


FFN_ROWS = 384
FFN_ORDER = ("y", "x", "z")
FFN_BACK = ("z", "x")
ORDERS = (("core", "x", "y", "z"), ("core", "y", "x", "z"))


def all_order(index):
    order = ORDERS[index % 2]
    return order, order[::-1]


class FfnReduction(Reduction):
    def copies(self, stage):
        if stage > 0:
            return super().copies(stage)
        axis = self.axes["y"]
        return [
            send(
                self.source.at[j - 1, span(self.source_at, self.size)], self.landings[0].at[j - 1],
                self.sems, self.first_sem + j - 1, axis.device(axis.ahead(j)),
            )
            for j in range(1, axis.size)
        ]

    def plan(self):
        size, at = self.size, self.final_at
        out = [(self.axes["y"], size, at)]
        for name in self.order[1:]:
            axis = self.axes[name]
            size //= axis.size
            at = at + axis.place * size
            out.append((axis, size, at))
        return out

    def settle(self, stage):
        if stage > 0:
            return super().settle(stage)
        axis = self.axes["y"]
        for copy in self.copies(0):
            copy.wait()
        terms = [(self.source.at[axis.size - 1], self.source_at)]
        terms += [(self.landings[0].at[j - 1], 0) for j in range(1, axis.size)]
        add_rows(self.landings[0].at[0], 0, terms, self.size)


def link_plan(sizes, width, share, quads):
    out = []
    devices = math.prod(sizes.values())
    y = sizes["y"]
    for height, columns in ((width, share), (share, width)):
        for _ in range(height // FFN_ROWS):
            shapes = [pltpu.VMEM((y - 1, FFN_ROWS, columns), BF16)]
            shapes += landing_shapes(FFN_ORDER[1:], sizes, FFN_ROWS, columns, BF16)
            out.append((shapes, copies_of(FFN_ORDER, FFN_BACK, sizes)))
    for index in range(quads + 1):
        order, back = all_order(index)
        out.append((landing_shapes(order, sizes, padded(2 * width, devices), width // 2, BF16), copies_of(order, back, sizes)))
    order, back = all_order(quads)
    out.append((landing_shapes(order, sizes, 8 * devices, PAIR, F32), copies_of(order, back, sizes)))
    return out


def padded(size, devices):
    return -(-size // (16 * devices)) * 16 * devices


def schedule(axes, sizes, quads, seqs, gwo_ref, pu_ref, pd_ref, gwlow_ref, mini_ref, all_ref, up_ref, down_ref, few_ref, links, outs):
    all_out, up_out, down_out, few_out, out_sem = outs
    calls = quads * seqs * (QUAD // PAIR)
    per_quad = seqs * (QUAD // PAIR)
    width, share = pu_ref.shape[1], pu_ref.shape[2]
    devices = math.prod(sizes.values())
    groups = link_plan(sizes, width, share, quads)
    taken, position = [], 0
    for shapes, _ in groups:
        taken.append((links[position : position + len(shapes)], links[position + len(shapes) : position + len(shapes) + 2]))
        position += len(shapes) + 2
    ticks = {0: [lambda: greet(axes)]}

    stores = []

    def enlist(reduction, times, done, place):
        for time, event in zip(times, reduction.events(), strict=True):
            ticks.setdefault(time, []).append(event)
        store = pltpu.make_async_copy(done, place, out_sem.at[len(stores)])
        ticks[times[-1]].append(store.start)
        stores.append(store)

    number = 0
    begin = (0, 0, 3, 6)
    for source, final, place in ((pu_ref, up_ref, up_out), (pd_ref, down_ref, down_out)):
        for start in range(0, source.shape[1], FFN_ROWS):
            landings, sems = taken[number]
            reduction = FfnReduction(axes, FFN_ORDER, FFN_BACK, source, start, FFN_ROWS, final, start, landings, sems)
            done = 3 * (number + 1)
            enlist(reduction, (begin[number], done, done + 2, done + 4, done + 6, done + 8),
                   final.at[span(start, FFN_ROWS)], place.at[span(start, FFN_ROWS)])
            number += 1
    size = padded(2 * width, devices)
    for index in range(quads + 1):
        landings, sems = taken[number]
        order, back = all_order(index)
        source = gwo_ref if index == 0 else gwlow_ref.at[index - 1]
        reduction = Reduction(axes, order, back, source, 0, size, all_ref.at[index], 0, landings, sems)
        first = index * per_quad
        enlist(reduction, (first, first + 1, first + 3, first + 5, first + 6, first + 7, first + 9, first + 11, first + 12),
               all_ref.at[index], all_out.at[index])
        number += 1
    landings, sems = taken[number]
    order, back = all_order(quads)
    reduction = Reduction(axes, order, back, mini_ref, 0, 8 * devices, few_ref, 0, landings, sems)
    enlist(reduction, (calls, calls + 1, calls + 3, calls + 5, calls + 6, calls + 7, calls + 9, calls + 11, calls + 12), few_ref, few_out)
    ticks[max(ticks) + 1] = [store.wait for store in stores]
    return ticks


def attend_back(dctx, att, inv, q, k, v, sq, sk, weight, slope, tokens, seg_col, seg_pad, w_qkv, flipped, dproj, gwo, pu, pd, small, dp_size, tensor_size, length):
    count, width = tokens.shape
    seqs = count // length
    quads = width // QUAD
    per = QUAD // HEAD
    blocks = length // BLK
    own = pl.BlockSpec((length, QUAD), lambda p, r: (r, p))
    big = pl.BlockSpec((1, per, length, length), lambda p, r: (r, p, 0, 0))
    wide = pl.BlockSpec((length, width), lambda p, r: (r, 0))

    def part(k):
        return pl.BlockSpec((width, QUAD), lambda p, r, k=k: (0, p + k * quads))

    sizes = {"core": CORES, "y": tensor_size // CORES, "x": dp_size // DEPTH, "z": DEPTH}
    devices = dp_size * tensor_size
    share = pu.shape[2]
    grown = padded(2 * width, devices)
    gwo = jnp.pad(gwo, ((0, grown - gwo.shape[0]), (0, 0)))
    minis = 8 * devices
    scratch = []
    for shapes, count_of in link_plan(sizes, width, share, quads):
        scratch += shapes + [pltpu.SemaphoreType.DMA((count_of,)), pltpu.SemaphoreType.DMA((count_of,))]

    def whole(*shape):
        return pl.BlockSpec(shape, lambda p, r: (0,) * len(shape), pipeline_mode=pl.Buffered(1))

    taps_spec = pl.BlockSpec((1, per, 2 * BLK), lambda p, r: (p, 0, 0))
    return pl.pallas_call(
        functools.partial(attend_back_kernel, plan=(None, sizes, dp_size, tensor_size), quads=quads, seqs=seqs),
        grid=(quads, seqs),
        in_specs=[own] * 8
        + [big] * 2
        + [
            wide,
            pl.BlockSpec((length, 1), lambda p, r: (r, 0)),
            pl.BlockSpec((1, 1, length + 2 * HALO), lambda p, r: (r, 0, 0)),
            part(0), part(1), part(2),
            taps_spec,
            wide,
            whole(*gwo.shape), whole(*pu.shape), whole(*pd.shape), whole(*small.shape),
        ],
        out_specs=[
            pl.BlockSpec((length, width), lambda p, r: (jnp.where(p == quads - 1, r, 0), 0)),
        ]
        + [pl.BlockSpec(memory_space=pl.ANY)] * 4,
        out_shape=[
            jax.ShapeDtypeStruct((count, width), BF16),
            jax.ShapeDtypeStruct((quads + 1, grown, width // 2), BF16),
            jax.ShapeDtypeStruct((width, share), BF16),
            jax.ShapeDtypeStruct((share, width), BF16),
            jax.ShapeDtypeStruct((minis, PAIR), F32),
        ],
        scratch_shapes=[
            pltpu.VMEM((blocks, BLK, 2 * BLK), BF16),
            pltpu.VMEM((2, length + 2 * HALO, 2 * PAIR), BF16),
            pltpu.VMEM((2, length + 2 * HALO, PAIR), BF16),
            pltpu.VMEM((length, length), BF16),
            pltpu.VMEM((length, PAIR), F32),
            pltpu.VMEM((length, PAIR), F32),
            pltpu.VMEM((length, PAIR), F32),
            pltpu.VMEM((length, 3 * QUAD), BF16),
            pltpu.VMEM((width, 3 * QUAD), F32),
            pltpu.VMEM((count, width), F32),
            pltpu.VMEM((per, BLK, 2 * BLK), F32),
            pltpu.VMEM((quads, grown, width // 2), BF16),
            pltpu.VMEM((quads, 8, 3 * QUAD), F32),
            pltpu.VMEM((minis, PAIR), F32),
            pltpu.VMEM((quads + 1, grown, width // 2), BF16),
            pltpu.VMEM((width, share), BF16),
            pltpu.VMEM((share, width), BF16),
            pltpu.VMEM((minis, PAIR), F32),
            pltpu.SemaphoreType.DMA((quads + 2 + (width + share) // FFN_ROWS,)),
        ]
        + scratch,
        compiler_params=pltpu.CompilerParams(vmem_limit_bytes=60 * 2**20, collective_id=1, has_side_effects=True),
        name="attend_backward",
    )(dctx, att, inv, q, k, v, sq, sk, weight, slope, tokens, seg_col, seg_pad, w_qkv, w_qkv, w_qkv, flipped, dproj, gwo, pu, pd, small)


def body(
    tokens, segment_ids, w_qkv, b_qkv, conv_kernel, w_out, b_out, norm1_gain, norm1_bias,
    w_up, b_up, w_down, b_down, norm2_gain, norm2_bias, cotangent,
):
    seqs, length = segment_ids.shape
    width = tokens.shape[1]
    heads, span_of = conv_kernel.shape
    per = QUAD // HEAD
    radius = span_of // 2
    first_tap = HALO - radius

    def spread(kernel):
        padded = jnp.pad(kernel, ((0, 0), (first_tap, 2 * BLK - first_tap - span_of)))
        return padded.reshape(heads // per, per, 2 * BLK)

    seg_col = segment_ids.reshape(-1, 1)
    seg_pad = jnp.pad(segment_ids, ((0, 0), (HALO, HALO)), constant_values=-1)[:, None, :]
    taps, flipped = spread(conv_kernel), spread(conv_kernel[:, ::-1])

    up_all = lax.all_gather(w_up, "tensor")
    down_all = lax.all_gather(w_down, "tensor")
    bias_all = lax.all_gather(b_up, "tensor")[:, None, :]
    dp_size, tensor_size = lax.axis_size("dp"), lax.axis_size("tensor")
    share = w_up.shape[1]

    q, k, v, sq, sk, weight, slope, att, inv, ctx, res = attend(
        tokens, seg_col, seg_pad, w_qkv, b_qkv[None], taps, w_out, b_out[None], length
    )
    out, dproj, dctx, gwo, pu, pd, small = feed_forward(
        res, cotangent, ctx, w_out, norm1_gain[None], norm1_bias[None], norm2_gain[None], norm2_bias[None],
        b_down[None], bias_all, up_all, down_all,
    )
    gt, grads, grad_up, grad_down, few = attend_back(
        dctx, att, inv, q, k, v, sq, sk, weight, slope, tokens, seg_col, seg_pad, w_qkv, flipped, dproj,
        gwo, pu, pd, small, dp_size, tensor_size, length,
    )
    quads = width // QUAD
    grads = grads[:, : 2 * width].astype(F32).reshape(quads + 1, 2, width, width // 2).transpose(0, 2, 1, 3)
    grads = grads.reshape(quads + 1, width, width)
    gwo = grads[0]
    gw = grads[1:].reshape(quads, width, 3, QUAD).transpose(1, 2, 0, 3).reshape(width, 3 * width)
    lines = width // PAIR
    gg2, gs2, gbd, gg1, gs1, gbo = few[: 6 * lines].reshape(6, width)
    gbu = few[6 * lines : 6 * lines + tensor_size * share // PAIR].reshape(tensor_size, share)
    grad_b_up = lax.dynamic_index_in_dim(gbu, lax.axis_index("tensor"), 0, False)
    base = small.shape[0]
    gb = few[base : base + 3 * lines].reshape(quads, 3, QUAD).transpose(1, 0, 2).reshape(3 * width)
    base += 3 * lines
    first_lane = (first_tap + BLK - 1 + BLK) % (2 * BLK)
    grad_conv = few[base : base + heads, first_lane : first_lane + span_of]
    return (
        out, gt, gw, gb, grad_conv, gwo, gbo, gg1, gs1,
        grad_up.astype(F32), grad_b_up, grad_down.astype(F32), gbd, gg2, gs2,
    )


def solution(mesh):
    placed = (
        P(("dp", "tensor"), None),
        P(("dp", "tensor"), None),
        P(), P(), P(), P(), P(), P(), P(),
        P(None, "tensor"),
        P("tensor"),
        P("tensor", None),
        P(), P(), P(),
        P(("dp", "tensor"), None),
    )
    return jax.shard_map(
        body,
        mesh=mesh,
        in_specs=placed,
        out_specs=(
            P(("dp", "tensor"), None),
            P(("dp", "tensor"), None),
            P(), P(), P(), P(), P(), P(), P(),
            P(None, "tensor"),
            P("tensor"),
            P("tensor", None),
            P(), P(), P(),
        ),
        check_vma=False,
    )
```

```python
import functools
import math

import jax
import jax.numpy as jnp
from jax import lax
from jax.experimental import pallas as pl
from jax.experimental.pallas import tpu as pltpu
from jax.sharding import PartitionSpec as P

F32 = jnp.float32
BF16 = jnp.bfloat16
EPS_NORM = 1e-5
EPS_UNIT = 1e-6
SHRINK = 0.95
TAU = 8
SLOPE = TAU / math.pi
ARC = (0.49999996, -0.06830509, 0.02825875, -0.01557005, 0.00864352, -0.00363107, 0.00076235)
QUAD = 256
PAIR = 128
HEAD = 64
BLK = 128
HALO = 64


def dot_nn(a, b):
    return lax.dot_general(a, b, (((1,), (0,)), ((), ())), preferred_element_type=F32)


def dot_nt(a, b):
    return lax.dot_general(a, b, (((1,), (1,)), ((), ())), preferred_element_type=F32)


def dot_tn(a, b):
    return lax.dot_general(a, b, (((0,), (0,)), ((), ())), preferred_element_type=F32)


def lanes(shape):
    return lax.broadcasted_iota(jnp.int32, shape, len(shape) - 1)


def rows(shape):
    return lax.broadcasted_iota(jnp.int32, shape, len(shape) - 2)


def head_sum(values):
    width = values.shape[-1]
    ones = (rows((width, width)) // HEAD == lanes((width, width)) // HEAD).astype(BF16)
    high = values.astype(BF16)
    low = (values - high.astype(F32)).astype(BF16)
    return dot_nn(high, ones) + dot_nn(low, ones)


def closeness_terms(cosine):
    size = jnp.abs(cosine)
    room = 1.0 - size
    inverse = lax.rsqrt(room)
    poly = jnp.full_like(size, ARC[-1])
    for coefficient in ARC[-2::-1]:
        poly = poly * size + coefficient
    small = room * inverse * poly
    close = jnp.where(cosine >= 0.0, 1.0 - small, small)
    two = close * close
    four = two * two
    slope = (four * two) * (close * inverse) * lax.rsqrt(1.0 + size)
    return four * four, slope


def head_mask(half, shape):
    return (lanes(shape) // HEAD == half).astype(BF16)


def window_of(block, blocks):
    low = max(0, block * BLK - 256)
    high = min(blocks * BLK, block * BLK + BLK + 256)
    return low, high


def band(taps, count):
    spread = jnp.broadcast_to(taps, (count, taps.shape[1]))
    return pltpu.roll(spread, 0, 1, stride=1, stride_axis=0)


def norm_stats(values):
    centred = values - jnp.mean(values, -1, keepdims=True)
    scaling = lax.rsqrt(jnp.mean(centred * centred, -1, keepdims=True) + EPS_NORM)
    return centred * scaling, scaling


def build_masks(seg_col, seg_pad, same_ref, near_ref):
    length = seg_col.shape[0]
    for start in range(0, length, BLK):
        own = seg_col[start : start + BLK]
        same_ref[start : start + BLK, :] = jnp.where(
            own == seg_pad[:, HALO : HALO + length], 1.0, 0.0
        ).astype(BF16)
        near_ref[start // BLK] = jnp.where(
            own == seg_pad[:, start : start + 2 * BLK], 1.0, 0.0
        ).astype(BF16)


def build_near(seg_col, seg_pad, near_ref):
    length = seg_col.shape[0]
    for start in range(0, length, BLK):
        own = seg_col[start : start + BLK]
        near_ref[start // BLK] = jnp.where(
            own == seg_pad[:, start : start + 2 * BLK], 1.0, 0.0
        ).astype(BF16)


def attend_kernel(
    x_ref, col_ref, pad_ref, wq_ref, wk_ref, wv_ref, bq_ref, bk_ref, bv_ref, tap_ref, wo_ref, bo_ref,
    wu_ref, wd_ref, bu_ref,
    q_ref, k_ref, v_ref, sq_ref, sk_ref, w_ref, s_ref, att_ref, inv_ref, ctx_ref, res_ref,
    up_ref, down_ref, bias_ref,
    same_ref, near_ref, vv_ref, send_sem, recv_sem, copy_sem,
    *, dp_size, tensor_size,
):
    row, quad = pl.program_id(0), pl.program_id(1)
    quads, seqs = pl.num_programs(1), pl.num_programs(0)
    ticks = gather_plan(dp_size, tensor_size, (wu_ref, wd_ref, bu_ref), (up_ref, down_ref, bias_ref), (send_sem, recv_sem), copy_sem)
    length = x_ref.shape[0]
    blocks = length // BLK

    @pl.when(quad == 0)
    def _():
        build_masks(col_ref[...], pad_ref[0], same_ref, near_ref)
        for half in range(2):
            edge = jnp.zeros((HALO, 2 * PAIR), BF16)
            vv_ref[half, :HALO] = edge
            vv_ref[half, HALO + length :] = edge
            vv_ref[half, HALO : HALO + length, PAIR:] = head_mask(half, (length, PAIR))

    for start in range(0, length, BLK):
        here = slice(start, start + BLK)
        x = x_ref[here]
        for w, b, unit, scale, factor in (
            (wq_ref, bq_ref, q_ref, sq_ref, SHRINK),
            (wk_ref, bk_ref, k_ref, sk_ref, 1.0),
        ):
            part = dot_nn(x, w[...]) + b[...]
            scaling = lax.rsqrt(head_sum(part * part) + EPS_UNIT)
            unit[here] = (part * (scaling * factor)).astype(BF16)
            scale[here] = scaling.astype(BF16)
        v_ref[here] = (dot_nn(x, wv_ref[...]) + bv_ref[...]).astype(BF16)

    def one_pair(pair, carry):
        turn = (row * quads + quad) * (QUAD // PAIR) + pair
        for when, events in ticks.items():

            @pl.when(turn == when)
            def _(events=events):
                for event in events:
                    event()

        at = pl.ds(pl.multiple_of(pair * PAIR, PAIR), PAIR)
        v = v_ref[:, at]
        for half in range(2):
            vv_ref[half, HALO : HALO + length, :PAIR] = v * head_mask(half, (length, PAIR))
        for block in range(blocks):
            here = slice(block * BLK, block * BLK + BLK)
            low, high = window_of(block, blocks)
            q = q_ref[here, at]
            total = jnp.zeros((BLK, 2 * PAIR), F32)
            near = jnp.zeros((BLK, PAIR), F32)
            for half in range(2):
                head = pair * 2 + half
                q_half = q * head_mask(half, (BLK, PAIR))
                for start in range(low, high, KCH):
                    stop = min(start + KCH, high)
                    cosine = dot_nt(q_half, k_ref[start:stop, at])
                    weight, slope = closeness_terms(cosine)
                    same = same_ref[here, start:stop]
                    weight = weight.astype(BF16) * same
                    w_ref[0, head, here, start:stop] = weight
                    s_ref[0, head, here, start:stop] = slope.astype(BF16) * same
                    total += dot_nn(weight, vv_ref[half, HALO + start : HALO + stop])
                if low > 0:
                    w_ref[0, head, here, :low] = jnp.zeros((BLK, low), BF16)
                if high < length:
                    w_ref[0, head, here, high:] = jnp.zeros((BLK, length - high), BF16)
                taps = band(tap_ref[0, pl.ds(head, 1)], BLK).astype(BF16) * near_ref[block]
                near += dot_nn(taps, vv_ref[half, block * BLK : block * BLK + 2 * BLK, :PAIR])
            inverse = 1.0 / (1.0 + total[:, PAIR:])
            attended = total[:, :PAIR] * inverse
            att_ref[here, at] = attended.astype(BF16)
            inv_ref[here, at] = inverse.astype(BF16)
            ctx_ref[here, at] = (attended + near).astype(BF16)
        return carry

    lax.fori_loop(0, QUAD // PAIR, one_pair, 0)

    @pl.when(quad == 0)
    def _():
        res_ref[...] = x_ref[...].astype(F32) + bo_ref[...]

    for start in range(0, length, BLK):
        here = slice(start, start + BLK)
        res_ref[here] += dot_nn(ctx_ref[here], wo_ref[...])


def gather_plan(dp_size, tensor_size, own, whole, sems, copy_sem):
    axes = slice_axes(dp_size, tensor_size)
    y, x, core = axes["y"], axes["x"], axes["core"]
    mate = core.device(core.ahead(1))
    number = iter(range(1000))

    def mine(place):
        return place * CORES + core.place

    def rows_at(ref, place):
        size = ref.shape[-2] // x.size
        return span(place * size, size)

    def at_y(which):
        source, target = own[which], whole[which]
        out = []
        for j in range(1, y.size):
            if which < 2:
                block = rows_at(source, x.place)
                pair = (source.at[block], target.at[mine(y.place), block])
            else:
                pair = (source, target.at[mine(y.place)])
            out.append(send(*pair, sems, next(number), y.device(y.ahead(j))))
        return out

    def at_x(which):
        target = whole[which]
        out = []
        for j in range(1, y.size):
            block = target.at[mine(y.ahead(j)), rows_at(target, x.place)]
            out += [send(block, block, sems, next(number), x.device(x.ahead(i))) for i in range(1, x.size)]
        return out

    def to_mate(which):
        target = whole[which]
        return [
            send(target.at[mine(y.ahead(j))], target.at[mine(y.ahead(j))], sems, next(number), mate)
            for j in range(1, y.size)
        ]

    keep = [pltpu.make_async_copy(own[i], whole[i].at[mine(y.place)], copy_sem.at[i]) for i in range(3)]
    give = [send(own[i], whole[i].at[mine(y.place)], sems, next(number), mate) for i in range(3)]
    ys, xs, mates = [at_y(i) for i in range(3)], [at_x(i) for i in range(2)], [to_mate(i) for i in range(3)]

    def start(copies):
        return [copy.start for copy in copies]

    def wait(copies):
        return [copy.wait for copy in copies]

    steps = [
        [lambda: greet(axes, ("core", "y", "x"))] + start(ys[0] + ys[2] + give + keep),
        wait(ys[0] + ys[2]) + start(xs[0] + ys[1] + mates[2]),
        wait(xs[0] + ys[1]) + start(mates[0] + xs[1]),
        wait(xs[1]) + start(mates[1]),
    ]
    last = wait(mates[0] + mates[1] + mates[2] + give + keep)
    return dict(zip(GATHER_TIMES, steps)) | {GATHER_TIMES[len(steps)]: last}


GATHER_TIMES = (0, 4, 7, 10, 11)


KCH = 256


def attend(tokens, seg_col, seg_pad, w_qkv, vectors, taps, w_out, w_up, w_down, b_up, dp_size, tensor_size, length):
    count, width = tokens.shape
    seqs = count // length
    quads = width // QUAD
    heads = width // HEAD
    per = QUAD // HEAD
    blocks = length // BLK
    own = pl.BlockSpec((length, QUAD), lambda r, p: (r, p))
    act = jax.ShapeDtypeStruct((count, width), BF16)
    big = jax.ShapeDtypeStruct((seqs, heads, length, length), BF16)
    big_spec = pl.BlockSpec((1, per, length, length), lambda r, p: (r, p, 0, 0))

    def part(rows_of, k):
        return pl.BlockSpec((rows_of, QUAD), lambda r, p, k=k: (0, p + k * quads))

    others = tensor_size // CORES - 1
    copies = 3 + 6 * others + 2 * others * (dp_size // DEPTH - 1)
    return pl.pallas_call(
        functools.partial(attend_kernel, dp_size=dp_size, tensor_size=tensor_size),
        grid=(seqs, quads),
        in_specs=[
            pl.BlockSpec((length, width), lambda r, p: (r, 0)),
            pl.BlockSpec((length, 1), lambda r, p: (r, 0)),
            pl.BlockSpec((1, 1, length + 2 * HALO), lambda r, p: (r, 0, 0)),
            part(width, 0), part(width, 1), part(width, 2),
            part(1, 0), part(1, 1), part(1, 2),
            pl.BlockSpec((1, per, 2 * BLK), lambda r, p: (p, 0, 0)),
            pl.BlockSpec((QUAD, width), lambda r, p: (p, 0)),
            pl.BlockSpec((1, width), lambda r, p: (0, 3)),
        ]
        + [
            pl.BlockSpec(part.shape, lambda r, p: (0, 0), pipeline_mode=pl.Buffered(1))
            for part in (w_up, w_down, b_up)
        ],
        out_specs=[own] * 5 + [big_spec] * 2 + [own] * 3 + [pl.BlockSpec((length, width), lambda r, p: (r, 0))]
        + [pl.BlockSpec(memory_space=pl.ANY)] * 3,
        out_shape=[act] * 5 + [big] * 2 + [act] * 3 + [jax.ShapeDtypeStruct((count, width), F32)]
        + [jax.ShapeDtypeStruct((tensor_size,) + part.shape, part.dtype) for part in (w_up, w_down, b_up)],
        scratch_shapes=[
            pltpu.VMEM((length, length), BF16),
            pltpu.VMEM((blocks, BLK, 2 * BLK), BF16),
            pltpu.VMEM((2, length + 2 * HALO, 2 * PAIR), BF16),
            pltpu.SemaphoreType.DMA((copies,)),
            pltpu.SemaphoreType.DMA((copies,)),
            pltpu.SemaphoreType.DMA((3,)),
        ],
        compiler_params=pltpu.CompilerParams(vmem_limit_bytes=56 * 2**20, collective_id=2, has_side_effects=True),
        name="attend_forward",
    )(tokens, seg_col, seg_pad, w_qkv, w_qkv, w_qkv, vectors, vectors, vectors, taps, w_out, vectors, w_up, w_down, b_up)


DEPTH = 4
CORES = 2


class Axis:
    def __init__(self, size, place, device):
        self.size, self.place, self.device = size, place, device

    def ahead(self, j):
        return lax.rem(self.place + j, self.size)


def slice_axes(dp_size, tensor_size):
    dp, tensor = lax.axis_index("dp"), lax.axis_index("tensor")
    across = dp_size // DEPTH
    z, x = dp // across, lax.rem(dp, across)
    y, core = tensor // CORES, lax.rem(tensor, CORES)
    return {
        "core": Axis(CORES, core, lambda p: (dp, y * CORES + p)),
        "y": Axis(tensor_size // CORES, y, lambda p: (dp, p * CORES + core)),
        "x": Axis(across, x, lambda p: (z * across + p, tensor)),
        "z": Axis(DEPTH, z, lambda p: (p * across + x, tensor)),
    }


def greet(axes, names=("core", "y", "x", "z")):
    barrier = pltpu.get_barrier_semaphore()
    count = 0
    for axis in (axes[name] for name in names):
        for j in range(1, axis.size):
            pl.semaphore_signal(
                barrier, inc=1, device_id=axis.device(axis.ahead(j)), device_id_type=pl.DeviceIdType.MESH
            )
            count += 1
    pl.semaphore_wait(barrier, count)


def send(source, target, sems, at, device):
    return pltpu.make_async_remote_copy(
        src_ref=source, dst_ref=target, send_sem=sems[0].at[at], recv_sem=sems[1].at[at],
        device_id=device, device_id_type=pl.DeviceIdType.MESH,
    )


def span(start, size):
    if isinstance(start, int):
        return pl.ds(start, size)
    return pl.ds(pl.multiple_of(start, math.gcd(size, 16)), size)


def add_rows(target, target_at, terms, size):
    tile = next(t for t in (64, 48, 32, 24, 16, 12, 8) if size % t == 0)

    def one(i, carry):
        total = None
        for ref, start in terms:
            rows_of = ref[span(start + i * tile, tile)].astype(F32)
            total = rows_of if total is None else total + rows_of
        target[span(target_at + i * tile, tile)] = total.astype(target.dtype)
        return carry

    lax.fori_loop(0, size // tile, one, 0)


class Reduction:
    def __init__(self, axes, order, back, source, source_at, size, final, final_at, landings, sems, first_sem=0):
        self.axes, self.order, self.back = axes, order, back
        self.source, self.source_at, self.size = source, source_at, size
        self.final, self.final_at = final, final_at
        self.landings, self.sems = landings, sems
        self.first_sem = first_sem

    def plan(self):
        size, at, out = self.size, self.final_at, []
        for name in self.order:
            axis = self.axes[name]
            size //= axis.size
            at = at + axis.place * size
            out.append((axis, size, at))
        return out

    def copies(self, stage):
        stages = self.plan()
        sem = self.first_sem
        for axis, _, _ in stages[:stage]:
            sem += axis.size - 1
        axis, size, _ = stages[stage]
        held, held_at = (self.source, self.source_at) if stage == 0 else (self.landings[stage - 1].at[0], 0)
        return [
            send(
                held.at[span(held_at + axis.ahead(j) * size, size)], self.landings[stage].at[j - 1],
                self.sems, sem + j - 1, axis.device(axis.ahead(j)),
            )
            for j in range(1, axis.size)
        ]

    def settle(self, stage):
        for copy in self.copies(stage):
            copy.wait()
        axis, size, final_at = self.plan()[stage]
        held, held_at = (self.source, self.source_at) if stage == 0 else (self.landings[stage - 1].at[0], 0)
        terms = [(held, held_at + axis.place * size)]
        terms += [(self.landings[stage].at[j - 1], 0) for j in range(1, axis.size)]
        if stage == len(self.order) - 1:
            add_rows(self.final, final_at, terms, size)
        else:
            add_rows(self.landings[stage].at[0], 0, terms, size)

    def gathers(self, which):
        stages = self.plan()
        sem = self.first_sem + sum(axis.size - 1 for axis, _, _ in stages)
        for name in self.back[:which]:
            sem += self.axes[name].size - 1
        depth = self.order.index(self.back[which])
        axis, size, at = stages[depth]
        block = self.final.at[span(at, size)]
        return [send(block, block, self.sems, sem + j - 1, axis.device(axis.ahead(j))) for j in range(1, axis.size)]

    def events(self):
        out = []
        count = len(self.order)

        def begin(copies):
            for copy in copies:
                copy.start()

        for stage in range(count):
            def event(stage=stage):
                if stage > 0:
                    self.settle(stage - 1)
                begin(self.copies(stage))

            out.append(event)
        for which in range(len(self.back)):
            def event(which=which):
                if which == 0:
                    self.settle(count - 1)
                else:
                    for copy in self.gathers(which - 1):
                        copy.wait()
                begin(self.gathers(which))

            out.append(event)

        def last():
            for copy in self.gathers(len(self.back) - 1):
                copy.wait()

        out.append(last)
        return out


def landing_shapes(order, sizes, size, columns, dtype):
    shapes = []
    for name in order:
        size //= sizes[name]
        shapes.append(pltpu.VMEM((sizes[name] - 1, size, columns), dtype))
    return shapes


def copies_of(order, back, sizes):
    return sum(sizes[name] - 1 for name in order) + sum(sizes[name] - 1 for name in back)

GELU_A = math.sqrt(2.0 / math.pi)
GELU_B = 0.044715
TILE = 256
UNROLL = 4


def gelu_terms(pre):
    square = pre * pre
    swing = jnp.tanh(pre * (GELU_A + GELU_A * GELU_B * square))
    gate = 0.5 + 0.5 * swing
    steep = GELU_A + 3.0 * GELU_A * GELU_B * square
    return pre * gate, gate + 0.5 * pre * (1.0 - swing * swing) * steep


def norm_backward(grad_out, unit, scaling, gain):
    grad_unit = grad_out * gain
    return scaling * (
        grad_unit
        - jnp.mean(grad_unit, -1, keepdims=True)
        - unit * jnp.mean(grad_unit * unit, -1, keepdims=True)
    )


def column_sum(values):
    return jnp.sum(values, 0, keepdims=True)


def ffn_kernel(
    res_ref, cot_ref, ctx_ref, wo_ref, gain1_ref, shift1_ref, gain2_ref, shift2_ref, bd_ref, bu_ref, wu_ref, wd_ref,
    out_ref, dproj_ref, dctx_ref, gwo_ref, pu_ref, pd_ref, small_ref,
    low_ref, acc_ref, hid_ref, slope_ref, dffn_ref, dpre_ref, sendu_ref, sendd_ref, recvu_ref, recvd_ref, pdown_ref, yland_ref,
    send_sem, recv_sem,
):
    parts = pl.num_programs(0) // 2
    step = pl.program_id(0)
    count, width = res_ref.shape
    share = dpre_ref.shape[1]
    tiles = count // TILE
    f = part_order(step, parts)
    late = jnp.maximum(step - parts, 0)
    heights = parts // CORES
    slot = late // CORES
    dp, tensor = lax.axis_index("dp"), lax.axis_index("tensor")
    height, core = tensor // CORES, lax.rem(tensor, CORES)
    mate = (dp, height * CORES + 1 - core)

    def up_to_mate(which):
        return send(sendu_ref.at[which], recvu_ref.at[which], (send_sem.at[0], recv_sem.at[0]), which, mate)

    def down_to_mate(which):
        return send(sendd_ref.at[which], recvd_ref.at[which], (send_sem.at[1], recv_sem.at[1]), which, mate)

    def to_height(which):
        there = (dp, lax.rem(height + 1 + which, heights) * CORES + core)
        return send(pdown_ref.at[which], yland_ref.at[which], (send_sem.at[2], recv_sem.at[2]), which, there)

    def down_part(late):
        part = part_order(parts + late, parts)
        piece = math.gcd(TILE, share)
        for start in range(0, share, piece):
            cut = slice(start, start + piece)
            yield cut, dot_tn(hid_ref[part, :, cut], dffn_ref[...]).astype(BF16)

    @pl.when(step == 0)
    def _():
        barrier = pltpu.get_barrier_semaphore()
        peers = [mate] + [(dp, lax.rem(height + j, heights) * CORES + core) for j in range(1, heights)]
        for peer in peers:
            pl.semaphore_signal(barrier, inc=1, device_id=peer, device_id_type=pl.DeviceIdType.MESH)
        pl.semaphore_wait(barrier, len(peers))

    def put_row(row, values):
        for i in range(values.shape[1] // PAIR):
            small_ref[pl.ds(row + i, 1)] = values[:, i * PAIR : (i + 1) * PAIR]

    def at(t):
        return pl.ds(pl.multiple_of(t * TILE, TILE), TILE)

    @pl.when(step == 0)
    def _():
        def one(t, carry):
            unit, _ = norm_stats(res_ref[at(t)])
            low_ref[at(t)] = (unit * gain1_ref[...] + shift1_ref[...]).astype(BF16)
            acc_ref[at(t)] = jnp.zeros((TILE, width), F32)
            return carry

        lax.fori_loop(0, tiles, one, 0, unroll=UNROLL)

    @pl.when(step < parts)
    def _():
        def one(t, carry):
            pre = dot_nn(low_ref[at(t)], wu_ref[0]) + bu_ref[0].astype(F32)
            hidden, slope = gelu_terms(pre)
            hidden = hidden.astype(BF16)
            hid_ref[f, at(t)] = hidden
            slope_ref[f, at(t)] = slope.astype(BF16)
            acc_ref[at(t)] += dot_nn(hidden, wd_ref[0])
            return carry

        lax.fori_loop(0, tiles, one, 0, unroll=UNROLL)

    @pl.when(step == parts)
    def _():
        def one(t, sums):
            unit, _ = norm_stats(res_ref[at(t)])
            first = unit * gain1_ref[...] + shift1_ref[...]
            unit, scaling = norm_stats(first + acc_ref[at(t)] + bd_ref[...])
            out_ref[at(t)] = (unit * gain2_ref[...] + shift2_ref[...]).astype(BF16)
            grad = cot_ref[at(t)].astype(F32)
            d_res = norm_backward(grad, unit, scaling, gain2_ref[...])
            d_ffn = d_res.astype(BF16)
            acc_ref[at(t)] = d_res
            dffn_ref[at(t)] = d_ffn
            return (
                sums[0] + column_sum(grad * unit),
                sums[1] + column_sum(grad),
                sums[2] + column_sum(d_ffn.astype(F32)),
            )

        zero = jnp.zeros((1, width), F32)
        sums = lax.fori_loop(0, tiles, one, (zero, zero, zero), unroll=UNROLL)
        small_ref[...] = jnp.zeros_like(small_ref)
        for i, values in enumerate(sums):
            put_row(i * (width // PAIR), values)

        def theirs(which, carry):
            for cut, values in down_part(CORES * which):
                sendd_ref[which, cut] = values
            down_to_mate(which).start()
            return carry

        def ours(which, carry):
            for cut, values in down_part(CORES * which + 1):
                pdown_ref[which, cut] = values
            return carry

        lax.fori_loop(0, heights, theirs, 0)
        lax.fori_loop(0, heights, ours, 0)

    @pl.when(step >= parts)
    def _():
        def one(t, total):
            d_hidden = dot_nt(dffn_ref[at(t)], wd_ref[0])
            d_pre = (d_hidden * slope_ref[f, at(t)].astype(F32)).astype(BF16)
            dpre_ref[at(t)] = d_pre
            acc_ref[at(t)] += dot_nt(d_pre, wu_ref[0])
            return total + column_sum(d_pre.astype(F32))

        bias = lax.fori_loop(0, tiles, one, jnp.zeros((1, share), F32), unroll=UNROLL)
        put_row(6 * (width // PAIR) + f * (share // PAIR), bias)

        for which in range(heights):

            @pl.when(late == which)
            def _(which=which):
                down_to_mate(which).wait()
                add_rows(pdown_ref.at[which], 0, [(pdown_ref.at[which], 0), (recvd_ref.at[which], 0)], share)
                if which < heights - 1:
                    to_height(which).start()

        @pl.when(lax.rem(late, CORES) == 0)
        def _():
            for start in range(0, width, TILE):
                cut = slice(start, start + TILE)
                sendu_ref[slot, cut] = dot_tn(low_ref[:, cut], dpre_ref[...]).astype(BF16)
            up_to_mate(slot).start()

        @pl.when(lax.rem(late, CORES) == 1)
        def _():
            up_to_mate(slot).wait()
            for start in range(0, width, TILE):
                cut = slice(start, start + TILE)
                values = dot_tn(low_ref[:, cut], dpre_ref[...])
                pu_ref[slot, cut] = (values + recvu_ref[slot, cut].astype(F32)).astype(BF16)

    @pl.when(step == 2 * parts - 1)
    def _():
        def one(t, sums):
            unit, scaling = norm_stats(res_ref[at(t)])
            grad = acc_ref[at(t)]
            d_proj = norm_backward(grad, unit, scaling, gain1_ref[...]).astype(BF16)
            dproj_ref[at(t)] = d_proj
            dctx_ref[at(t)] = dot_nt(d_proj, wo_ref[...]).astype(BF16)
            return (
                sums[0] + column_sum(grad * unit),
                sums[1] + column_sum(grad),
                sums[2] + column_sum(d_proj.astype(F32)),
            )

        zero = jnp.zeros((1, width), F32)
        sums = lax.fori_loop(0, tiles, one, (zero, zero, zero), unroll=UNROLL)
        for i, values in enumerate(sums):
            put_row((3 + i) * (width // PAIR), values)
        for start in range(0, width, TILE):
            values = dot_tn(ctx_ref[:, start : start + TILE], dproj_ref[...]).astype(BF16)
            gwo_ref[start : start + TILE] = values[:, : width // 2]
            gwo_ref[width + start : width + start + TILE] = values[:, width // 2 :]
        for which in range(heights - 1):
            to_height(which).wait()
        terms = [(pdown_ref.at[heights - 1], 0)] + [(yland_ref.at[which], 0) for which in range(heights - 1)]
        add_rows(pd_ref, 0, terms, share)


def part_order(step, parts):
    tensor = lax.axis_index("tensor")
    height, core = tensor // CORES, lax.rem(tensor, CORES)
    late = jnp.maximum(step - parts, 0)
    there = lax.rem(height + 1 + late // CORES, parts // CORES)
    whose = jnp.where(lax.rem(late, CORES) == 0, 1 - core, core)
    return jnp.where(step < parts, step, there * CORES + whose)


def feed_forward(res, cot, ctx, w_out, vectors, b_up, w_up, w_down):
    count, width = res.shape
    parts, _, share = w_up.shape
    heights = parts // 2
    smalls = 6 * width // PAIR + parts * share // PAIR
    smalls = -(-smalls // 8) * 8

    def whole(*shape):
        return pl.BlockSpec(shape, lambda s: (0,) * len(shape), pipeline_mode=pl.Buffered(1))

    def per_part(*shape):
        return pl.BlockSpec((1,) + shape, lambda s: (part_order(s, parts),) + (0,) * len(shape))

    act = jax.ShapeDtypeStruct((count, width), BF16)
    return pl.pallas_call(
        ffn_kernel,
        grid=(2 * parts,),
        in_specs=[whole(count, width)] * 3
        + [whole(width, width)]
        + [pl.BlockSpec((1, width), lambda s, k=k: (0, k), pipeline_mode=pl.Buffered(1)) for k in range(4, 9)]
        + [per_part(1, share), per_part(width, share), per_part(share, width)],
        out_specs=[whole(count, width)] * 3
        + [whole(2 * width, width // 2), whole(heights, width, share), whole(share, width), whole(smalls, PAIR)],
        out_shape=[act] * 3
        + [
            jax.ShapeDtypeStruct((2 * width, width // 2), BF16),
            jax.ShapeDtypeStruct((heights, width, share), BF16),
            jax.ShapeDtypeStruct((share, width), BF16),
            jax.ShapeDtypeStruct((smalls, PAIR), F32),
        ],
        scratch_shapes=[
            pltpu.VMEM((count, width), BF16),
            pltpu.VMEM((count, width), F32),
            pltpu.VMEM((parts, count, share), BF16),
            pltpu.VMEM((parts, count, share), BF16),
            pltpu.VMEM((count, width), BF16),
            pltpu.VMEM((count, share), BF16),
            pltpu.VMEM((heights, width, share), BF16),
            pltpu.VMEM((heights, share, width), BF16),
            pltpu.VMEM((heights, width, share), BF16),
            pltpu.VMEM((heights, share, width), BF16),
            pltpu.VMEM((heights, share, width), BF16),
            pltpu.VMEM((heights - 1, share, width), BF16),
            pltpu.SemaphoreType.DMA((3, heights)),
            pltpu.SemaphoreType.DMA((3, heights)),
        ],
        compiler_params=pltpu.CompilerParams(vmem_limit_bytes=60 * 2**20, collective_id=0, has_side_effects=True),
        name="feed_forward",
    )(res, cot, ctx, w_out, *[vectors] * 5, b_up, w_up, w_down)


def attend_back_kernel(
    dctx_ref, att_ref, inv_ref, q_ref, k_ref, v_ref, sq_ref, sk_ref, w_ref, s_ref, x_ref, col_ref, pad_ref,
    wqkv_ref, flip_ref, dproj_ref, gwo_ref, pu_ref, pd_ref, small_ref,
    gt_ref, all_out, up_out, down_out, few_out,
    near_ref, vv_ref, dpad_ref, dcos_ref, dq_ref, dk_ref, dv_ref, joined_ref, gwacc_ref, conv_ref,
    gwlow_ref, gb_ref, mini_ref, all_ref, up_ref, down_ref, few_ref, out_sem, *links,
    plan, quads, seqs,
):
    quad, row = pl.program_id(0), pl.program_id(1)
    length = x_ref.shape[0]
    blocks = length // BLK
    inside = slice(HALO, HALO + length)

    _, sizes, dp_size, tensor_size = plan
    axes = slice_axes(dp_size, tensor_size)
    ticks = schedule(axes, sizes, quads, seqs, gwo_ref, pu_ref, pd_ref, gwlow_ref, mini_ref, all_ref, up_ref, down_ref, few_ref, links,
        (all_out, up_out, down_out, few_out, out_sem))
    calls = quads * seqs * (QUAD // HEAD)

    build_near(col_ref[...], pad_ref[0], near_ref)
    for half in range(2):
        edge = jnp.zeros((HALO, PAIR), BF16)
        for ref in (vv_ref, dpad_ref):
            ref[half, :HALO, :PAIR] = edge
            ref[half, HALO + length :, :PAIR] = edge
        vv_ref[half, inside, PAIR:] = head_mask(half, (length, PAIR))

    @pl.when(row == 0)
    def _():
        conv_ref[...] = jnp.zeros_like(conv_ref)
        gwacc_ref[...] = jnp.zeros_like(gwacc_ref)

    @pl.when((quad == 0) & (row == 0))
    def _():
        gb_ref[...] = jnp.zeros_like(gb_ref)
        mini_ref[...] = jnp.zeros_like(mini_ref)
        mini_ref[: small_ref.shape[0]] = small_ref[...]
        filled = 2 * gwacc_ref.shape[0]
        if gwlow_ref.shape[1] > filled:
            gwlow_ref[:, filled:] = jnp.zeros((quads, gwlow_ref.shape[1] - filled, gwlow_ref.shape[2]), BF16)

    def one_pair(pair, carry):
        at = pl.ds(pl.multiple_of(pair * PAIR, PAIR), PAIR)
        inverse = inv_ref[:, at].astype(F32)
        d_ctx = dctx_ref[:, at]
        d_summed = (d_ctx.astype(F32) * inverse).astype(BF16)
        d_total = (-d_summed.astype(F32) * att_ref[:, at].astype(F32)).astype(BF16)
        both = jnp.concatenate([d_summed, d_total], 1)
        dk = jnp.zeros((length, PAIR), F32)
        dv = jnp.zeros((length, PAIR), F32)
        turn = (quad * seqs + row) * (QUAD // PAIR) + pair
        for half in range(2):
            for when in range(half, calls, 2):
                if ticks.get(when):

                    @pl.when(turn == when // 2)
                    def _(when=when):
                        for event in ticks[when]:
                            event()

            head = pair * 2 + half
            mask = head_mask(half, (length, PAIR))
            vv_ref[half, inside, :PAIR] = v_ref[:, at] * mask
            dpad_ref[half, inside] = d_ctx * mask
            k_half = k_ref[:, at] * mask
            for block in range(blocks):
                here = slice(block * BLK, block * BLK + BLK)
                low, high = window_of(block, blocks)
                d_weight = dot_nt(both[here], vv_ref[half, HALO + low : HALO + high])
                d_cos = d_weight.astype(BF16) * s_ref[0, head, here, low:high]
                dcos_ref[here, low:high] = d_cos
                if low > 0:
                    dcos_ref[here, :low] = jnp.zeros((BLK, low), BF16)
                if high < length:
                    dcos_ref[here, high:] = jnp.zeros((BLK, length - high), BF16)
                grown = dot_nn(d_cos, k_half[low:high])
                if half == 0:
                    dq_ref[here] = grown
                else:
                    dq_ref[here] += grown
                window = slice(block * BLK, block * BLK + 2 * BLK)
                near = near_ref[block]
                taps = band(flip_ref[0, pl.ds(head, 1)], BLK).astype(BF16) * near
                grown = dot_nn(taps, dpad_ref[half, window])
                if half == 0:
                    dv_ref[here] = grown
                else:
                    dv_ref[here] += grown
                conv_ref[head] += near.astype(F32) * dot_nt(d_ctx[here], vv_ref[half, window, :PAIR])
            dk += dot_tn(dcos_ref[...], q_ref[:, at] * mask)
            dv += dot_tn(w_ref[0, head], d_summed * mask)
        dv_ref[...] += dv
        grad = SLOPE * dq_ref[...]
        unit = q_ref[:, at].astype(F32)
        d_query = sq_ref[:, at].astype(F32) * (SHRINK * grad - unit * (head_sum(grad * unit) / SHRINK))
        grad = SLOPE * dk
        unit = k_ref[:, at].astype(F32)
        d_key = sk_ref[:, at].astype(F32) * (grad - unit * head_sum(grad * unit))
        for part, values in enumerate((d_query, d_key, dv_ref[...])):
            joined_ref[quad, row, :, pl.ds(pl.multiple_of(part * QUAD + pair * PAIR, PAIR), PAIR)] = values.astype(BF16)
        return carry

    lax.fori_loop(0, QUAD // PAIR, one_pair, 0)

    gb_ref[quad, :1] += column_sum(joined_ref[quad, row].astype(F32))
    width = gwacc_ref.shape[0]
    for start in range(0, width, TILE):
        cut = slice(start, start + TILE)
        gwacc_ref[cut] += dot_tn(x_ref[:, cut], joined_ref[quad, row])

    @pl.when(row == seqs - 1)
    def _():
        half = gwacc_ref.shape[1] // 2
        for start in range(0, width, TILE):
            for side in range(2):
                values = gwacc_ref[start : start + TILE, side * half : (side + 1) * half]
                gwlow_ref[quad, side * width + start : side * width + start + TILE] = values.astype(BF16)
        base = small_ref.shape[0]
        lines = gb_ref.shape[2] // PAIR
        for i in range(lines):
            mini_ref[pl.ds(base + quad * lines + i, 1)] = gb_ref[quad, :1, i * PAIR : (i + 1) * PAIR]
        base += quads * lines
        for head in range(QUAD // HEAD):
            sums = conv_ref[head]
            high = sums.astype(BF16)
            turn = (rows((BLK, BLK)) + lanes((BLK, BLK)) == BLK - 1).astype(BF16)
            turned = dot_nn(turn, high) + dot_nn(turn, (sums - high.astype(F32)).astype(BF16))
            turned = pltpu.roll(turned, BLK, 1, stride=1, stride_axis=0)
            mini_ref[pl.ds(base + quad * (QUAD // HEAD) + head, 1)] = column_sum(turned)[:, :PAIR]

    last = (quad == quads - 1) & (row == seqs - 1)

    @pl.when(last)
    def _():
        for event in ticks.get(calls, ()):
            event()

    @pl.when(quad == quads - 1)
    def _():
        for start in range(0, length, TILE):
            cut = slice(start, start + TILE)
            grown = dproj_ref[cut].astype(F32)
            for q in range(quads):
                for part in range(3):
                    to = part * width + q * QUAD
                    grown += dot_nt(joined_ref[q, row, cut, part * QUAD : (part + 1) * QUAD], wqkv_ref[:, to : to + QUAD])
            gt_ref[cut] = grown.astype(BF16)

    @pl.when(last)
    def _():
        for when in sorted(ticks):
            if when > calls:
                for event in ticks[when]:
                    event()


FFN_TIMES = (
    ((3, 7, 14, 21, 34), (0, 4, 8, 16, 25)),
    ((0, 8, 12, 20, 37, 50), (5, 17, 29, 48, 57, 61)),
)
ALL_TIMES = (
    (6, 8, 15, 19, 26, 39, 47, 52, 56),
    (10, 12, 16, 19, 27, 40, 46, 53, 58),
    (16, 18, 22, 32, 44, 51, 55, 60, 62),
    (25, 30, 36, 42, 49, 54, 59, 63, 64),
)
MINI_TIMES = (25, 28, 31, 33, 35, 38, 41, 43, 45)
FFN_ROWS = 384
FFN_ORDER = ("y", "x", "z")
FFN_BACK = ("z", "x")
ORDERS = (("core", "x", "y", "z"), ("core", "y", "x", "z"))
CHOICE = (1, 0, 1, 1)


def all_order(index):
    order = ORDERS[CHOICE[index]]
    return order, order[::-1]


class FfnReduction(Reduction):
    def copies(self, stage):
        if stage > 0:
            return super().copies(stage)
        axis = self.axes["y"]
        return [
            send(
                self.source.at[j - 1, span(self.source_at, self.size)], self.landings[0].at[j - 1],
                self.sems, self.first_sem + j - 1, axis.device(axis.ahead(j)),
            )
            for j in range(1, axis.size)
        ]

    def plan(self):
        size, at = self.size, self.final_at
        out = [(self.axes["y"], size, at)]
        for name in self.order[1:]:
            axis = self.axes[name]
            size //= axis.size
            at = at + axis.place * size
            out.append((axis, size, at))
        return out

    def settle(self, stage):
        if stage > 0:
            return super().settle(stage)
        axis = self.axes["y"]
        for copy in self.copies(0):
            copy.wait()
        terms = [(self.source.at[axis.size - 1], self.source_at)]
        terms += [(self.landings[0].at[j - 1], 0) for j in range(1, axis.size)]
        add_rows(self.landings[0].at[0], 0, terms, self.size)


def link_plan(sizes, width, share, quads):
    out = []
    devices = math.prod(sizes.values())
    y = sizes["y"]
    for height, columns, order in ((share, width, FFN_ORDER[1:]), (width, share, FFN_ORDER)):
        for _ in range(height // FFN_ROWS):
            shapes = [pltpu.VMEM((y - 1, FFN_ROWS, columns), BF16)] if order is FFN_ORDER else []
            shapes += landing_shapes(FFN_ORDER[1:], sizes, FFN_ROWS, columns, BF16)
            out.append((shapes, copies_of(order, FFN_BACK, sizes)))
    for index in range(quads + 1):
        order, back = all_order(index)
        out.append((landing_shapes(order, sizes, padded(2 * width, devices), width // 2, BF16), copies_of(order, back, sizes)))
    order, back = all_order(quads)
    out.append((landing_shapes(order, sizes, 8 * devices, PAIR, F32), copies_of(order, back, sizes)))
    return out


def padded(size, devices):
    return -(-size // (16 * devices)) * 16 * devices


def schedule(axes, sizes, quads, seqs, gwo_ref, pu_ref, pd_ref, gwlow_ref, mini_ref, all_ref, up_ref, down_ref, few_ref, links, outs):
    all_out, up_out, down_out, few_out, out_sem = outs
    calls = quads * seqs * (QUAD // HEAD)
    share, width = pd_ref.shape
    devices = math.prod(sizes.values())
    groups = link_plan(sizes, width, share, quads)
    taken, position = [], 0
    for shapes, _ in groups:
        taken.append((links[position : position + len(shapes)], links[position + len(shapes) : position + len(shapes) + 2]))
        position += len(shapes) + 2
    ticks = {0: [lambda: greet(axes)]}

    stores = []

    def enlist(reduction, times, done, place):
        for time, event in zip(times, reduction.events(), strict=True):
            ticks.setdefault(time, []).append(event)
        store = pltpu.make_async_copy(done, place, out_sem.at[len(stores)])
        ticks[times[-1]].append(store.start)
        stores.append(store)

    number = 0
    for source, final, place in ((pd_ref, down_ref, down_out), (pu_ref, up_ref, up_out)):
        for start in range(0, final.shape[0], FFN_ROWS):
            landings, sems = taken[number]
            block = span(start, FFN_ROWS)
            if source is pd_ref:
                reduction = Reduction(axes, FFN_ORDER[1:], FFN_BACK, source, start, FFN_ROWS, final, start, landings, sems)
            else:
                reduction = FfnReduction(axes, FFN_ORDER, FFN_BACK, source, start, FFN_ROWS, final, start, landings, sems)
            times = FFN_TIMES[source is pu_ref][start // FFN_ROWS]
            enlist(reduction, times, final.at[block], place.at[block])
            number += 1
    size = padded(2 * width, devices)
    for index in range(quads + 1):
        landings, sems = taken[number]
        order, back = all_order(index)
        source = gwo_ref if index == 0 else gwlow_ref.at[index - 1]
        reduction = Reduction(axes, order, back, source, 0, size, all_ref.at[index], 0, landings, sems)
        enlist(reduction, ALL_TIMES[index], all_ref.at[index], all_out.at[index])
        number += 1
    landings, sems = taken[number]
    order, back = all_order(quads)
    reduction = Reduction(axes, order, back, mini_ref, 0, 8 * devices, few_ref, 0, landings, sems)
    enlist(reduction, MINI_TIMES, few_ref, few_out)
    ticks[max(ticks) + 1] = [store.wait for store in stores]
    return ticks


def attend_back(dctx, att, inv, q, k, v, sq, sk, weight, slope, tokens, seg_col, seg_pad, w_qkv, flipped, dproj, gwo, pu, pd, small, dp_size, tensor_size, length):
    count, width = tokens.shape
    seqs = count // length
    quads = width // QUAD
    per = QUAD // HEAD
    blocks = length // BLK
    own = pl.BlockSpec((length, QUAD), lambda p, r: (r, p))
    big = pl.BlockSpec((1, per, length, length), lambda p, r: (r, p, 0, 0))
    wide = pl.BlockSpec((length, width), lambda p, r: (r, 0))

    sizes = {"core": CORES, "y": tensor_size // CORES, "x": dp_size // DEPTH, "z": DEPTH}
    devices = dp_size * tensor_size
    share = pd.shape[0]
    grown = padded(2 * width, devices)
    gwo = jnp.pad(gwo, ((0, grown - gwo.shape[0]), (0, 0)))
    minis = 8 * devices
    scratch = []
    for shapes, count_of in link_plan(sizes, width, share, quads):
        scratch += shapes + [pltpu.SemaphoreType.DMA((count_of,)), pltpu.SemaphoreType.DMA((count_of,))]

    def whole(*shape):
        return pl.BlockSpec(shape, lambda p, r: (0,) * len(shape), pipeline_mode=pl.Buffered(1))

    taps_spec = pl.BlockSpec((1, per, 2 * BLK), lambda p, r: (p, 0, 0))
    return pl.pallas_call(
        functools.partial(attend_back_kernel, plan=(None, sizes, dp_size, tensor_size), quads=quads, seqs=seqs),
        grid=(quads, seqs),
        in_specs=[own] * 8
        + [big] * 2
        + [
            wide,
            pl.BlockSpec((length, 1), lambda p, r: (r, 0)),
            pl.BlockSpec((1, 1, length + 2 * HALO), lambda p, r: (r, 0, 0)),
            whole(width, 3 * width),
            taps_spec,
            wide,
            whole(*gwo.shape), whole(*pu.shape), whole(*pd.shape), whole(*small.shape),
        ],
        out_specs=[
            pl.BlockSpec((length, width), lambda p, r: (jnp.where(p == quads - 1, r, 0), 0)),
        ]
        + [pl.BlockSpec(memory_space=pl.ANY)] * 4,
        out_shape=[
            jax.ShapeDtypeStruct((count, width), BF16),
            jax.ShapeDtypeStruct((quads + 1, grown, width // 2), BF16),
            jax.ShapeDtypeStruct((width, share), BF16),
            jax.ShapeDtypeStruct((share, width), BF16),
            jax.ShapeDtypeStruct((minis, PAIR), F32),
        ],
        scratch_shapes=[
            pltpu.VMEM((blocks, BLK, 2 * BLK), BF16),
            pltpu.VMEM((2, length + 2 * HALO, 2 * PAIR), BF16),
            pltpu.VMEM((2, length + 2 * HALO, PAIR), BF16),
            pltpu.VMEM((length, length), BF16),
            pltpu.VMEM((length, PAIR), F32),
            pltpu.VMEM((length, PAIR), F32),
            pltpu.VMEM((length, PAIR), F32),
            pltpu.VMEM((quads, seqs, length, 3 * QUAD), BF16),
            pltpu.VMEM((width, 3 * QUAD), F32),
            pltpu.VMEM((per, BLK, 2 * BLK), F32),
            pltpu.VMEM((quads, grown, width // 2), BF16),
            pltpu.VMEM((quads, 8, 3 * QUAD), F32),
            pltpu.VMEM((minis, PAIR), F32),
            pltpu.VMEM((quads + 1, grown, width // 2), BF16),
            pltpu.VMEM((width, share), BF16),
            pltpu.VMEM((share, width), BF16),
            pltpu.VMEM((minis, PAIR), F32),
            pltpu.SemaphoreType.DMA((quads + 2 + (width + share) // FFN_ROWS,)),
        ]
        + scratch,
        compiler_params=pltpu.CompilerParams(vmem_limit_bytes=60 * 2**20, collective_id=1, has_side_effects=True),
        name="attend_backward",
    )(dctx, att, inv, q, k, v, sq, sk, weight, slope, tokens, seg_col, seg_pad, w_qkv, flipped, dproj, gwo, pu, pd, small)


def spread_kernel(low_ref, high_ref, up_ref, down_ref, few_ref, gw_ref, gwo_ref, gup_ref, gdown_ref, *vectors, first_lane, base):
    width = gwo_ref.shape[1]
    half = width // 2
    quads = low_ref.shape[0] - 1
    gwo_ref[:, :half] = low_ref[0].astype(F32)
    gwo_ref[:, half:] = high_ref[0].astype(F32)
    for quad in range(quads):
        for part in range(3):
            for start in range(part * QUAD, (part + 1) * QUAD, PAIR):
                side, lane = (low_ref, start) if start < half else (high_ref, start - half)
                to = part * width + quad * QUAD + start - part * QUAD
                gw_ref[:, to : to + PAIR] = side[1 + quad, :, lane : lane + PAIR].astype(F32)
    gup_ref[...] = up_ref[...].astype(F32)
    gdown_ref[...] = down_ref[...].astype(F32)

    @pl.when(pl.program_id(0) == 0)
    def _():
        gb_ref, conv_ref, *six, gbu_ref = vectors
        lines = width // PAIR

        def copy_line(target, to, line):
            target[:, to * PAIR : (to + 1) * PAIR] = few_ref[pl.ds(line, 1)]

        for number, target in enumerate(six):
            for i in range(lines):
                copy_line(target, i, number * lines + i)
        share = gbu_ref.shape[1] // PAIR
        mine = lax.axis_index("tensor") * share
        for i in range(share):
            copy_line(gbu_ref, i, 6 * lines + mine + i)
        per = QUAD // PAIR
        for quad in range(quads):
            for part in range(3):
                for i in range(per):
                    copy_line(gb_ref, (part * width + quad * QUAD) // PAIR + i, base + (quad * 3 + part) * per + i)
        heads, taps = conv_ref.shape
        kept = few_ref[base + 3 * lines : base + 3 * lines + heads]
        conv_ref[...] = pltpu.roll(kept, PAIR - first_lane, 1)[:, :taps]


def spread_out(grads, up, down, few, width, heads, taps, first_lane, base):
    chunks = grads.shape[0]
    quads = chunks - 1
    steps = 6
    rows_of = width // steps
    share = up.shape[1]
    down_rows = share // steps

    def whole(*shape):
        return pl.BlockSpec(shape, lambda s: (0,) * len(shape))

    def by_rows(count, columns):
        return pl.BlockSpec((count, columns), lambda s: (s, 0))

    row = jax.ShapeDtypeStruct((1, width), F32)
    return pl.pallas_call(
        functools.partial(spread_kernel, first_lane=first_lane, base=base),
        grid=(steps,),
        in_specs=[
            pl.BlockSpec((chunks, rows_of, width // 2), lambda s: (0, s, 0)),
            pl.BlockSpec((chunks, rows_of, width // 2), lambda s: (0, steps + s, 0)),
            by_rows(rows_of, share),
            by_rows(down_rows, width),
            whole(*few.shape),
        ],
        out_specs=[
            by_rows(rows_of, 3 * width), by_rows(rows_of, width), by_rows(rows_of, share), by_rows(down_rows, width),
            whole(1, 3 * width), whole(heads, taps),
        ]
        + [whole(1, width)] * 6
        + [whole(1, share)],
        out_shape=[
            jax.ShapeDtypeStruct((width, 3 * width), F32),
            jax.ShapeDtypeStruct((width, width), F32),
            jax.ShapeDtypeStruct((width, share), F32),
            jax.ShapeDtypeStruct((share, width), F32),
            jax.ShapeDtypeStruct((1, 3 * width), F32),
            jax.ShapeDtypeStruct((heads, taps), F32),
        ]
        + [row] * 6
        + [jax.ShapeDtypeStruct((1, share), F32)],
        compiler_params=pltpu.CompilerParams(vmem_limit_bytes=40 * 2**20),
        name="spread_out",
    )(grads, grads, up, down, few)


def body(
    tokens, segment_ids, w_qkv, b_qkv, conv_kernel, w_out, b_out, norm1_gain, norm1_bias,
    w_up, b_up, w_down, b_down, norm2_gain, norm2_bias, cotangent,
):
    seqs, length = segment_ids.shape
    width = tokens.shape[1]
    heads, span_of = conv_kernel.shape
    per = QUAD // HEAD
    radius = span_of // 2
    first_tap = HALO - radius

    def spread(kernel):
        padded = jnp.pad(kernel, ((0, 0), (first_tap, 2 * BLK - first_tap - span_of)))
        return padded.reshape(heads // per, per, 2 * BLK)

    seg_col = segment_ids.reshape(-1, 1)
    seg_pad = jnp.pad(segment_ids, ((0, 0), (HALO, HALO)), constant_values=-1)[:, None, :]
    taps, flipped = spread(conv_kernel), spread(conv_kernel[:, ::-1])

    dp_size, tensor_size = lax.axis_size("dp"), lax.axis_size("tensor")
    vectors = jnp.concatenate([b_qkv, b_out, norm1_gain, norm1_bias, norm2_gain, norm2_bias, b_down])[None]

    q, k, v, sq, sk, weight, slope, att, inv, ctx, res, up_all, down_all, bias_all = attend(
        tokens, seg_col, seg_pad, w_qkv, vectors, taps, w_out, w_up, w_down, b_up.astype(F32)[None],
        dp_size, tensor_size, length,
    )
    out, dproj, dctx, gwo, pu, pd, small = feed_forward(res, cotangent, ctx, w_out, vectors, bias_all, up_all, down_all)
    gt, grads, grad_up, grad_down, few = attend_back(
        dctx, att, inv, q, k, v, sq, sk, weight, slope, tokens, seg_col, seg_pad, w_qkv, flipped, dproj,
        gwo, pu, pd, small, dp_size, tensor_size, length,
    )
    first_lane = (first_tap + BLK - 1 + BLK) % (2 * BLK)
    gw, gwo, grad_up, grad_down, gb, grad_conv, gg2, gs2, gbd, gg1, gs1, gbo, gbu = spread_out(
        grads, grad_up, grad_down, few, width, heads, span_of, first_lane, small.shape[0]
    )
    return (
        out, gt, gw, gb[0], grad_conv, gwo, gbo[0], gg1[0], gs1[0],
        grad_up, gbu[0], grad_down, gbd[0], gg2[0], gs2[0],
    )


def solution(mesh):
    placed = (
        P(("dp", "tensor"), None),
        P(("dp", "tensor"), None),
        P(), P(), P(), P(), P(), P(), P(),
        P(None, "tensor"),
        P("tensor"),
        P("tensor", None),
        P(), P(), P(),
        P(("dp", "tensor"), None),
    )
    return jax.shard_map(
        body,
        mesh=mesh,
        in_specs=placed,
        out_specs=(
            P(("dp", "tensor"), None),
            P(("dp", "tensor"), None),
            P(), P(), P(), P(), P(), P(), P(),
            P(None, "tensor"),
            P("tensor"),
            P("tensor", None),
            P(), P(), P(),
        ),
        check_vma=False,
    )
```

```python
import functools
import math

import jax
import jax.numpy as jnp
from jax import lax
from jax.experimental import pallas as pl
from jax.experimental.pallas import tpu as pltpu
from jax.sharding import PartitionSpec as P

F32 = jnp.float32
BF16 = jnp.bfloat16
EPS_NORM = 1e-5
EPS_UNIT = 1e-6
SHRINK = 0.95
TAU = 8
SLOPE = TAU / math.pi
ARC = (0.49999996, -0.06830509, 0.02825875, -0.01557005, 0.00864352, -0.00363107, 0.00076235)
QUAD = 256
PAIR = 128
HEAD = 64
BLK = 128
HALO = 64


def dot_nn(a, b):
    return lax.dot_general(a, b, (((1,), (0,)), ((), ())), preferred_element_type=F32)


def dot_nt(a, b):
    return lax.dot_general(a, b, (((1,), (1,)), ((), ())), preferred_element_type=F32)


def dot_tn(a, b):
    return lax.dot_general(a, b, (((0,), (0,)), ((), ())), preferred_element_type=F32)


def lanes(shape):
    return lax.broadcasted_iota(jnp.int32, shape, len(shape) - 1)


def rows(shape):
    return lax.broadcasted_iota(jnp.int32, shape, len(shape) - 2)


def head_sum(values):
    width = values.shape[-1]
    ones = (rows((width, width)) // HEAD == lanes((width, width)) // HEAD).astype(BF16)
    high = values.astype(BF16)
    low = (values - high.astype(F32)).astype(BF16)
    return dot_nn(high, ones) + dot_nn(low, ones)


def closeness_terms(cosine):
    size = jnp.abs(cosine)
    room = 1.0 - size
    inverse = lax.rsqrt(room)
    poly = jnp.full_like(size, ARC[-1])
    for coefficient in ARC[-2::-1]:
        poly = poly * size + coefficient
    small = room * inverse * poly
    close = jnp.where(cosine >= 0.0, 1.0 - small, small)
    two = close * close
    four = two * two
    slope = (four * two) * (close * inverse) * lax.rsqrt(1.0 + size)
    return four * four, slope


def head_mask(half, shape):
    return (lanes(shape) // HEAD == half).astype(BF16)


def window_of(block, blocks):
    low = max(0, block * BLK - 256)
    high = min(blocks * BLK, block * BLK + BLK + 256)
    return low, high


def band(taps, count):
    spread = jnp.broadcast_to(taps, (count, taps.shape[1]))
    return pltpu.roll(spread, 0, 1, stride=1, stride_axis=0)


def norm_stats(values):
    centred = values - jnp.mean(values, -1, keepdims=True)
    scaling = lax.rsqrt(jnp.mean(centred * centred, -1, keepdims=True) + EPS_NORM)
    return centred * scaling, scaling


def segment_rows(seg_ref, row):
    ids = seg_ref[pl.ds(row, 1)].astype(F32)
    edge = jnp.full((1, HALO), -1.0, F32)
    return jnp.concatenate([edge, ids, edge], 1), jnp.broadcast_to(ids, (PAIR, ids.shape[1])).T[:, :1]


def build_same(seg_pad, seg_col, same_ref):
    length = seg_col.shape[0]
    for start in range(0, length, BLK):
        own = seg_col[start : start + BLK]
        same_ref[start : start + BLK, :] = jnp.where(
            own == seg_pad[:, HALO : HALO + length], 1.0, 0.0
        ).astype(BF16)


def build_near(seg_pad, seg_col, near_ref):
    length = seg_col.shape[0]
    for start in range(0, length, BLK):
        own = seg_col[start : start + BLK]
        near_ref[start // BLK] = jnp.where(
            own == seg_pad[:, start : start + 2 * BLK], 1.0, 0.0
        ).astype(BF16)


def place_taps(kernel, reverse):
    taps = kernel.shape[1]
    shape = (taps, 2 * BLK)
    tap = taps - 1 - rows(shape) if reverse else rows(shape)
    return dot_nn(kernel.astype(BF16), (lanes(shape) == tap + HALO - taps // 2).astype(BF16))


def attend_kernel(
    x_ref, seg_ref, wq_ref, wk_ref, wv_ref, b_ref, kernel_ref, wo_ref, bo_ref,
    wu_ref, wd_ref, bu_ref,
    q_ref, k_ref, v_ref, sq_ref, sk_ref, w_ref, s_ref, att_ref, inv_ref, ctx_ref, res_ref,
    up_ref, down_ref, bias_ref,
    same_ref, near_ref, vv_ref, tap_ref, mine_ref, send_sem, recv_sem, copy_sem,
    *, dp_size, tensor_size,
):
    row, quad = pl.program_id(0), pl.program_id(1)
    quads, seqs = pl.num_programs(1), pl.num_programs(0)
    ticks = gather_plan(dp_size, tensor_size, (wu_ref, wd_ref, mine_ref), (up_ref, down_ref, bias_ref), (send_sem, recv_sem), copy_sem)
    length = x_ref.shape[0]
    blocks = length // BLK

    @pl.when((row == 0) & (quad == 0))
    def _():
        tap_ref[...] = place_taps(kernel_ref[...], False)
        mine_ref[...] = bu_ref[...].astype(F32)[None, :]

    @pl.when(quad == 0)
    def _():
        seg_pad, seg_col = segment_rows(seg_ref, row)
        build_same(seg_pad, seg_col, same_ref)
        build_near(seg_pad, seg_col, near_ref)
        for half in range(2):
            edge = jnp.zeros((HALO, 2 * PAIR), BF16)
            vv_ref[half, :HALO] = edge
            vv_ref[half, HALO + length :] = edge
            vv_ref[half, HALO : HALO + length, PAIR:] = head_mask(half, (length, PAIR))

    def bias(part):
        start = pl.multiple_of(part * x_ref.shape[1] + quad * QUAD, QUAD)
        return b_ref[pl.ds(start, QUAD)][None, :]

    for start in range(0, length, BLK):
        here = slice(start, start + BLK)
        x = x_ref[here]
        for number, (w, unit, scale, factor) in enumerate(
            ((wq_ref, q_ref, sq_ref, SHRINK), (wk_ref, k_ref, sk_ref, 1.0))
        ):
            part = dot_nn(x, w[...]) + bias(number)
            scaling = lax.rsqrt(head_sum(part * part) + EPS_UNIT)
            unit[here] = (part * (scaling * factor)).astype(BF16)
            scale[here] = scaling.astype(BF16)
        v_ref[here] = (dot_nn(x, wv_ref[...]) + bias(2)).astype(BF16)

    def one_pair(pair, carry):
        turn = (row * quads + quad) * (QUAD // PAIR) + pair
        for when, events in ticks.items():

            @pl.when(turn == when)
            def _(events=events):
                for event in events:
                    event()

        at = pl.ds(pl.multiple_of(pair * PAIR, PAIR), PAIR)
        v = v_ref[:, at]
        for half in range(2):
            vv_ref[half, HALO : HALO + length, :PAIR] = v * head_mask(half, (length, PAIR))
        for block in range(blocks):
            here = slice(block * BLK, block * BLK + BLK)
            low, high = window_of(block, blocks)
            q = q_ref[here, at]
            total = jnp.zeros((BLK, 2 * PAIR), F32)
            near = jnp.zeros((BLK, PAIR), F32)
            for half in range(2):
                head = pair * 2 + half
                q_half = q * head_mask(half, (BLK, PAIR))
                for start in range(low, high, KCH):
                    stop = min(start + KCH, high)
                    cosine = dot_nt(q_half, k_ref[start:stop, at])
                    weight, slope = closeness_terms(cosine)
                    same = same_ref[here, start:stop]
                    weight = weight.astype(BF16) * same
                    w_ref[0, head, here, start:stop] = weight
                    s_ref[0, head, here, start:stop] = slope.astype(BF16) * same
                    total += dot_nn(weight, vv_ref[half, HALO + start : HALO + stop])
                if low > 0:
                    w_ref[0, head, here, :low] = jnp.zeros((BLK, low), BF16)
                if high < length:
                    w_ref[0, head, here, high:] = jnp.zeros((BLK, length - high), BF16)
                taps = band(tap_ref[pl.ds(quad * (QUAD // HEAD) + head, 1)], BLK).astype(BF16) * near_ref[block]
                near += dot_nn(taps, vv_ref[half, block * BLK : block * BLK + 2 * BLK, :PAIR])
            inverse = 1.0 / (1.0 + total[:, PAIR:])
            attended = total[:, :PAIR] * inverse
            att_ref[here, at] = attended.astype(BF16)
            inv_ref[here, at] = inverse.astype(BF16)
            ctx_ref[here, at] = (attended + near).astype(BF16)
        return carry

    lax.fori_loop(0, QUAD // PAIR, one_pair, 0)

    @pl.when(quad == 0)
    def _():
        res_ref[...] = x_ref[...].astype(F32) + bo_ref[...][None, :]

    for start in range(0, length, BLK):
        here = slice(start, start + BLK)
        res_ref[here] += dot_nn(ctx_ref[here], wo_ref[...])


def gather_plan(dp_size, tensor_size, own, whole, sems, copy_sem):
    axes = slice_axes(dp_size, tensor_size)
    y, x, core = axes["y"], axes["x"], axes["core"]
    mate = core.device(core.ahead(1))
    number = iter(range(1000))

    def mine(place):
        return place * CORES + core.place

    def half_of(ref, piece):
        size = ref.shape[-2] // 2
        return span(piece % 2 * size, size)

    def rows_at(ref, piece, place):
        size = ref.shape[-2] // (2 * x.size)
        return span(piece % 2 * x.size * size + place * size, size)

    def at_y(piece):
        source, target = own[piece // 2], whole[piece // 2]
        out = []
        for j in range(1, y.size):
            if piece < 4:
                block = rows_at(source, piece, x.place)
                pair = (source.at[block], target.at[mine(y.place), block])
            else:
                pair = (source, target.at[mine(y.place)])
            out.append(send(*pair, sems, next(number), y.device(y.ahead(j))))
        return out

    def at_x(piece):
        target = whole[piece // 2]
        out = []
        for j in range(1, y.size):
            block = target.at[mine(y.ahead(j)), rows_at(target, piece, x.place)]
            out += [send(block, block, sems, next(number), x.device(x.ahead(i))) for i in range(1, x.size)]
        return out

    def to_mate(piece):
        target = whole[piece // 2]
        out = []
        for j in range(1, y.size):
            block = target.at[mine(y.ahead(j))]
            block = block.at[half_of(target, piece)] if piece < 4 else block
            out.append(send(block, block, sems, next(number), mate))
        return out

    keep = [pltpu.make_async_copy(own[i], whole[i].at[mine(y.place)], copy_sem.at[i]) for i in range(3)]
    give = [send(own[i], whole[i].at[mine(y.place)], sems, next(number), mate) for i in range(3)]
    ys, xs, mates = [at_y(i) for i in range(5)], [at_x(i) for i in range(4)], [to_mate(i) for i in range(5)]

    def start(copies):
        return [copy.start for copy in copies]

    def wait(copies):
        return [copy.wait for copy in copies]

    steps = [
        [lambda: greet(axes, ("core", "y", "x"))] + start(ys[0] + ys[1] + ys[4] + give + keep),
        wait(ys[0] + ys[4]) + start(xs[0] + ys[2] + mates[4]),
        wait(ys[1]) + start(xs[1] + ys[3]),
        wait(ys[2] + xs[0]) + start(xs[2] + mates[0]),
        wait(ys[3] + xs[1]) + start(xs[3] + mates[1]),
        wait(xs[2] + xs[3]) + start(mates[2] + mates[3]),
    ]
    last = wait([copy for piece in mates for copy in piece] + give + keep)
    return dict(zip(GATHER_TIMES, steps)) | {GATHER_TIMES[len(steps)]: last}


GATHER_TIMES = (0, 4, 5, 7, 8, 10, 11)


KCH = 256


def attend(tokens, segment_ids, w_qkv, b_qkv, kernel, w_out, b_out, w_up, w_down, b_up, dp_size, tensor_size):
    count, width = tokens.shape
    seqs, length = segment_ids.shape
    quads = width // QUAD
    heads = width // HEAD
    per = QUAD // HEAD
    blocks = length // BLK
    own = pl.BlockSpec((length, QUAD), lambda r, p: (r, p))
    act = jax.ShapeDtypeStruct((count, width), BF16)
    big = jax.ShapeDtypeStruct((seqs, heads, length, length), BF16)
    big_spec = pl.BlockSpec((1, per, length, length), lambda r, p: (r, p, 0, 0))

    def part(rows_of, k):
        return pl.BlockSpec((rows_of, QUAD), lambda r, p, k=k: (0, p + k * quads))

    def whole(*shape):
        return pl.BlockSpec(shape, lambda r, p: (0,) * len(shape), pipeline_mode=pl.Buffered(1))

    others = tensor_size // CORES - 1
    copies = 3 + 10 * others + 4 * others * (dp_size // DEPTH - 1)
    return pl.pallas_call(
        functools.partial(attend_kernel, dp_size=dp_size, tensor_size=tensor_size),
        grid=(seqs, quads),
        in_specs=[
            pl.BlockSpec((length, width), lambda r, p: (r, 0)),
            whole(*segment_ids.shape),
            part(width, 0), part(width, 1), part(width, 2),
            whole(*b_qkv.shape),
            whole(*kernel.shape),
            pl.BlockSpec((QUAD, width), lambda r, p: (p, 0)),
            whole(*b_out.shape),
        ]
        + [
            whole(*each.shape) for each in (w_up, w_down, b_up)
        ],
        out_specs=[own] * 5 + [big_spec] * 2 + [own] * 3 + [pl.BlockSpec((length, width), lambda r, p: (r, 0))]
        + [pl.BlockSpec(memory_space=pl.ANY)] * 3,
        out_shape=[act] * 5 + [big] * 2 + [act] * 3 + [jax.ShapeDtypeStruct((count, width), F32)]
        + [jax.ShapeDtypeStruct((tensor_size,) + part.shape, BF16) for part in (w_up, w_down)]
        + [jax.ShapeDtypeStruct((tensor_size, 1, b_up.shape[0]), F32)],
        scratch_shapes=[
            pltpu.VMEM((length, length), BF16),
            pltpu.VMEM((blocks, BLK, 2 * BLK), BF16),
            pltpu.VMEM((2, length + 2 * HALO, 2 * PAIR), BF16),
            pltpu.VMEM((heads, 2 * BLK), F32),
            pltpu.VMEM((1, b_up.shape[0]), F32),
            pltpu.SemaphoreType.DMA((copies,)),
            pltpu.SemaphoreType.DMA((copies,)),
            pltpu.SemaphoreType.DMA((3,)),
        ],
        compiler_params=pltpu.CompilerParams(vmem_limit_bytes=56 * 2**20, collective_id=2, has_side_effects=True),
        name="attend_forward",
    )(tokens, segment_ids, w_qkv, w_qkv, w_qkv, b_qkv, kernel, w_out, b_out, w_up, w_down, b_up)


DEPTH = 4
CORES = 2


class Axis:
    def __init__(self, size, place, device):
        self.size, self.place, self.device = size, place, device

    def ahead(self, j):
        return lax.rem(self.place + j, self.size)


def slice_axes(dp_size, tensor_size):
    dp, tensor = lax.axis_index("dp"), lax.axis_index("tensor")
    across = dp_size // DEPTH
    z, x = dp // across, lax.rem(dp, across)
    y, core = tensor // CORES, lax.rem(tensor, CORES)
    return {
        "core": Axis(CORES, core, lambda p: (dp, y * CORES + p)),
        "y": Axis(tensor_size // CORES, y, lambda p: (dp, p * CORES + core)),
        "x": Axis(across, x, lambda p: (z * across + p, tensor)),
        "z": Axis(DEPTH, z, lambda p: (p * across + x, tensor)),
    }


def greet(axes, names=("core", "y", "x", "z")):
    barrier = pltpu.get_barrier_semaphore()
    count = 0
    for axis in (axes[name] for name in names):
        for j in range(1, axis.size):
            pl.semaphore_signal(
                barrier, inc=1, device_id=axis.device(axis.ahead(j)), device_id_type=pl.DeviceIdType.MESH
            )
            count += 1
    pl.semaphore_wait(barrier, count)


def send(source, target, sems, at, device):
    return pltpu.make_async_remote_copy(
        src_ref=source, dst_ref=target, send_sem=sems[0].at[at], recv_sem=sems[1].at[at],
        device_id=device, device_id_type=pl.DeviceIdType.MESH,
    )


def span(start, size):
    if isinstance(start, int):
        return pl.ds(start, size)
    return pl.ds(pl.multiple_of(start, math.gcd(size, 16)), size)


def add_rows(target, target_at, terms, size):
    tile = next(t for t in (64, 48, 32, 24, 16, 12, 8) if size % t == 0)

    def one(i, carry):
        total = None
        for ref, start in terms:
            rows_of = ref[span(start + i * tile, tile)].astype(F32)
            total = rows_of if total is None else total + rows_of
        target[span(target_at + i * tile, tile)] = total.astype(target.dtype)
        return carry

    lax.fori_loop(0, size // tile, one, 0)


class Reduction:
    def __init__(self, axes, order, back, source, source_at, size, final, final_at, landings, sems, first_sem=0):
        self.axes, self.order, self.back = axes, order, back
        self.source, self.source_at, self.size = source, source_at, size
        self.final, self.final_at = final, final_at
        self.landings, self.sems = landings, sems
        self.first_sem = first_sem

    def plan(self):
        size, at, out = self.size, self.final_at, []
        for name in self.order:
            axis = self.axes[name]
            size //= axis.size
            at = at + axis.place * size
            out.append((axis, size, at))
        return out

    def copies(self, stage):
        stages = self.plan()
        sem = self.first_sem
        for axis, _, _ in stages[:stage]:
            sem += axis.size - 1
        axis, size, _ = stages[stage]
        held, held_at = (self.source, self.source_at) if stage == 0 else (self.landings[stage - 1].at[0], 0)
        return [
            send(
                held.at[span(held_at + axis.ahead(j) * size, size)], self.landings[stage].at[j - 1],
                self.sems, sem + j - 1, axis.device(axis.ahead(j)),
            )
            for j in range(1, axis.size)
        ]

    def settle(self, stage):
        for copy in self.copies(stage):
            copy.wait()
        axis, size, final_at = self.plan()[stage]
        held, held_at = (self.source, self.source_at) if stage == 0 else (self.landings[stage - 1].at[0], 0)
        terms = [(held, held_at + axis.place * size)]
        terms += [(self.landings[stage].at[j - 1], 0) for j in range(1, axis.size)]
        if stage == len(self.order) - 1:
            add_rows(self.final, final_at, terms, size)
        else:
            add_rows(self.landings[stage].at[0], 0, terms, size)

    def gathers(self, which):
        stages = self.plan()
        sem = self.first_sem + sum(axis.size - 1 for axis, _, _ in stages)
        for name in self.back[:which]:
            sem += self.axes[name].size - 1
        depth = self.order.index(self.back[which])
        axis, size, at = stages[depth]
        block = self.final.at[span(at, size)]
        return [send(block, block, self.sems, sem + j - 1, axis.device(axis.ahead(j))) for j in range(1, axis.size)]

    def events(self):
        out = []
        count = len(self.order)

        def begin(copies):
            for copy in copies:
                copy.start()

        for stage in range(count):
            def event(stage=stage):
                if stage > 0:
                    self.settle(stage - 1)
                begin(self.copies(stage))

            out.append(event)
        for which in range(len(self.back)):
            def event(which=which):
                if which == 0:
                    self.settle(count - 1)
                else:
                    for copy in self.gathers(which - 1):
                        copy.wait()
                begin(self.gathers(which))

            out.append(event)

        def last():
            for copy in self.gathers(len(self.back) - 1):
                copy.wait()

        out.append(last)
        return out


def landing_shapes(order, sizes, size, columns, dtype):
    shapes = []
    for name in order:
        size //= sizes[name]
        shapes.append(pltpu.VMEM((sizes[name] - 1, size, columns), dtype))
    return shapes


def copies_of(order, back, sizes):
    return sum(sizes[name] - 1 for name in order) + sum(sizes[name] - 1 for name in back)

GELU_A = math.sqrt(2.0 / math.pi)
GELU_B = 0.044715
TILE = 256
UNROLL = 4


def gelu_terms(pre):
    square = pre * pre
    swing = jnp.tanh(pre * (GELU_A + GELU_A * GELU_B * square))
    gate = 0.5 + 0.5 * swing
    steep = GELU_A + 3.0 * GELU_A * GELU_B * square
    return pre * gate, gate + 0.5 * pre * (1.0 - swing * swing) * steep


def norm_backward(grad_out, unit, scaling, gain):
    grad_unit = grad_out * gain
    return scaling * (
        grad_unit
        - jnp.mean(grad_unit, -1, keepdims=True)
        - unit * jnp.mean(grad_unit * unit, -1, keepdims=True)
    )


def column_sum(values):
    return jnp.sum(values, 0, keepdims=True)


def ffn_kernel(
    res_ref, cot_ref, ctx_ref, wo_ref, gain1_ref, shift1_ref, gain2_ref, shift2_ref, bd_ref, bu_ref, wu_ref, wd_ref,
    out_ref, dproj_ref, dctx_ref, gwo_ref, pu_ref, pd_ref, small_ref,
    low_ref, acc_ref, hid_ref, slope_ref, dffn_ref, dpre_ref, sendu_ref, sendd_ref, recvu_ref, recvd_ref, pdown_ref, yland_ref,
    send_sem, recv_sem,
):
    parts = pl.num_programs(0) // 2
    step = pl.program_id(0)
    count, width = res_ref.shape
    share = dpre_ref.shape[1]
    tiles = count // TILE
    f = part_order(step, parts)
    late = jnp.maximum(step - parts, 0)
    heights = parts // CORES
    slot = late // CORES
    dp, tensor = lax.axis_index("dp"), lax.axis_index("tensor")
    height, core = tensor // CORES, lax.rem(tensor, CORES)
    mate = (dp, height * CORES + 1 - core)

    def up_to_mate(which):
        return send(sendu_ref.at[which], recvu_ref.at[which], (send_sem.at[0], recv_sem.at[0]), which, mate)

    def down_to_mate(which):
        return send(sendd_ref.at[which], recvd_ref.at[which], (send_sem.at[1], recv_sem.at[1]), which, mate)

    def to_height(which):
        there = (dp, lax.rem(height + 1 + which, heights) * CORES + core)
        return send(pdown_ref.at[which], yland_ref.at[which], (send_sem.at[2], recv_sem.at[2]), which, there)

    def down_part(late):
        part = part_order(parts + late, parts)
        piece = math.gcd(TILE, share)
        for start in range(0, share, piece):
            cut = slice(start, start + piece)
            yield cut, dot_tn(hid_ref[part, :, cut], dffn_ref[...]).astype(BF16)

    @pl.when(step == 0)
    def _():
        barrier = pltpu.get_barrier_semaphore()
        peers = [mate] + [(dp, lax.rem(height + j, heights) * CORES + core) for j in range(1, heights)]
        for peer in peers:
            pl.semaphore_signal(barrier, inc=1, device_id=peer, device_id_type=pl.DeviceIdType.MESH)
        pl.semaphore_wait(barrier, len(peers))

    def put_row(row, values):
        for i in range(values.shape[1] // PAIR):
            small_ref[pl.ds(row + i, 1)] = values[:, i * PAIR : (i + 1) * PAIR]

    def at(t):
        return pl.ds(pl.multiple_of(t * TILE, TILE), TILE)

    @pl.when(step == 0)
    def _():
        def one(t, carry):
            unit, _ = norm_stats(res_ref[at(t)])
            low_ref[at(t)] = (unit * gain1_ref[...][None, :] + shift1_ref[...][None, :]).astype(BF16)
            acc_ref[at(t)] = jnp.zeros((TILE, width), F32)
            return carry

        lax.fori_loop(0, tiles, one, 0, unroll=UNROLL)

    @pl.when(step < parts)
    def _():
        def one(t, carry):
            pre = dot_nn(low_ref[at(t)], wu_ref[0]) + bu_ref[0].astype(F32)
            hidden, slope = gelu_terms(pre)
            hidden = hidden.astype(BF16)
            hid_ref[f, at(t)] = hidden
            slope_ref[f, at(t)] = slope.astype(BF16)
            acc_ref[at(t)] += dot_nn(hidden, wd_ref[0])
            return carry

        lax.fori_loop(0, tiles, one, 0, unroll=UNROLL)

    @pl.when(step == parts)
    def _():
        def one(t, sums):
            unit, _ = norm_stats(res_ref[at(t)])
            first = unit * gain1_ref[...][None, :] + shift1_ref[...][None, :]
            unit, scaling = norm_stats(first + acc_ref[at(t)] + bd_ref[...][None, :])
            out_ref[at(t)] = (unit * gain2_ref[...][None, :] + shift2_ref[...][None, :]).astype(BF16)
            grad = cot_ref[at(t)].astype(F32)
            d_res = norm_backward(grad, unit, scaling, gain2_ref[...][None, :])
            d_ffn = d_res.astype(BF16)
            acc_ref[at(t)] = d_res
            dffn_ref[at(t)] = d_ffn
            return (
                sums[0] + column_sum(grad * unit),
                sums[1] + column_sum(grad),
                sums[2] + column_sum(d_ffn.astype(F32)),
            )

        zero = jnp.zeros((1, width), F32)
        sums = lax.fori_loop(0, tiles, one, (zero, zero, zero), unroll=UNROLL)
        small_ref[...] = jnp.zeros_like(small_ref)
        for i, values in enumerate(sums):
            put_row(i * (width // PAIR), values)

        def theirs(which, carry):
            for cut, values in down_part(CORES * which):
                sendd_ref[which, cut] = values
            down_to_mate(which).start()
            return carry

        def ours(which, carry):
            for cut, values in down_part(CORES * which + 1):
                pdown_ref[which, cut] = values
            return carry

        lax.fori_loop(0, heights, theirs, 0)
        lax.fori_loop(0, heights, ours, 0)

    @pl.when(step >= parts)
    def _():
        def one(t, total):
            d_hidden = dot_nt(dffn_ref[at(t)], wd_ref[0])
            d_pre = (d_hidden * slope_ref[f, at(t)].astype(F32)).astype(BF16)
            dpre_ref[at(t)] = d_pre
            acc_ref[at(t)] += dot_nt(d_pre, wu_ref[0])
            return total + column_sum(d_pre.astype(F32))

        bias = lax.fori_loop(0, tiles, one, jnp.zeros((1, share), F32), unroll=UNROLL)
        put_row(6 * (width // PAIR) + f * (share // PAIR), bias)

        for which in range(heights):

            @pl.when(late == which)
            def _(which=which):
                down_to_mate(which).wait()
                add_rows(pdown_ref.at[which], 0, [(pdown_ref.at[which], 0), (recvd_ref.at[which], 0)], share)
                if which < heights - 1:
                    to_height(which).start()

        @pl.when(lax.rem(late, CORES) == 0)
        def _():
            for start in range(0, width, TILE):
                cut = slice(start, start + TILE)
                sendu_ref[slot, cut] = dot_tn(low_ref[:, cut], dpre_ref[...]).astype(BF16)
            up_to_mate(slot).start()

        @pl.when(lax.rem(late, CORES) == 1)
        def _():
            up_to_mate(slot).wait()
            for start in range(0, width, TILE):
                cut = slice(start, start + TILE)
                values = dot_tn(low_ref[:, cut], dpre_ref[...])
                pu_ref[slot, cut] = (values + recvu_ref[slot, cut].astype(F32)).astype(BF16)

    @pl.when(step == 2 * parts - 1)
    def _():
        def one(t, sums):
            unit, scaling = norm_stats(res_ref[at(t)])
            grad = acc_ref[at(t)]
            d_proj = norm_backward(grad, unit, scaling, gain1_ref[...][None, :]).astype(BF16)
            dproj_ref[at(t)] = d_proj
            dctx_ref[at(t)] = dot_nt(d_proj, wo_ref[...]).astype(BF16)
            return (
                sums[0] + column_sum(grad * unit),
                sums[1] + column_sum(grad),
                sums[2] + column_sum(d_proj.astype(F32)),
            )

        zero = jnp.zeros((1, width), F32)
        sums = lax.fori_loop(0, tiles, one, (zero, zero, zero), unroll=UNROLL)
        for i, values in enumerate(sums):
            put_row((3 + i) * (width // PAIR), values)
        for start in range(0, width, TILE):
            values = dot_tn(ctx_ref[:, start : start + TILE], dproj_ref[...]).astype(BF16)
            gwo_ref[start : start + TILE] = values[:, : width // 2]
            gwo_ref[width + start : width + start + TILE] = values[:, width // 2 :]
        for which in range(heights - 1):
            to_height(which).wait()
        terms = [(pdown_ref.at[heights - 1], 0)] + [(yland_ref.at[which], 0) for which in range(heights - 1)]
        add_rows(pd_ref, 0, terms, share)


def part_order(step, parts):
    tensor = lax.axis_index("tensor")
    height, core = tensor // CORES, lax.rem(tensor, CORES)
    late = jnp.maximum(step - parts, 0)
    there = lax.rem(height + 1 + late // CORES, parts // CORES)
    whose = jnp.where(lax.rem(late, CORES) == 0, 1 - core, core)
    return jnp.where(step < parts, step, there * CORES + whose)


def feed_forward(res, cot, ctx, w_out, gain1, shift1, gain2, shift2, b_down, b_up, w_up, w_down):
    count, width = res.shape
    parts, _, share = w_up.shape
    heights = parts // 2
    smalls = 6 * width // PAIR + parts * share // PAIR
    smalls = -(-smalls // 8) * 8

    def whole(*shape):
        return pl.BlockSpec(shape, lambda s: (0,) * len(shape), pipeline_mode=pl.Buffered(1))

    def per_part(*shape):
        return pl.BlockSpec((1,) + shape, lambda s: (part_order(s, parts),) + (0,) * len(shape))

    act = jax.ShapeDtypeStruct((count, width), BF16)
    return pl.pallas_call(
        ffn_kernel,
        grid=(2 * parts,),
        in_specs=[whole(count, width)] * 3
        + [whole(width, width)]
        + [whole(width)] * 5
        + [per_part(1, share), per_part(width, share), per_part(share, width)],
        out_specs=[whole(count, width)] * 3
        + [whole(2 * width, width // 2), whole(heights, width, share), whole(share, width), whole(smalls, PAIR)],
        out_shape=[act] * 3
        + [
            jax.ShapeDtypeStruct((2 * width, width // 2), BF16),
            jax.ShapeDtypeStruct((heights, width, share), BF16),
            jax.ShapeDtypeStruct((share, width), BF16),
            jax.ShapeDtypeStruct((smalls, PAIR), F32),
        ],
        scratch_shapes=[
            pltpu.VMEM((count, width), BF16),
            pltpu.VMEM((count, width), F32),
            pltpu.VMEM((parts, count, share), BF16),
            pltpu.VMEM((parts, count, share), BF16),
            pltpu.VMEM((count, width), BF16),
            pltpu.VMEM((count, share), BF16),
            pltpu.VMEM((heights, width, share), BF16),
            pltpu.VMEM((heights, share, width), BF16),
            pltpu.VMEM((heights, width, share), BF16),
            pltpu.VMEM((heights, share, width), BF16),
            pltpu.VMEM((heights, share, width), BF16),
            pltpu.VMEM((heights - 1, share, width), BF16),
            pltpu.SemaphoreType.DMA((3, heights)),
            pltpu.SemaphoreType.DMA((3, heights)),
        ],
        compiler_params=pltpu.CompilerParams(vmem_limit_bytes=60 * 2**20, collective_id=0, has_side_effects=True),
        name="feed_forward",
    )(res, cot, ctx, w_out, gain1, shift1, gain2, shift2, b_down, b_up, w_up, w_down)


def attend_back_kernel(
    dctx_ref, att_ref, inv_ref, q_ref, k_ref, v_ref, sq_ref, sk_ref, w_ref, s_ref, x_ref, seg_ref,
    wqkv_ref, kernel_ref, dproj_ref, gwo_ref, pu_ref, pd_ref, small_ref,
    gt_ref, all_out, up_out, down_out, few_out,
    near_ref, vv_ref, dpad_ref, dcos_ref, dq_ref, dk_ref, dv_ref, joined_ref, gwacc_ref, conv_ref,
    gwlow_ref, gb_ref, flip_ref, mini_ref, all_ref, up_ref, down_ref, few_ref, out_sem, *links,
    plan, quads, seqs,
):
    quad, row = pl.program_id(0), pl.program_id(1)
    length = x_ref.shape[0]
    blocks = length // BLK
    inside = slice(HALO, HALO + length)

    _, sizes, dp_size, tensor_size = plan
    axes = slice_axes(dp_size, tensor_size)
    ticks = schedule(axes, sizes, quads, seqs, gwo_ref, pu_ref, pd_ref, gwlow_ref, mini_ref, all_ref, up_ref, down_ref, few_ref, links,
        (all_out, up_out, down_out, few_out, out_sem))
    calls = quads * seqs * (QUAD // HEAD)

    build_near(*segment_rows(seg_ref, row), near_ref)
    for half in range(2):
        edge = jnp.zeros((HALO, PAIR), BF16)
        for ref in (vv_ref, dpad_ref):
            ref[half, :HALO, :PAIR] = edge
            ref[half, HALO + length :, :PAIR] = edge
        vv_ref[half, inside, PAIR:] = head_mask(half, (length, PAIR))

    @pl.when(row == 0)
    def _():
        conv_ref[...] = jnp.zeros_like(conv_ref)
        gwacc_ref[...] = jnp.zeros_like(gwacc_ref)

    @pl.when((quad == 0) & (row == 0))
    def _():
        gb_ref[...] = jnp.zeros_like(gb_ref)
        flip_ref[...] = place_taps(kernel_ref[...], True)
        mini_ref[...] = jnp.zeros_like(mini_ref)
        mini_ref[: small_ref.shape[0]] = small_ref[...]
        filled = 2 * gwacc_ref.shape[0]
        if gwlow_ref.shape[1] > filled:
            gwlow_ref[:, filled:] = jnp.zeros((quads, gwlow_ref.shape[1] - filled, gwlow_ref.shape[2]), BF16)

    def one_pair(pair, carry):
        at = pl.ds(pl.multiple_of(pair * PAIR, PAIR), PAIR)
        inverse = inv_ref[:, at].astype(F32)
        d_ctx = dctx_ref[:, at]
        d_summed = (d_ctx.astype(F32) * inverse).astype(BF16)
        d_total = (-d_summed.astype(F32) * att_ref[:, at].astype(F32)).astype(BF16)
        both = jnp.concatenate([d_summed, d_total], 1)
        dk = jnp.zeros((length, PAIR), F32)
        dv = jnp.zeros((length, PAIR), F32)
        turn = (quad * seqs + row) * (QUAD // PAIR) + pair
        for half in range(2):
            for when in range(half, calls, 2):
                if ticks.get(when):

                    @pl.when(turn == when // 2)
                    def _(when=when):
                        for event in ticks[when]:
                            event()

            head = pair * 2 + half
            mask = head_mask(half, (length, PAIR))
            vv_ref[half, inside, :PAIR] = v_ref[:, at] * mask
            dpad_ref[half, inside] = d_ctx * mask
            k_half = k_ref[:, at] * mask
            for block in range(blocks):
                here = slice(block * BLK, block * BLK + BLK)
                low, high = window_of(block, blocks)
                d_weight = dot_nt(both[here], vv_ref[half, HALO + low : HALO + high])
                d_cos = d_weight.astype(BF16) * s_ref[0, head, here, low:high]
                dcos_ref[here, low:high] = d_cos
                if low > 0:
                    dcos_ref[here, :low] = jnp.zeros((BLK, low), BF16)
                if high < length:
                    dcos_ref[here, high:] = jnp.zeros((BLK, length - high), BF16)
                grown = dot_nn(d_cos, k_half[low:high])
                if half == 0:
                    dq_ref[here] = grown
                else:
                    dq_ref[here] += grown
                window = slice(block * BLK, block * BLK + 2 * BLK)
                near = near_ref[block]
                taps = band(flip_ref[pl.ds(quad * (QUAD // HEAD) + head, 1)], BLK).astype(BF16) * near
                grown = dot_nn(taps, dpad_ref[half, window])
                if half == 0:
                    dv_ref[here] = grown
                else:
                    dv_ref[here] += grown
                conv_ref[head] += near.astype(F32) * dot_nt(d_ctx[here], vv_ref[half, window, :PAIR])
            dk += dot_tn(dcos_ref[...], q_ref[:, at] * mask)
            dv += dot_tn(w_ref[0, head], d_summed * mask)
        dv_ref[...] += dv
        grad = SLOPE * dq_ref[...]
        unit = q_ref[:, at].astype(F32)
        d_query = sq_ref[:, at].astype(F32) * (SHRINK * grad - unit * (head_sum(grad * unit) / SHRINK))
        grad = SLOPE * dk
        unit = k_ref[:, at].astype(F32)
        d_key = sk_ref[:, at].astype(F32) * (grad - unit * head_sum(grad * unit))
        for part, values in enumerate((d_query, d_key, dv_ref[...])):
            joined_ref[quad, row, :, pl.ds(pl.multiple_of(part * QUAD + pair * PAIR, PAIR), PAIR)] = values.astype(BF16)
        return carry

    lax.fori_loop(0, QUAD // PAIR, one_pair, 0)

    gb_ref[quad, :1] += column_sum(joined_ref[quad, row].astype(F32))
    width = gwacc_ref.shape[0]
    for start in range(0, width, TILE):
        cut = slice(start, start + TILE)
        gwacc_ref[cut] += dot_tn(x_ref[:, cut], joined_ref[quad, row])

    @pl.when(row == seqs - 1)
    def _():
        half = gwacc_ref.shape[1] // 2
        for start in range(0, width, TILE):
            for side in range(2):
                values = gwacc_ref[start : start + TILE, side * half : (side + 1) * half]
                gwlow_ref[quad, side * width + start : side * width + start + TILE] = values.astype(BF16)
        base = small_ref.shape[0]
        lines = gb_ref.shape[2] // PAIR
        for i in range(lines):
            mini_ref[pl.ds(base + quad * lines + i, 1)] = gb_ref[quad, :1, i * PAIR : (i + 1) * PAIR]
        base += quads * lines
        for head in range(QUAD // HEAD):
            sums = conv_ref[head]
            high = sums.astype(BF16)
            turn = (rows((BLK, BLK)) + lanes((BLK, BLK)) == BLK - 1).astype(BF16)
            turned = dot_nn(turn, high) + dot_nn(turn, (sums - high.astype(F32)).astype(BF16))
            turned = pltpu.roll(turned, BLK, 1, stride=1, stride_axis=0)
            mini_ref[pl.ds(base + quad * (QUAD // HEAD) + head, 1)] = column_sum(turned)[:, :PAIR]

    last = (quad == quads - 1) & (row == seqs - 1)

    @pl.when(last)
    def _():
        for event in ticks.get(calls, ()):
            event()

    @pl.when(quad == quads - 1)
    def _():
        for start in range(0, length, TILE):
            cut = slice(start, start + TILE)
            grown = dproj_ref[cut].astype(F32)
            for q in range(quads):
                for part in range(3):
                    to = part * width + q * QUAD
                    grown += dot_nt(joined_ref[q, row, cut, part * QUAD : (part + 1) * QUAD], wqkv_ref[:, to : to + QUAD])
            gt_ref[cut] = grown.astype(BF16)

    @pl.when(last)
    def _():
        for when in sorted(ticks):
            if when > calls:
                for event in ticks[when]:
                    event()


FFN_PLAN = (
    (
        (("x", "z"), (4, 9, 15, 24, 54)),
        (("z", "x"), (3, 27, 30, 50, 59)),
    ),
    (
        (("x", "z"), (0, 8, 15, 21, 34, 43)),
        (("x", "z"), (7, 19, 23, 29, 38, 56)),
    ),
)
ALL_PLAN = (
    (
        (3, 1, (2, 4, 11, 13, 16, 29, 35, 45, 55)),
    ),
    (
        (3, 0, (10, 11, 17, 26, 31, 41, 47, 52, 59)),
    ),
    (
        (3, 0, (19, 21, 28, 37, 42, 48, 51, 57, 60)),
    ),
    (
        (3, 1, (24, 25, 32, 36, 39, 44, 48, 55, 58)),
    ),
)
MINI_ORDER = 1
MINI_TIMES = (25, 27, 33, 40, 46, 49, 52, 53, 55)
FFN_ROWS = 384
ORDERS = (("core", "x", "y", "z"), ("core", "y", "x", "z"))


def all_parts(index, size, devices):
    parts = ALL_PLAN[index]
    if sum(units for units, _, _ in parts) * 16 * devices != size:
        parts = ((size // (16 * devices), parts[-1][1], parts[-1][2]),)
    out, start = [], 0
    for units, order, times in parts:
        rows_of = units * 16 * devices
        out.append((start, rows_of, ORDERS[order], times))
        start += rows_of
    return out


class FfnReduction(Reduction):
    def copies(self, stage):
        if stage > 0:
            return super().copies(stage)
        axis = self.axes["y"]
        return [
            send(
                self.source.at[j - 1, span(self.source_at, self.size)], self.landings[0].at[j - 1],
                self.sems, self.first_sem + j - 1, axis.device(axis.ahead(j)),
            )
            for j in range(1, axis.size)
        ]

    def plan(self):
        size, at = self.size, self.final_at
        out = [(self.axes["y"], size, at)]
        for name in self.order[1:]:
            axis = self.axes[name]
            size //= axis.size
            at = at + axis.place * size
            out.append((axis, size, at))
        return out

    def settle(self, stage):
        if stage > 0:
            return super().settle(stage)
        axis = self.axes["y"]
        for copy in self.copies(0):
            copy.wait()
        terms = [(self.source.at[axis.size - 1], self.source_at)]
        terms += [(self.landings[0].at[j - 1], 0) for j in range(1, axis.size)]
        add_rows(self.landings[0].at[0], 0, terms, self.size)


def link_plan(sizes, width, share, quads):
    out = []
    devices = math.prod(sizes.values())
    y = sizes["y"]
    for late, (height, columns) in enumerate(((share, width), (width, share))):
        for start in range(0, height, FFN_ROWS):
            order = FFN_PLAN[late][start // FFN_ROWS][0]
            shapes = [pltpu.VMEM((y - 1, FFN_ROWS, columns), BF16)] if late else []
            shapes += landing_shapes(order, sizes, FFN_ROWS, columns, BF16)
            out.append((shapes, copies_of((("y",) if late else ()) + order, order, sizes)))
    size = padded(2 * width, devices)
    for index in range(quads + 1):
        for _, rows_of, order, _ in all_parts(index, size, devices):
            out.append((landing_shapes(order, sizes, rows_of, width // 2, BF16), copies_of(order, order, sizes)))
    order = ORDERS[MINI_ORDER]
    out.append((landing_shapes(order, sizes, 8 * devices, PAIR, F32), copies_of(order, order, sizes)))
    return out


def padded(size, devices):
    return -(-size // (16 * devices)) * 16 * devices


def schedule(axes, sizes, quads, seqs, gwo_ref, pu_ref, pd_ref, gwlow_ref, mini_ref, all_ref, up_ref, down_ref, few_ref, links, outs):
    all_out, up_out, down_out, few_out, out_sem = outs
    calls = quads * seqs * (QUAD // HEAD)
    share, width = pd_ref.shape
    devices = math.prod(sizes.values())
    groups = link_plan(sizes, width, share, quads)
    taken, position = [], 0
    for shapes, _ in groups:
        taken.append((links[position : position + len(shapes)], links[position + len(shapes) : position + len(shapes) + 2]))
        position += len(shapes) + 2
    ticks = {0: [lambda: greet(axes)]}

    stores = []

    def enlist(reduction, times, done, place):
        for time, event in zip(times, reduction.events(), strict=True):
            ticks.setdefault(time, []).append(event)
        store = pltpu.make_async_copy(done, place, out_sem.at[len(stores)])
        ticks[times[-1]].append(store.start)
        stores.append(store)

    number = 0
    for late, (source, final, place) in enumerate(((pd_ref, down_ref, down_out), (pu_ref, up_ref, up_out))):
        for start in range(0, final.shape[0], FFN_ROWS):
            landings, sems = taken[number]
            block = span(start, FFN_ROWS)
            order, times = FFN_PLAN[late][start // FFN_ROWS]
            kind = FfnReduction if late else Reduction
            whole_order = ("y",) + order if late else order
            reduction = kind(axes, whole_order, order[::-1], source, start, FFN_ROWS, final, start, landings, sems)
            enlist(reduction, times, final.at[block], place.at[block])
            number += 1
    size = padded(2 * width, devices)
    for index in range(quads + 1):
        source = gwo_ref if index == 0 else gwlow_ref.at[index - 1]
        for start, rows_of, order, times in all_parts(index, size, devices):
            landings, sems = taken[number]
            final = all_ref.at[index]
            reduction = Reduction(axes, order, order[::-1], source, start, rows_of, final, start, landings, sems)
            enlist(reduction, times, final.at[span(start, rows_of)], all_out.at[index, span(start, rows_of)])
            number += 1
    landings, sems = taken[number]
    order = ORDERS[MINI_ORDER]
    reduction = Reduction(axes, order, order[::-1], mini_ref, 0, 8 * devices, few_ref, 0, landings, sems)
    enlist(reduction, MINI_TIMES, few_ref, few_out)
    ticks[max(ticks) + 1] = [store.wait for store in stores]
    return ticks


def attend_back(dctx, att, inv, q, k, v, sq, sk, weight, slope, tokens, segment_ids, w_qkv, kernel, dproj, gwo, pu, pd, small, dp_size, tensor_size):
    count, width = tokens.shape
    seqs, length = segment_ids.shape
    quads = width // QUAD
    per = QUAD // HEAD
    blocks = length // BLK
    own = pl.BlockSpec((length, QUAD), lambda p, r: (r, p))
    big = pl.BlockSpec((1, per, length, length), lambda p, r: (r, p, 0, 0))
    wide = pl.BlockSpec((length, width), lambda p, r: (r, 0))

    sizes = {"core": CORES, "y": tensor_size // CORES, "x": dp_size // DEPTH, "z": DEPTH}
    devices = dp_size * tensor_size
    share = pd.shape[0]
    grown = padded(2 * width, devices)
    gwo = jnp.pad(gwo, ((0, grown - gwo.shape[0]), (0, 0)))
    minis = 8 * devices
    scratch = []
    for shapes, count_of in link_plan(sizes, width, share, quads):
        scratch += shapes + [pltpu.SemaphoreType.DMA((count_of,)), pltpu.SemaphoreType.DMA((count_of,))]

    def whole(*shape):
        return pl.BlockSpec(shape, lambda p, r: (0,) * len(shape), pipeline_mode=pl.Buffered(1))

    return pl.pallas_call(
        functools.partial(attend_back_kernel, plan=(None, sizes, dp_size, tensor_size), quads=quads, seqs=seqs),
        grid=(quads, seqs),
        in_specs=[own] * 8
        + [big] * 2
        + [
            wide,
            whole(*segment_ids.shape),
            whole(width, 3 * width),
            whole(*kernel.shape),
            wide,
            whole(*gwo.shape), whole(*pu.shape), whole(*pd.shape), whole(*small.shape),
        ],
        out_specs=[
            pl.BlockSpec((length, width), lambda p, r: (jnp.where(p == quads - 1, r, 0), 0)),
        ]
        + [pl.BlockSpec(memory_space=pl.ANY)] * 4,
        out_shape=[
            jax.ShapeDtypeStruct((count, width), BF16),
            jax.ShapeDtypeStruct((quads + 1, grown, width // 2), BF16),
            jax.ShapeDtypeStruct((width, share), BF16),
            jax.ShapeDtypeStruct((share, width), BF16),
            jax.ShapeDtypeStruct((minis, PAIR), F32),
        ],
        scratch_shapes=[
            pltpu.VMEM((blocks, BLK, 2 * BLK), BF16),
            pltpu.VMEM((2, length + 2 * HALO, 2 * PAIR), BF16),
            pltpu.VMEM((2, length + 2 * HALO, PAIR), BF16),
            pltpu.VMEM((length, length), BF16),
            pltpu.VMEM((length, PAIR), F32),
            pltpu.VMEM((length, PAIR), F32),
            pltpu.VMEM((length, PAIR), F32),
            pltpu.VMEM((quads, seqs, length, 3 * QUAD), BF16),
            pltpu.VMEM((width, 3 * QUAD), F32),
            pltpu.VMEM((per, BLK, 2 * BLK), F32),
            pltpu.VMEM((quads, grown, width // 2), BF16),
            pltpu.VMEM((quads, 8, 3 * QUAD), F32),
            pltpu.VMEM((width // HEAD, 2 * BLK), F32),
            pltpu.VMEM((minis, PAIR), F32),
            pltpu.VMEM((quads + 1, grown, width // 2), BF16),
            pltpu.VMEM((width, share), BF16),
            pltpu.VMEM((share, width), BF16),
            pltpu.VMEM((minis, PAIR), F32),
            pltpu.SemaphoreType.DMA((len(link_plan(sizes, width, share, quads)),)),
        ]
        + scratch,
        compiler_params=pltpu.CompilerParams(vmem_limit_bytes=60 * 2**20, collective_id=1, has_side_effects=True),
        name="attend_backward",
    )(dctx, att, inv, q, k, v, sq, sk, weight, slope, tokens, segment_ids, w_qkv, kernel, dproj, gwo, pu, pd, small)


def spread_kernel(low_ref, high_ref, up_ref, down_ref, few_ref, a_ref, b_ref, gw_ref, gwo_ref, gup_ref, gdown_ref, a_out, b_out, *vectors, first_lane, base):
    width = gwo_ref.shape[1]
    half = width // 2
    quads = low_ref.shape[0] - 1
    gwo_ref[:, :half] = low_ref[0].astype(F32)
    gwo_ref[:, half:] = high_ref[0].astype(F32)
    for quad in range(quads):
        for part in range(3):
            for start in range(part * QUAD, (part + 1) * QUAD, PAIR):
                side, lane = (low_ref, start) if start < half else (high_ref, start - half)
                to = part * width + quad * QUAD + start - part * QUAD
                gw_ref[:, to : to + PAIR] = side[1 + quad, :, lane : lane + PAIR].astype(F32)
    a_out[...] = a_ref[...]
    b_out[...] = b_ref[...]
    gup_ref[...] = up_ref[...].astype(F32)
    gdown_ref[...] = down_ref[...].astype(F32)

    @pl.when(pl.program_id(0) == 0)
    def _():
        gb_ref, conv_ref, *six, gbu_ref = vectors
        lines = width // PAIR

        def copy_line(target, to, line):
            target[to * PAIR : (to + 1) * PAIR] = few_ref[line]

        for number, target in enumerate(six):
            for i in range(lines):
                copy_line(target, i, number * lines + i)
        share = gbu_ref.shape[0] // PAIR
        mine = lax.axis_index("tensor") * share
        for i in range(share):
            copy_line(gbu_ref, i, 6 * lines + mine + i)
        per = QUAD // PAIR
        for quad in range(quads):
            for part in range(3):
                for i in range(per):
                    copy_line(gb_ref, (part * width + quad * QUAD) // PAIR + i, base + (quad * 3 + part) * per + i)
        heads, taps = conv_ref.shape
        kept = few_ref[base + 3 * lines : base + 3 * lines + heads]
        conv_ref[...] = pltpu.roll(kept, PAIR - first_lane, 1)[:, :taps]


def spread_out(grads, up, down, few, out, gt, width, heads, taps, first_lane, base):
    chunks = grads.shape[0]
    quads = chunks - 1
    steps = 8
    rows_of = width // steps
    share = up.shape[1]
    down_rows = share // steps

    def whole(*shape):
        return pl.BlockSpec(shape, lambda s: (0,) * len(shape))

    def by_rows(count, columns):
        return pl.BlockSpec((count, columns), lambda s: (s, 0))

    row = jax.ShapeDtypeStruct((width,), F32)
    return pl.pallas_call(
        functools.partial(spread_kernel, first_lane=first_lane, base=base),
        grid=(steps,),
        in_specs=[
            pl.BlockSpec((chunks, rows_of, width // 2), lambda s: (0, s, 0)),
            pl.BlockSpec((chunks, rows_of, width // 2), lambda s: (0, steps + s, 0)),
            by_rows(rows_of, share),
            by_rows(down_rows, width),
            whole(*few.shape),
            by_rows(out.shape[0] // steps, width), by_rows(out.shape[0] // steps, width),
        ],
        out_specs=[
            by_rows(rows_of, 3 * width), by_rows(rows_of, width), by_rows(rows_of, share), by_rows(down_rows, width),
            by_rows(out.shape[0] // steps, width), by_rows(out.shape[0] // steps, width),
            whole(3 * width), whole(heads, taps),
        ]
        + [whole(width)] * 6
        + [whole(share)],
        out_shape=[
            jax.ShapeDtypeStruct((width, 3 * width), F32),
            jax.ShapeDtypeStruct((width, width), F32),
            jax.ShapeDtypeStruct((width, share), F32),
            jax.ShapeDtypeStruct((share, width), F32),
            jax.ShapeDtypeStruct(out.shape, out.dtype),
            jax.ShapeDtypeStruct(gt.shape, gt.dtype),
            jax.ShapeDtypeStruct((3 * width,), F32),
            jax.ShapeDtypeStruct((heads, taps), F32),
        ]
        + [row] * 6
        + [jax.ShapeDtypeStruct((share,), F32)],
        compiler_params=pltpu.CompilerParams(vmem_limit_bytes=60 * 2**20),
        name="spread_out",
    )(grads, grads, up, down, few, out, gt)


def body(
    tokens, segment_ids, w_qkv, b_qkv, conv_kernel, w_out, b_out, norm1_gain, norm1_bias,
    w_up, b_up, w_down, b_down, norm2_gain, norm2_bias, cotangent,
):
    width = tokens.shape[1]
    heads, taps = conv_kernel.shape
    dp_size, tensor_size = lax.axis_size("dp"), lax.axis_size("tensor")
    q, k, v, sq, sk, weight, slope, att, inv, ctx, res, up_all, down_all, bias_all = attend(
        tokens, segment_ids, w_qkv, b_qkv, conv_kernel, w_out, b_out, w_up, w_down, b_up, dp_size, tensor_size
    )
    out, dproj, dctx, gwo, pu, pd, small = feed_forward(
        res, cotangent, ctx, w_out, norm1_gain, norm1_bias, norm2_gain, norm2_bias, b_down, bias_all, up_all, down_all
    )
    gt, grads, grad_up, grad_down, few = attend_back(
        dctx, att, inv, q, k, v, sq, sk, weight, slope, tokens, segment_ids, w_qkv, conv_kernel, dproj,
        gwo, pu, pd, small, dp_size, tensor_size,
    )
    first_lane = (HALO - taps // 2 + BLK - 1 + BLK) % (2 * BLK)
    gw, gwo, grad_up, grad_down, out, gt, gb, grad_conv, gg2, gs2, gbd, gg1, gs1, gbo, gbu = spread_out(
        grads, grad_up, grad_down, few, out, gt, width, heads, taps, first_lane, small.shape[0]
    )
    return (out, gt, gw, gb, grad_conv, gwo, gbo, gg1, gs1, grad_up, gbu, grad_down, gbd, gg2, gs2)


def solution(mesh):
    placed = (
        P(("dp", "tensor"), None),
        P(("dp", "tensor"), None),
        P(), P(), P(), P(), P(), P(), P(),
        P(None, "tensor"),
        P("tensor"),
        P("tensor", None),
        P(), P(), P(),
        P(("dp", "tensor"), None),
    )
    return jax.shard_map(
        body,
        mesh=mesh,
        in_specs=placed,
        out_specs=(
            P(("dp", "tensor"), None),
            P(("dp", "tensor"), None),
            P(), P(), P(), P(), P(), P(), P(),
            P(None, "tensor"),
            P("tensor"),
            P("tensor", None),
            P(), P(), P(),
        ),
        check_vma=False,
    )
```

```python
import functools
import math

import jax
import jax.numpy as jnp
from jax import lax
from jax.experimental import pallas as pl
from jax.experimental.pallas import tpu as pltpu
from jax.sharding import PartitionSpec as P

F32 = jnp.float32
BF16 = jnp.bfloat16
EPS_NORM = 1e-5
EPS_UNIT = 1e-6
SHRINK = 0.95
TAU = 8
SLOPE = TAU / math.pi
ARC = (0.49999996, -0.06830509, 0.02825875, -0.01557005, 0.00864352, -0.00363107, 0.00076235)
QUAD = 256
PAIR = 128
HEAD = 64
BLK = 128
HALO = 64


def dot_nn(a, b):
    return lax.dot_general(a, b, (((1,), (0,)), ((), ())), preferred_element_type=F32)


def dot_nt(a, b):
    return lax.dot_general(a, b, (((1,), (1,)), ((), ())), preferred_element_type=F32)


def dot_tn(a, b):
    return lax.dot_general(a, b, (((0,), (0,)), ((), ())), preferred_element_type=F32)


def lanes(shape):
    return lax.broadcasted_iota(jnp.int32, shape, len(shape) - 1)


def rows(shape):
    return lax.broadcasted_iota(jnp.int32, shape, len(shape) - 2)


def head_sum(values):
    width = values.shape[-1]
    ones = (rows((width, width)) // HEAD == lanes((width, width)) // HEAD).astype(BF16)
    high = values.astype(BF16)
    low = (values - high.astype(F32)).astype(BF16)
    return dot_nn(high, ones) + dot_nn(low, ones)


def closeness_terms(cosine):
    size = jnp.abs(cosine)
    room = 1.0 - size
    inverse = lax.rsqrt(room)
    poly = jnp.full_like(size, ARC[-1])
    for coefficient in ARC[-2::-1]:
        poly = poly * size + coefficient
    small = room * inverse * poly
    close = jnp.where(cosine >= 0.0, 1.0 - small, small)
    two = close * close
    four = two * two
    slope = (four * two) * (close * inverse) * lax.rsqrt(1.0 + size)
    return four * four, slope


def head_mask(half, shape):
    return (lanes(shape) // HEAD == half).astype(BF16)


def window_of(block, blocks):
    low = max(0, block * BLK - 256)
    high = min(blocks * BLK, block * BLK + BLK + 256)
    return low, high


def band(taps, count):
    spread = jnp.broadcast_to(taps, (count, taps.shape[1]))
    return pltpu.roll(spread, 0, 1, stride=1, stride_axis=0)


def norm_stats(values):
    centred = values - jnp.mean(values, -1, keepdims=True)
    scaling = lax.rsqrt(jnp.mean(centred * centred, -1, keepdims=True) + EPS_NORM)
    return centred * scaling, scaling


def segment_rows(seg_ref, row):
    ids = seg_ref[pl.ds(row, 1)].astype(F32)
    edge = jnp.full((1, HALO), -1.0, F32)
    return jnp.concatenate([edge, ids, edge], 1), jnp.broadcast_to(ids, (PAIR, ids.shape[1])).T[:, :1]


def build_same(seg_pad, seg_col, same_ref):
    length = seg_col.shape[0]
    for start in range(0, length, BLK):
        own = seg_col[start : start + BLK]
        same_ref[start : start + BLK, :] = jnp.where(
            own == seg_pad[:, HALO : HALO + length], 1.0, 0.0
        ).astype(BF16)


def build_near(seg_pad, seg_col, near_ref):
    length = seg_col.shape[0]
    for start in range(0, length, BLK):
        own = seg_col[start : start + BLK]
        near_ref[start // BLK] = jnp.where(
            own == seg_pad[:, start : start + 2 * BLK], 1.0, 0.0
        ).astype(BF16)


def place_taps(kernel, reverse):
    taps = kernel.shape[1]
    shape = (taps, 2 * BLK)
    tap = taps - 1 - rows(shape) if reverse else rows(shape)
    return dot_nn(kernel.astype(BF16), (lanes(shape) == tap + HALO - taps // 2).astype(BF16))


def attend_kernel(
    x_ref, seg_ref, wq_ref, wk_ref, wv_ref, b_ref, kernel_ref, wo_ref, bo_ref,
    wu_ref, wd_ref, bu_ref,
    q_ref, k_ref, v_ref, sq_ref, sk_ref, w_ref, s_ref, att_ref, inv_ref, ctx_ref, res_ref,
    up_ref, down_ref, bias_ref,
    same_ref, near_ref, vv_ref, tap_ref, mine_ref, send_sem, recv_sem, copy_sem,
    *, dp_size, tensor_size,
):
    row, quad = pl.program_id(0), pl.program_id(1)
    quads, seqs = pl.num_programs(1), pl.num_programs(0)
    ticks = gather_plan(dp_size, tensor_size, (wu_ref, wd_ref, mine_ref), (up_ref, down_ref, bias_ref), (send_sem, recv_sem), copy_sem)
    length = x_ref.shape[0]
    blocks = length // BLK

    @pl.when((row == 0) & (quad == 0))
    def _():
        tap_ref[...] = place_taps(kernel_ref[...], False)
        mine_ref[...] = bu_ref[...].astype(F32)[None, :]

    @pl.when(quad == 0)
    def _():
        seg_pad, seg_col = segment_rows(seg_ref, row)
        build_same(seg_pad, seg_col, same_ref)
        build_near(seg_pad, seg_col, near_ref)
        for half in range(2):
            edge = jnp.zeros((HALO, 2 * PAIR), BF16)
            vv_ref[half, :HALO] = edge
            vv_ref[half, HALO + length :] = edge
            vv_ref[half, HALO : HALO + length, PAIR:] = head_mask(half, (length, PAIR))

    def bias(part):
        start = pl.multiple_of(part * x_ref.shape[1] + quad * QUAD, QUAD)
        return b_ref[pl.ds(start, QUAD)][None, :]

    for start in range(0, length, ROWS):
        here = slice(start, start + ROWS)
        x = x_ref[here]
        for number, (w, unit, scale, factor) in enumerate(
            ((wq_ref, q_ref, sq_ref, SHRINK), (wk_ref, k_ref, sk_ref, 1.0))
        ):
            part = dot_nn(x, w[...]) + bias(number)
            scaling = lax.rsqrt(head_sum(part * part) + EPS_UNIT)
            unit[here] = (part * (scaling * factor)).astype(BF16)
            scale[here] = scaling.astype(BF16)
        v_ref[here] = (dot_nn(x, wv_ref[...]) + bias(2)).astype(BF16)

    def one_pair(pair, carry):
        turn = (row * quads + quad) * (QUAD // PAIR) + pair
        for when, events in ticks.items():

            @pl.when(turn == when)
            def _(events=events):
                for event in events:
                    event()

        at = pl.ds(pl.multiple_of(pair * PAIR, PAIR), PAIR)
        v = v_ref[:, at]
        for half in range(2):
            vv_ref[half, HALO : HALO + length, :PAIR] = v * head_mask(half, (length, PAIR))
        for block in range(blocks):
            here = slice(block * BLK, block * BLK + BLK)
            low, high = window_of(block, blocks)
            q = q_ref[here, at]
            total = jnp.zeros((BLK, 2 * PAIR), F32)
            near = jnp.zeros((BLK, PAIR), F32)
            for half in range(2):
                head = pair * 2 + half
                q_half = q * head_mask(half, (BLK, PAIR))
                for start in range(low, high, KCH):
                    stop = min(start + KCH, high)
                    cosine = dot_nt(q_half, k_ref[start:stop, at])
                    weight, slope = closeness_terms(cosine)
                    same = same_ref[here, start:stop]
                    weight = weight.astype(BF16) * same
                    w_ref[0, head, here, start:stop] = weight
                    s_ref[0, head, here, start:stop] = slope.astype(BF16) * same
                    total += dot_nn(weight, vv_ref[half, HALO + start : HALO + stop])
                if low > 0:
                    w_ref[0, head, here, :low] = jnp.zeros((BLK, low), BF16)
                if high < length:
                    w_ref[0, head, here, high:] = jnp.zeros((BLK, length - high), BF16)
                taps = band(tap_ref[pl.ds(quad * (QUAD // HEAD) + head, 1)], BLK).astype(BF16) * near_ref[block]
                near += dot_nn(taps, vv_ref[half, block * BLK : block * BLK + 2 * BLK, :PAIR])
            inverse = 1.0 / (1.0 + total[:, PAIR:])
            attended = total[:, :PAIR] * inverse
            att_ref[here, at] = attended.astype(BF16)
            inv_ref[here, at] = inverse.astype(BF16)
            ctx_ref[here, at] = (attended + near).astype(BF16)
        return carry

    lax.fori_loop(0, QUAD // PAIR, one_pair, 0)

    @pl.when(quad == 0)
    def _():
        res_ref[...] = x_ref[...].astype(F32) + bo_ref[...][None, :]

    for start in range(0, length, ROWS):
        here = slice(start, start + ROWS)
        res_ref[here] += dot_nn(ctx_ref[here], wo_ref[...])


def gather_plan(dp_size, tensor_size, own, whole, sems, copy_sem):
    axes = slice_axes(dp_size, tensor_size)
    y, x, core = axes["y"], axes["x"], axes["core"]
    mate = core.device(core.ahead(1))
    number = iter(range(1000))

    def mine(place):
        return place * CORES + core.place

    def half_of(ref, piece):
        size = ref.shape[-2] // 2
        return span(piece % 2 * size, size)

    def rows_at(ref, piece, place):
        size = ref.shape[-2] // (2 * x.size)
        return span(piece % 2 * x.size * size + place * size, size)

    def at_y(piece):
        source, target = own[piece // 2], whole[piece // 2]
        out = []
        for j in range(1, y.size):
            if piece < 4:
                block = rows_at(source, piece, x.place)
                pair = (source.at[block], target.at[mine(y.place), block])
            else:
                pair = (source, target.at[mine(y.place)])
            out.append(send(*pair, sems, next(number), y.device(y.ahead(j))))
        return out

    def at_x(piece):
        target = whole[piece // 2]
        out = []
        for j in range(1, y.size):
            block = target.at[mine(y.ahead(j)), rows_at(target, piece, x.place)]
            out += [send(block, block, sems, next(number), x.device(x.ahead(i))) for i in range(1, x.size)]
        return out

    def to_mate(piece):
        target = whole[piece // 2]
        out = []
        for j in range(1, y.size):
            block = target.at[mine(y.ahead(j))]
            block = block.at[half_of(target, piece)] if piece < 4 else block
            out.append(send(block, block, sems, next(number), mate))
        return out

    keep = [pltpu.make_async_copy(own[i], whole[i].at[mine(y.place)], copy_sem.at[i]) for i in range(3)]
    give = [send(own[i], whole[i].at[mine(y.place)], sems, next(number), mate) for i in range(3)]
    ys, xs, mates = [at_y(i) for i in range(5)], [at_x(i) for i in range(4)], [to_mate(i) for i in range(5)]

    def start(copies):
        return [copy.start for copy in copies]

    def wait(copies):
        return [copy.wait for copy in copies]

    steps = [
        [lambda: greet(axes, ("core", "y", "x"))] + start(ys[0] + ys[1] + ys[4] + give + keep),
        wait(ys[0] + ys[4]) + start(xs[0] + ys[2] + mates[4]),
        wait(ys[1]) + start(xs[1] + ys[3]),
        wait(ys[2] + xs[0]) + start(xs[2] + mates[0]),
        wait(ys[3] + xs[1]) + start(xs[3] + mates[1]),
        wait(xs[2] + xs[3]) + start(mates[2] + mates[3]),
    ]
    last = wait([copy for piece in mates for copy in piece] + give + keep)
    return dict(zip(GATHER_TIMES, steps)) | {GATHER_TIMES[len(steps)]: last}


GATHER_TIMES = (0, 4, 5, 7, 8, 10, 11)


KCH = 256
ROWS = 256


def attend(tokens, segment_ids, w_qkv, b_qkv, kernel, w_out, b_out, w_up, w_down, b_up, dp_size, tensor_size):
    count, width = tokens.shape
    seqs, length = segment_ids.shape
    quads = width // QUAD
    heads = width // HEAD
    per = QUAD // HEAD
    blocks = length // BLK
    own = pl.BlockSpec((length, QUAD), lambda r, p: (r, p))
    act = jax.ShapeDtypeStruct((count, width), BF16)
    big = jax.ShapeDtypeStruct((seqs, heads, length, length), BF16)
    big_spec = pl.BlockSpec((1, per, length, length), lambda r, p: (r, p, 0, 0))

    def part(rows_of, k):
        return pl.BlockSpec((rows_of, QUAD), lambda r, p, k=k: (0, p + k * quads))

    def whole(*shape):
        return pl.BlockSpec(shape, lambda r, p: (0,) * len(shape), pipeline_mode=pl.Buffered(1))

    others = tensor_size // CORES - 1
    copies = 3 + 10 * others + 4 * others * (dp_size // DEPTH - 1)
    return pl.pallas_call(
        functools.partial(attend_kernel, dp_size=dp_size, tensor_size=tensor_size),
        grid=(seqs, quads),
        in_specs=[
            pl.BlockSpec((length, width), lambda r, p: (r, 0)),
            whole(*segment_ids.shape),
            part(width, 0), part(width, 1), part(width, 2),
            whole(*b_qkv.shape),
            whole(*kernel.shape),
            pl.BlockSpec((QUAD, width), lambda r, p: (p, 0)),
            whole(*b_out.shape),
        ]
        + [
            whole(*each.shape) for each in (w_up, w_down, b_up)
        ],
        out_specs=[own] * 5 + [big_spec] * 2 + [own] * 3 + [pl.BlockSpec((length, width), lambda r, p: (r, 0))]
        + [pl.BlockSpec(memory_space=pl.ANY)] * 3,
        out_shape=[act] * 5 + [big] * 2 + [act] * 3 + [jax.ShapeDtypeStruct((count, width), F32)]
        + [jax.ShapeDtypeStruct((tensor_size,) + part.shape, BF16) for part in (w_up, w_down)]
        + [jax.ShapeDtypeStruct((tensor_size, 1, b_up.shape[0]), F32)],
        scratch_shapes=[
            pltpu.VMEM((length, length), BF16),
            pltpu.VMEM((blocks, BLK, 2 * BLK), BF16),
            pltpu.VMEM((2, length + 2 * HALO, 2 * PAIR), BF16),
            pltpu.VMEM((heads, 2 * BLK), F32),
            pltpu.VMEM((1, b_up.shape[0]), F32),
            pltpu.SemaphoreType.DMA((copies,)),
            pltpu.SemaphoreType.DMA((copies,)),
            pltpu.SemaphoreType.DMA((3,)),
        ],
        compiler_params=pltpu.CompilerParams(vmem_limit_bytes=56 * 2**20, collective_id=2, has_side_effects=True),
        name="attend_forward",
    )(tokens, segment_ids, w_qkv, w_qkv, w_qkv, b_qkv, kernel, w_out, b_out, w_up, w_down, b_up)


DEPTH = 4
CORES = 2


class Axis:
    def __init__(self, size, place, device):
        self.size, self.place, self.device = size, place, device

    def ahead(self, j):
        return lax.rem(self.place + j, self.size)


def slice_axes(dp_size, tensor_size):
    dp, tensor = lax.axis_index("dp"), lax.axis_index("tensor")
    across = dp_size // DEPTH
    z, x = dp // across, lax.rem(dp, across)
    y, core = tensor // CORES, lax.rem(tensor, CORES)
    return {
        "core": Axis(CORES, core, lambda p: (dp, y * CORES + p)),
        "y": Axis(tensor_size // CORES, y, lambda p: (dp, p * CORES + core)),
        "x": Axis(across, x, lambda p: (z * across + p, tensor)),
        "z": Axis(DEPTH, z, lambda p: (p * across + x, tensor)),
    }


def greet(axes, names=("core", "y", "x", "z")):
    barrier = pltpu.get_barrier_semaphore()
    count = 0
    for axis in (axes[name] for name in names):
        for j in range(1, axis.size):
            pl.semaphore_signal(
                barrier, inc=1, device_id=axis.device(axis.ahead(j)), device_id_type=pl.DeviceIdType.MESH
            )
            count += 1
    pl.semaphore_wait(barrier, count)


def send(source, target, sems, at, device):
    return pltpu.make_async_remote_copy(
        src_ref=source, dst_ref=target, send_sem=sems[0].at[at], recv_sem=sems[1].at[at],
        device_id=device, device_id_type=pl.DeviceIdType.MESH,
    )


def span(start, size):
    if isinstance(start, int):
        return pl.ds(start, size)
    return pl.ds(pl.multiple_of(start, math.gcd(size, 16)), size)


def add_rows(target, target_at, terms, size):
    tile = next(t for t in (64, 48, 32, 24, 16, 12, 8) if size % t == 0)

    def one(i, carry):
        total = None
        for ref, start in terms:
            rows_of = ref[span(start + i * tile, tile)].astype(F32)
            total = rows_of if total is None else total + rows_of
        target[span(target_at + i * tile, tile)] = total.astype(target.dtype)
        return carry

    lax.fori_loop(0, size // tile, one, 0)


class Reduction:
    def __init__(self, axes, order, back, source, source_at, size, final, final_at, landings, sems, first_sem=0):
        self.axes, self.order, self.back = axes, order, back
        self.source, self.source_at, self.size = source, source_at, size
        self.final, self.final_at = final, final_at
        self.landings, self.sems = landings, sems
        self.first_sem = first_sem

    def plan(self):
        size, at, out = self.size, self.final_at, []
        for name in self.order:
            axis = self.axes[name]
            size //= axis.size
            at = at + axis.place * size
            out.append((axis, size, at))
        return out

    def copies(self, stage):
        stages = self.plan()
        sem = self.first_sem
        for axis, _, _ in stages[:stage]:
            sem += axis.size - 1
        axis, size, _ = stages[stage]
        held, held_at = (self.source, self.source_at) if stage == 0 else (self.landings[stage - 1].at[0], 0)
        return [
            send(
                held.at[span(held_at + axis.ahead(j) * size, size)], self.landings[stage].at[j - 1],
                self.sems, sem + j - 1, axis.device(axis.ahead(j)),
            )
            for j in range(1, axis.size)
        ]

    def settle(self, stage):
        for copy in self.copies(stage):
            copy.wait()
        axis, size, final_at = self.plan()[stage]
        held, held_at = (self.source, self.source_at) if stage == 0 else (self.landings[stage - 1].at[0], 0)
        terms = [(held, held_at + axis.place * size)]
        terms += [(self.landings[stage].at[j - 1], 0) for j in range(1, axis.size)]
        if stage == len(self.order) - 1:
            add_rows(self.final, final_at, terms, size)
        else:
            add_rows(self.landings[stage].at[0], 0, terms, size)

    def gathers(self, which):
        stages = self.plan()
        sem = self.first_sem + sum(axis.size - 1 for axis, _, _ in stages)
        for name in self.back[:which]:
            sem += self.axes[name].size - 1
        depth = self.order.index(self.back[which])
        axis, size, at = stages[depth]
        block = self.final.at[span(at, size)]
        return [send(block, block, self.sems, sem + j - 1, axis.device(axis.ahead(j))) for j in range(1, axis.size)]

    def events(self):
        out = []
        count = len(self.order)

        def begin(copies):
            first = len(copies) // 2
            for copy in copies[first:] + copies[:first]:
                copy.start()

        for stage in range(count):
            def event(stage=stage):
                if stage > 0:
                    self.settle(stage - 1)
                begin(self.copies(stage))

            out.append(event)
        for which in range(len(self.back)):
            def event(which=which):
                if which == 0:
                    self.settle(count - 1)
                else:
                    for copy in self.gathers(which - 1):
                        copy.wait()
                begin(self.gathers(which))

            out.append(event)

        def last():
            for copy in self.gathers(len(self.back) - 1):
                copy.wait()

        out.append(last)
        return out


def landing_shapes(order, sizes, size, columns, dtype):
    shapes = []
    for name in order:
        size //= sizes[name]
        shapes.append(pltpu.VMEM((sizes[name] - 1, size, columns), dtype))
    return shapes


def copies_of(order, back, sizes):
    return sum(sizes[name] - 1 for name in order) + sum(sizes[name] - 1 for name in back)

GELU_A = math.sqrt(2.0 / math.pi)
GELU_B = 0.044715
TILE = 256
UNROLL = 4


def gelu_terms(pre):
    square = pre * pre
    swing = jnp.tanh(pre * (GELU_A + GELU_A * GELU_B * square))
    gate = 0.5 + 0.5 * swing
    steep = GELU_A + 3.0 * GELU_A * GELU_B * square
    return pre * gate, gate + 0.5 * pre * (1.0 - swing * swing) * steep


def norm_backward(grad_out, unit, scaling, gain):
    grad_unit = grad_out * gain
    return scaling * (
        grad_unit
        - jnp.mean(grad_unit, -1, keepdims=True)
        - unit * jnp.mean(grad_unit * unit, -1, keepdims=True)
    )


def column_sum(values):
    return jnp.sum(values, 0, keepdims=True)


def ffn_kernel(
    res_ref, cot_hbm, ctx_hbm, wo_hbm, gain1_ref, shift1_ref, gain2_ref, shift2_ref, bd_ref, bu_ref, wu_ref, wd_ref,
    out_ref, dproj_ref, dctx_ref, gwo_ref, pu_ref, pd_ref, small_ref,
    low_ref, acc_ref, hid_ref, slope_ref, dffn_ref, dpre_ref, sendu_ref, sendd_ref, recvu_ref, recvd_ref, pdown_ref, yland_ref,
    send_sem, recv_sem, cot_ref, ctx_ref, wo_ref, load_sem,
):
    parts = pl.num_programs(0) // 2
    step = pl.program_id(0)
    count, width = res_ref.shape
    share = dpre_ref.shape[1]
    tiles = count // TILE
    f = part_order(step, parts)
    late = jnp.maximum(step - parts, 0)
    heights = parts // CORES
    slot = late // CORES
    dp, tensor = lax.axis_index("dp"), lax.axis_index("tensor")
    height, core = tensor // CORES, lax.rem(tensor, CORES)
    mate = (dp, height * CORES + 1 - core)

    def up_to_mate(which):
        return send(sendu_ref.at[which], recvu_ref.at[which], (send_sem.at[0], recv_sem.at[0]), which, mate)

    def down_to_mate(which):
        return send(sendd_ref.at[which], recvd_ref.at[which], (send_sem.at[1], recv_sem.at[1]), which, mate)

    def to_height(which):
        there = (dp, lax.rem(height + 1 + which, heights) * CORES + core)
        return send(pdown_ref.at[which], yland_ref.at[which], (send_sem.at[2], recv_sem.at[2]), which, there)

    def down_part(late):
        part = part_order(parts + late, parts)
        piece = math.gcd(TILE, share)
        for start in range(0, share, piece):
            cut = slice(start, start + piece)
            yield cut, dot_tn(hid_ref[part, :, cut], dffn_ref[...]).astype(BF16)

    def ready(which):
        down_to_mate(which).wait()
        add_rows(pdown_ref.at[which], 0, [(pdown_ref.at[which], 0), (recvd_ref.at[which], 0)], share)
        if which < heights - 1:
            to_height(which).start()

    loads = [
        pltpu.make_async_copy(source, target, load_sem.at[i])
        for i, (source, target) in enumerate(((cot_hbm, cot_ref), (ctx_hbm, ctx_ref), (wo_hbm, wo_ref)))
    ]

    @pl.when(step == 0)
    def _():
        for load in loads:
            load.start()
        barrier = pltpu.get_barrier_semaphore()
        peers = [mate] + [(dp, lax.rem(height + j, heights) * CORES + core) for j in range(1, heights)]
        for peer in peers:
            pl.semaphore_signal(barrier, inc=1, device_id=peer, device_id_type=pl.DeviceIdType.MESH)
        pl.semaphore_wait(barrier, len(peers))

    def put_row(row, values):
        for i in range(values.shape[1] // PAIR):
            small_ref[pl.ds(row + i, 1)] = values[:, i * PAIR : (i + 1) * PAIR]

    def at(t):
        return pl.ds(pl.multiple_of(t * TILE, TILE), TILE)

    @pl.when(step == 0)
    def _():
        def one(t, carry):
            unit, _ = norm_stats(res_ref[at(t)])
            low_ref[at(t)] = (unit * gain1_ref[...][None, :] + shift1_ref[...][None, :]).astype(BF16)
            acc_ref[at(t)] = jnp.zeros((TILE, width), F32)
            return carry

        lax.fori_loop(0, tiles, one, 0, unroll=UNROLL)

    @pl.when(step < parts)
    def _():
        def one(t, carry):
            pre = dot_nn(low_ref[at(t)], wu_ref[0]) + bu_ref[0].astype(F32)
            hidden, slope = gelu_terms(pre)
            hidden = hidden.astype(BF16)
            hid_ref[f, at(t)] = hidden
            slope_ref[f, at(t)] = slope.astype(BF16)
            acc_ref[at(t)] += dot_nn(hidden, wd_ref[0])
            return carry

        lax.fori_loop(0, tiles, one, 0, unroll=UNROLL)

    @pl.when(step == parts)
    def _():
        loads[0].wait()

        def one(t, sums):
            unit, _ = norm_stats(res_ref[at(t)])
            first = unit * gain1_ref[...][None, :] + shift1_ref[...][None, :]
            unit, scaling = norm_stats(first + acc_ref[at(t)] + bd_ref[...][None, :])
            out_ref[at(t)] = (unit * gain2_ref[...][None, :] + shift2_ref[...][None, :]).astype(BF16)
            grad = cot_ref[at(t)].astype(F32)
            d_res = norm_backward(grad, unit, scaling, gain2_ref[...][None, :])
            d_ffn = d_res.astype(BF16)
            acc_ref[at(t)] = d_res
            dffn_ref[at(t)] = d_ffn
            return (
                sums[0] + column_sum(grad * unit),
                sums[1] + column_sum(grad),
                sums[2] + column_sum(d_ffn.astype(F32)),
            )

        zero = jnp.zeros((1, width), F32)
        sums = lax.fori_loop(0, tiles, one, (zero, zero, zero), unroll=UNROLL)
        small_ref[...] = jnp.zeros_like(small_ref)
        for i, values in enumerate(sums):
            put_row(i * (width // PAIR), values)

        def theirs(which, carry):
            for cut, values in down_part(CORES * which):
                sendd_ref[which, cut] = values
            down_to_mate(which).start()
            return carry

        def ours(which, carry):
            for cut, values in down_part(CORES * which + 1):
                pdown_ref[which, cut] = values
            return carry

        for which in range(heights):
            theirs(which, 0)
            if which > 0:
                ready(which - 1)
            ours(which, 0)

    @pl.when(step >= parts)
    def _():
        def one(t, total):
            d_hidden = dot_nt(dffn_ref[at(t)], wd_ref[0])
            d_pre = (d_hidden * slope_ref[f, at(t)].astype(F32)).astype(BF16)
            dpre_ref[at(t)] = d_pre
            acc_ref[at(t)] += dot_nt(d_pre, wu_ref[0])
            return total + column_sum(d_pre.astype(F32))

        bias = lax.fori_loop(0, tiles, one, jnp.zeros((1, share), F32), unroll=UNROLL)
        put_row(6 * (width // PAIR) + f * (share // PAIR), bias)

        @pl.when(late == 0)
        def _():
            ready(heights - 1)

        @pl.when(lax.rem(late, CORES) == 0)
        def _():
            for start in range(0, width, TILE):
                cut = slice(start, start + TILE)
                sendu_ref[slot, cut] = dot_tn(low_ref[:, cut], dpre_ref[...]).astype(BF16)
            up_to_mate(slot).start()

        @pl.when(lax.rem(late, CORES) == 1)
        def _():
            up_to_mate(slot).wait()
            for start in range(0, width, TILE):
                cut = slice(start, start + TILE)
                values = dot_tn(low_ref[:, cut], dpre_ref[...])
                pu_ref[slot, cut] = (values + recvu_ref[slot, cut].astype(F32)).astype(BF16)

    @pl.when(step == 2 * parts - 1)
    def _():
        loads[1].wait()
        loads[2].wait()

        def one(t, sums):
            unit, scaling = norm_stats(res_ref[at(t)])
            grad = acc_ref[at(t)]
            d_proj = norm_backward(grad, unit, scaling, gain1_ref[...][None, :]).astype(BF16)
            dproj_ref[at(t)] = d_proj
            dctx_ref[at(t)] = dot_nt(d_proj, wo_ref[...]).astype(BF16)
            return (
                sums[0] + column_sum(grad * unit),
                sums[1] + column_sum(grad),
                sums[2] + column_sum(d_proj.astype(F32)),
            )

        zero = jnp.zeros((1, width), F32)
        sums = lax.fori_loop(0, tiles, one, (zero, zero, zero), unroll=UNROLL)
        for i, values in enumerate(sums):
            put_row((3 + i) * (width // PAIR), values)
        for start in range(0, width, TILE):
            values = dot_tn(ctx_ref[:, start : start + TILE], dproj_ref[...]).astype(BF16)
            gwo_ref[start : start + TILE] = values[:, : width // 2]
            gwo_ref[width + start : width + start + TILE] = values[:, width // 2 :]
        for which in range(heights - 1):
            to_height(which).wait()
        terms = [(pdown_ref.at[heights - 1], 0)] + [(yland_ref.at[which], 0) for which in range(heights - 1)]
        add_rows(pd_ref, 0, terms, share)


def part_order(step, parts):
    tensor = lax.axis_index("tensor")
    height, core = tensor // CORES, lax.rem(tensor, CORES)
    late = jnp.maximum(step - parts, 0)
    there = lax.rem(height + 1 + late // CORES, parts // CORES)
    whose = jnp.where(lax.rem(late, CORES) == 0, 1 - core, core)
    return jnp.where(step < parts, step, there * CORES + whose)


def feed_forward(res, cot, ctx, w_out, gain1, shift1, gain2, shift2, b_down, b_up, w_up, w_down):
    count, width = res.shape
    parts, _, share = w_up.shape
    heights = parts // 2
    smalls = 6 * width // PAIR + parts * share // PAIR
    smalls = -(-smalls // 8) * 8

    def whole(*shape):
        return pl.BlockSpec(shape, lambda s: (0,) * len(shape), pipeline_mode=pl.Buffered(1))

    def per_part(*shape):
        return pl.BlockSpec((1,) + shape, lambda s: (part_order(s, parts),) + (0,) * len(shape))

    act = jax.ShapeDtypeStruct((count, width), BF16)
    return pl.pallas_call(
        ffn_kernel,
        grid=(2 * parts,),
        in_specs=[whole(count, width)]
        + [pl.BlockSpec(memory_space=pl.ANY)] * 3
        + [whole(width)] * 5
        + [per_part(1, share), per_part(width, share), per_part(share, width)],
        out_specs=[whole(count, width)] * 3
        + [whole(2 * width, width // 2), whole(heights, width, share), whole(share, width), whole(smalls, PAIR)],
        out_shape=[act] * 3
        + [
            jax.ShapeDtypeStruct((2 * width, width // 2), BF16),
            jax.ShapeDtypeStruct((heights, width, share), BF16),
            jax.ShapeDtypeStruct((share, width), BF16),
            jax.ShapeDtypeStruct((smalls, PAIR), F32),
        ],
        scratch_shapes=[
            pltpu.VMEM((count, width), BF16),
            pltpu.VMEM((count, width), F32),
            pltpu.VMEM((parts, count, share), BF16),
            pltpu.VMEM((parts, count, share), BF16),
            pltpu.VMEM((count, width), BF16),
            pltpu.VMEM((count, share), BF16),
            pltpu.VMEM((heights, width, share), BF16),
            pltpu.VMEM((heights, share, width), BF16),
            pltpu.VMEM((heights, width, share), BF16),
            pltpu.VMEM((heights, share, width), BF16),
            pltpu.VMEM((heights, share, width), BF16),
            pltpu.VMEM((heights - 1, share, width), BF16),
            pltpu.SemaphoreType.DMA((3, heights)),
            pltpu.SemaphoreType.DMA((3, heights)),
            pltpu.VMEM((count, width), BF16),
            pltpu.VMEM((count, width), BF16),
            pltpu.VMEM((width, width), BF16),
            pltpu.SemaphoreType.DMA((3,)),
        ],
        compiler_params=pltpu.CompilerParams(vmem_limit_bytes=60 * 2**20, collective_id=0, has_side_effects=True),
        name="feed_forward",
    )(res, cot, ctx, w_out, gain1, shift1, gain2, shift2, b_down, b_up, w_up, w_down)


def attend_back_kernel(
    dctx_ref, att_ref, inv_ref, q_ref, k_ref, v_ref, sq_ref, sk_ref, w_ref, s_ref, x_ref, seg_ref,
    wqkv_hbm, kernel_ref, dproj_ref, gwo_ref, pu_ref, pd_ref, small_ref,
    gt_ref, all_out, up_out, down_out, few_out,
    near_ref, vv_ref, dpad_ref, dcos_ref, dq_ref, dk_ref, dv_ref, joined_ref, gwacc_ref, conv_ref,
    gwlow_ref, gb_ref, flip_ref, mini_ref, all_ref, up_ref, down_ref, few_ref, out_sem, wqkv_ref, load_sem, *links,
    plan, quads, seqs,
):
    quad, row = pl.program_id(0), pl.program_id(1)
    length = x_ref.shape[0]
    blocks = length // BLK
    inside = slice(HALO, HALO + length)

    _, sizes, dp_size, tensor_size = plan
    axes = slice_axes(dp_size, tensor_size)
    ticks = schedule(axes, sizes, quads, seqs, gwo_ref, pu_ref, pd_ref, gwlow_ref, mini_ref, all_ref, up_ref, down_ref, few_ref, links,
        (all_out, up_out, down_out, few_out, out_sem))
    calls = quads * seqs * (QUAD // HEAD)

    build_near(*segment_rows(seg_ref, row), near_ref)
    for half in range(2):
        edge = jnp.zeros((HALO, PAIR), BF16)
        for ref in (vv_ref, dpad_ref):
            ref[half, :HALO, :PAIR] = edge
            ref[half, HALO + length :, :PAIR] = edge
        vv_ref[half, inside, PAIR:] = head_mask(half, (length, PAIR))

    @pl.when(row == 0)
    def _():
        conv_ref[...] = jnp.zeros_like(conv_ref)
        gwacc_ref[...] = jnp.zeros_like(gwacc_ref)

    load = pltpu.make_async_copy(wqkv_hbm, wqkv_ref, load_sem)

    @pl.when((quad == 0) & (row == 0))
    def _():
        load.start()
        gb_ref[...] = jnp.zeros_like(gb_ref)
        flip_ref[...] = place_taps(kernel_ref[...], True)
        mini_ref[...] = jnp.zeros_like(mini_ref)
        mini_ref[: small_ref.shape[0]] = small_ref[...]
        filled = 2 * gwacc_ref.shape[0]
        if gwlow_ref.shape[1] > filled:
            gwlow_ref[:, filled:] = jnp.zeros((quads, gwlow_ref.shape[1] - filled, gwlow_ref.shape[2]), BF16)

    def one_pair(pair, carry):
        at = pl.ds(pl.multiple_of(pair * PAIR, PAIR), PAIR)
        inverse = inv_ref[:, at].astype(F32)
        d_ctx = dctx_ref[:, at]
        d_summed = (d_ctx.astype(F32) * inverse).astype(BF16)
        d_total = (-d_summed.astype(F32) * att_ref[:, at].astype(F32)).astype(BF16)
        both = jnp.concatenate([d_summed, d_total], 1)
        dk = jnp.zeros((PAIR, length), F32)
        dv = jnp.zeros((PAIR, length), F32)
        turn = (quad * seqs + row) * (QUAD // PAIR) + pair
        for half in range(2):
            for when in range(half, calls, 2):
                if ticks.get(when):

                    @pl.when(turn == when // 2)
                    def _(when=when):
                        for event in ticks[when]:
                            event()

            head = pair * 2 + half
            mask = head_mask(half, (length, PAIR))
            vv_ref[half, inside, :PAIR] = v_ref[:, at] * mask
            dpad_ref[half, inside] = d_ctx * mask
            k_half = k_ref[:, at] * mask
            for block in range(blocks):
                here = slice(block * BLK, block * BLK + BLK)
                low, high = window_of(block, blocks)
                d_weight = dot_nt(both[here], vv_ref[half, HALO + low : HALO + high])
                d_cos = d_weight.astype(BF16) * s_ref[0, head, here, low:high]
                dcos_ref[here, low:high] = d_cos
                if low > 0:
                    dcos_ref[here, :low] = jnp.zeros((BLK, low), BF16)
                if high < length:
                    dcos_ref[here, high:] = jnp.zeros((BLK, length - high), BF16)
                grown = dot_nn(d_cos, k_half[low:high])
                if half == 0:
                    dq_ref[here] = grown
                else:
                    dq_ref[here] += grown
                window = slice(block * BLK, block * BLK + 2 * BLK)
                near = near_ref[block]
                taps = band(flip_ref[pl.ds(quad * (QUAD // HEAD) + head, 1)], BLK).astype(BF16) * near
                grown = dot_nn(taps, dpad_ref[half, window])
                if half == 0:
                    dv_ref[here] = grown
                else:
                    dv_ref[here] += grown
                conv_ref[head] += near.astype(F32) * dot_nt(d_ctx[here], vv_ref[half, window, :PAIR])
            dk += dot_tn(q_ref[:, at] * mask, dcos_ref[...])
            dv += dot_tn(d_summed * mask, w_ref[0, head])
        dv_ref[...] += dv.T
        grad = SLOPE * dq_ref[...]
        unit = q_ref[:, at].astype(F32)
        d_query = sq_ref[:, at].astype(F32) * (SHRINK * grad - unit * (head_sum(grad * unit) / SHRINK))
        grad = SLOPE * dk.T
        unit = k_ref[:, at].astype(F32)
        d_key = sk_ref[:, at].astype(F32) * (grad - unit * head_sum(grad * unit))
        for part, values in enumerate((d_query, d_key, dv_ref[...])):
            joined_ref[quad, row, :, pl.ds(pl.multiple_of(part * QUAD + pair * PAIR, PAIR), PAIR)] = values.astype(BF16)
        return carry

    lax.fori_loop(0, QUAD // PAIR, one_pair, 0)

    gb_ref[quad, :1] += column_sum(joined_ref[quad, row].astype(F32))
    width = gwacc_ref.shape[0]
    for start in range(0, width, TILE):
        cut = slice(start, start + TILE)
        gwacc_ref[cut] += dot_tn(x_ref[:, cut], joined_ref[quad, row])

    @pl.when(row == seqs - 1)
    def _():
        half = gwacc_ref.shape[1] // 2
        for start in range(0, width, TILE):
            for side in range(2):
                values = gwacc_ref[start : start + TILE, side * half : (side + 1) * half]
                gwlow_ref[quad, side * width + start : side * width + start + TILE] = values.astype(BF16)
        base = small_ref.shape[0]
        lines = gb_ref.shape[2] // PAIR
        for i in range(lines):
            mini_ref[pl.ds(base + quad * lines + i, 1)] = gb_ref[quad, :1, i * PAIR : (i + 1) * PAIR]
        base += quads * lines
        for head in range(QUAD // HEAD):
            sums = conv_ref[head]
            high = sums.astype(BF16)
            turn = (rows((BLK, BLK)) + lanes((BLK, BLK)) == BLK - 1).astype(BF16)
            turned = dot_nn(turn, high) + dot_nn(turn, (sums - high.astype(F32)).astype(BF16))
            turned = pltpu.roll(turned, BLK, 1, stride=1, stride_axis=0)
            mini_ref[pl.ds(base + quad * (QUAD // HEAD) + head, 1)] = column_sum(turned)[:, :PAIR]

    last = (quad == quads - 1) & (row == seqs - 1)

    @pl.when(last)
    def _():
        for event in ticks.get(calls, ()):
            event()

    @pl.when((quad == quads - 1) & (row == 0))
    def _():
        load.wait()

    @pl.when(quad == quads - 1)
    def _():
        for start in range(0, length, TILE):
            cut = slice(start, start + TILE)
            grown = dproj_ref[cut].astype(F32)
            for q in range(quads):
                for part in range(3):
                    to = part * width + q * QUAD
                    grown += dot_nt(joined_ref[q, row, cut, part * QUAD : (part + 1) * QUAD], wqkv_ref[:, to : to + QUAD])
            gt_ref[cut] = grown.astype(BF16)

    @pl.when(last)
    def _():
        for when in sorted(ticks):
            if when > calls:
                for event in ticks[when]:
                    event()


FFN_PLAN = (
    (
        (("x", "z"), (4, 9, 15, 24, 54)),
        (("z", "x"), (3, 27, 30, 50, 59)),
    ),
    (
        (("x", "z"), (0, 8, 15, 21, 34, 43)),
        (("x", "z"), (7, 19, 23, 29, 38, 56)),
    ),
)
ALL_PLAN = (
    (
        (3, 1, (2, 4, 11, 13, 16, 29, 35, 45, 55)),
    ),
    (
        (3, 0, (10, 11, 17, 26, 31, 41, 47, 52, 59)),
    ),
    (
        (3, 0, (19, 21, 28, 37, 42, 48, 51, 57, 60)),
    ),
    (
        (3, 1, (24, 25, 32, 36, 39, 44, 48, 55, 58)),
    ),
)
MINI_ORDER = 1
MINI_TIMES = (25, 27, 33, 40, 46, 49, 52, 53, 55)
FFN_ROWS = 384
ORDERS = (("core", "x", "y", "z"), ("core", "y", "x", "z"))


def all_parts(index, size, devices):
    parts = ALL_PLAN[index]
    if sum(units for units, _, _ in parts) * 16 * devices != size:
        parts = ((size // (16 * devices), parts[-1][1], parts[-1][2]),)
    out, start = [], 0
    for units, order, times in parts:
        rows_of = units * 16 * devices
        out.append((start, rows_of, ORDERS[order], times))
        start += rows_of
    return out


class FfnReduction(Reduction):
    def copies(self, stage):
        if stage > 0:
            return super().copies(stage)
        axis = self.axes["y"]
        return [
            send(
                self.source.at[j - 1, span(self.source_at, self.size)], self.landings[0].at[j - 1],
                self.sems, self.first_sem + j - 1, axis.device(axis.ahead(j)),
            )
            for j in range(1, axis.size)
        ]

    def plan(self):
        size, at = self.size, self.final_at
        out = [(self.axes["y"], size, at)]
        for name in self.order[1:]:
            axis = self.axes[name]
            size //= axis.size
            at = at + axis.place * size
            out.append((axis, size, at))
        return out

    def settle(self, stage):
        if stage > 0:
            return super().settle(stage)
        axis = self.axes["y"]
        for copy in self.copies(0):
            copy.wait()
        terms = [(self.source.at[axis.size - 1], self.source_at)]
        terms += [(self.landings[0].at[j - 1], 0) for j in range(1, axis.size)]
        add_rows(self.landings[0].at[0], 0, terms, self.size)


def link_plan(sizes, width, share, quads):
    out = []
    devices = math.prod(sizes.values())
    y = sizes["y"]
    for late, (height, columns) in enumerate(((share, width), (width, share))):
        for start in range(0, height, FFN_ROWS):
            order = FFN_PLAN[late][start // FFN_ROWS][0]
            shapes = [pltpu.VMEM((y - 1, FFN_ROWS, columns), BF16)] if late else []
            shapes += landing_shapes(order, sizes, FFN_ROWS, columns, BF16)
            out.append((shapes, copies_of((("y",) if late else ()) + order, order, sizes)))
    size = padded(2 * width, devices)
    for index in range(quads + 1):
        for _, rows_of, order, _ in all_parts(index, size, devices):
            out.append((landing_shapes(order, sizes, rows_of, width // 2, BF16), copies_of(order, order, sizes)))
    order = ORDERS[MINI_ORDER]
    out.append((landing_shapes(order, sizes, 8 * devices, PAIR, F32), copies_of(order, order, sizes)))
    return out


def padded(size, devices):
    return -(-size // (16 * devices)) * 16 * devices


def schedule(axes, sizes, quads, seqs, gwo_ref, pu_ref, pd_ref, gwlow_ref, mini_ref, all_ref, up_ref, down_ref, few_ref, links, outs):
    all_out, up_out, down_out, few_out, out_sem = outs
    calls = quads * seqs * (QUAD // HEAD)
    share, width = pd_ref.shape
    devices = math.prod(sizes.values())
    groups = link_plan(sizes, width, share, quads)
    taken, position = [], 0
    for shapes, _ in groups:
        taken.append((links[position : position + len(shapes)], links[position + len(shapes) : position + len(shapes) + 2]))
        position += len(shapes) + 2
    ticks = {0: [lambda: greet(axes)]}

    stores = []

    def enlist(reduction, times, done, place):
        for time, event in zip(times, reduction.events(), strict=True):
            ticks.setdefault(time, []).append(event)
        store = pltpu.make_async_copy(done, place, out_sem.at[len(stores)])
        ticks[times[-1]].append(store.start)
        stores.append(store)

    number = 0
    for late, (source, final, place) in enumerate(((pd_ref, down_ref, down_out), (pu_ref, up_ref, up_out))):
        for start in range(0, final.shape[0], FFN_ROWS):
            landings, sems = taken[number]
            block = span(start, FFN_ROWS)
            order, times = FFN_PLAN[late][start // FFN_ROWS]
            kind = FfnReduction if late else Reduction
            whole_order = ("y",) + order if late else order
            reduction = kind(axes, whole_order, order[::-1], source, start, FFN_ROWS, final, start, landings, sems)
            enlist(reduction, times, final.at[block], place.at[block])
            number += 1
    size = padded(2 * width, devices)
    for index in range(quads + 1):
        source = gwo_ref if index == 0 else gwlow_ref.at[index - 1]
        for start, rows_of, order, times in all_parts(index, size, devices):
            landings, sems = taken[number]
            final = all_ref.at[index]
            reduction = Reduction(axes, order, order[::-1], source, start, rows_of, final, start, landings, sems)
            enlist(reduction, times, final.at[span(start, rows_of)], all_out.at[index, span(start, rows_of)])
            number += 1
    landings, sems = taken[number]
    order = ORDERS[MINI_ORDER]
    reduction = Reduction(axes, order, order[::-1], mini_ref, 0, 8 * devices, few_ref, 0, landings, sems)
    enlist(reduction, MINI_TIMES, few_ref, few_out)
    ticks[max(ticks) + 1] = [store.wait for store in stores]
    return ticks


def attend_back(dctx, att, inv, q, k, v, sq, sk, weight, slope, tokens, segment_ids, w_qkv, kernel, dproj, gwo, pu, pd, small, dp_size, tensor_size):
    count, width = tokens.shape
    seqs, length = segment_ids.shape
    quads = width // QUAD
    per = QUAD // HEAD
    blocks = length // BLK
    own = pl.BlockSpec((length, QUAD), lambda p, r: (r, p))
    big = pl.BlockSpec((1, per, length, length), lambda p, r: (r, p, 0, 0))
    wide = pl.BlockSpec((length, width), lambda p, r: (r, 0))

    sizes = {"core": CORES, "y": tensor_size // CORES, "x": dp_size // DEPTH, "z": DEPTH}
    devices = dp_size * tensor_size
    share = pd.shape[0]
    grown = padded(2 * width, devices)
    gwo = jnp.pad(gwo, ((0, grown - gwo.shape[0]), (0, 0)))
    minis = 8 * devices
    scratch = []
    for shapes, count_of in link_plan(sizes, width, share, quads):
        scratch += shapes + [pltpu.SemaphoreType.DMA((count_of,)), pltpu.SemaphoreType.DMA((count_of,))]

    def whole(*shape):
        return pl.BlockSpec(shape, lambda p, r: (0,) * len(shape), pipeline_mode=pl.Buffered(1))

    return pl.pallas_call(
        functools.partial(attend_back_kernel, plan=(None, sizes, dp_size, tensor_size), quads=quads, seqs=seqs),
        grid=(quads, seqs),
        in_specs=[own] * 8
        + [big] * 2
        + [
            wide,
            whole(*segment_ids.shape),
            pl.BlockSpec(memory_space=pl.ANY),
            whole(*kernel.shape),
            wide,
            whole(*gwo.shape), whole(*pu.shape), whole(*pd.shape), whole(*small.shape),
        ],
        out_specs=[
            pl.BlockSpec((length, width), lambda p, r: (jnp.where(p == quads - 1, r, 0), 0)),
        ]
        + [pl.BlockSpec(memory_space=pl.ANY)] * 4,
        out_shape=[
            jax.ShapeDtypeStruct((count, width), BF16),
            jax.ShapeDtypeStruct((quads + 1, grown, width // 2), BF16),
            jax.ShapeDtypeStruct((width, share), BF16),
            jax.ShapeDtypeStruct((share, width), BF16),
            jax.ShapeDtypeStruct((minis, PAIR), F32),
        ],
        scratch_shapes=[
            pltpu.VMEM((blocks, BLK, 2 * BLK), BF16),
            pltpu.VMEM((2, length + 2 * HALO, 2 * PAIR), BF16),
            pltpu.VMEM((2, length + 2 * HALO, PAIR), BF16),
            pltpu.VMEM((length, length), BF16),
            pltpu.VMEM((length, PAIR), F32),
            pltpu.VMEM((length, PAIR), F32),
            pltpu.VMEM((length, PAIR), F32),
            pltpu.VMEM((quads, seqs, length, 3 * QUAD), BF16),
            pltpu.VMEM((width, 3 * QUAD), F32),
            pltpu.VMEM((per, BLK, 2 * BLK), F32),
            pltpu.VMEM((quads, grown, width // 2), BF16),
            pltpu.VMEM((quads, 8, 3 * QUAD), F32),
            pltpu.VMEM((width // HEAD, 2 * BLK), F32),
            pltpu.VMEM((minis, PAIR), F32),
            pltpu.VMEM((quads + 1, grown, width // 2), BF16),
            pltpu.VMEM((width, share), BF16),
            pltpu.VMEM((share, width), BF16),
            pltpu.VMEM((minis, PAIR), F32),
            pltpu.SemaphoreType.DMA((len(link_plan(sizes, width, share, quads)),)),
            pltpu.VMEM((width, 3 * width), BF16),
            pltpu.SemaphoreType.DMA,
        ]
        + scratch,
        compiler_params=pltpu.CompilerParams(vmem_limit_bytes=60 * 2**20, collective_id=1, has_side_effects=True),
        name="attend_backward",
    )(dctx, att, inv, q, k, v, sq, sk, weight, slope, tokens, segment_ids, w_qkv, kernel, dproj, gwo, pu, pd, small)


def spread_kernel(low_ref, high_ref, up_ref, down_ref, few_ref, a_ref, b_ref, gw_ref, gwo_ref, gup_ref, gdown_ref, a_out, b_out, *vectors, first_lane, base):
    width = gwo_ref.shape[1]
    half = width // 2
    quads = low_ref.shape[0] - 1
    gwo_ref[:, :half] = low_ref[0].astype(F32)
    gwo_ref[:, half:] = high_ref[0].astype(F32)
    for quad in range(quads):
        for part in range(3):
            for start in range(part * QUAD, (part + 1) * QUAD, PAIR):
                side, lane = (low_ref, start) if start < half else (high_ref, start - half)
                to = part * width + quad * QUAD + start - part * QUAD
                gw_ref[:, to : to + PAIR] = side[1 + quad, :, lane : lane + PAIR].astype(F32)
    a_out[...] = a_ref[...]
    b_out[...] = b_ref[...]
    gup_ref[...] = up_ref[...].astype(F32)
    gdown_ref[...] = down_ref[...].astype(F32)

    @pl.when(pl.program_id(0) == 0)
    def _():
        gb_ref, conv_ref, *six, gbu_ref = vectors
        lines = width // PAIR

        def copy_line(target, to, line):
            target[to * PAIR : (to + 1) * PAIR] = few_ref[line]

        for number, target in enumerate(six):
            for i in range(lines):
                copy_line(target, i, number * lines + i)
        share = gbu_ref.shape[0] // PAIR
        mine = lax.axis_index("tensor") * share
        for i in range(share):
            copy_line(gbu_ref, i, 6 * lines + mine + i)
        per = QUAD // PAIR
        for quad in range(quads):
            for part in range(3):
                for i in range(per):
                    copy_line(gb_ref, (part * width + quad * QUAD) // PAIR + i, base + (quad * 3 + part) * per + i)
        heads, taps = conv_ref.shape
        kept = few_ref[base + 3 * lines : base + 3 * lines + heads]
        conv_ref[...] = pltpu.roll(kept, PAIR - first_lane, 1)[:, :taps]


def spread_out(grads, up, down, few, out, gt, width, heads, taps, first_lane, base):
    chunks = grads.shape[0]
    quads = chunks - 1
    steps = 8
    rows_of = width // steps
    share = up.shape[1]
    down_rows = share // steps

    def whole(*shape):
        return pl.BlockSpec(shape, lambda s: (0,) * len(shape))

    def by_rows(count, columns):
        return pl.BlockSpec((count, columns), lambda s: (s, 0))

    row = jax.ShapeDtypeStruct((width,), F32)
    return pl.pallas_call(
        functools.partial(spread_kernel, first_lane=first_lane, base=base),
        grid=(steps,),
        in_specs=[
            pl.BlockSpec((chunks, rows_of, width // 2), lambda s: (0, s, 0)),
            pl.BlockSpec((chunks, rows_of, width // 2), lambda s: (0, steps + s, 0)),
            by_rows(rows_of, share),
            by_rows(down_rows, width),
            whole(*few.shape),
            by_rows(out.shape[0] // steps, width), by_rows(out.shape[0] // steps, width),
        ],
        out_specs=[
            by_rows(rows_of, 3 * width), by_rows(rows_of, width), by_rows(rows_of, share), by_rows(down_rows, width),
            by_rows(out.shape[0] // steps, width), by_rows(out.shape[0] // steps, width),
            whole(3 * width), whole(heads, taps),
        ]
        + [whole(width)] * 6
        + [whole(share)],
        out_shape=[
            jax.ShapeDtypeStruct((width, 3 * width), F32),
            jax.ShapeDtypeStruct((width, width), F32),
            jax.ShapeDtypeStruct((width, share), F32),
            jax.ShapeDtypeStruct((share, width), F32),
            jax.ShapeDtypeStruct(out.shape, out.dtype),
            jax.ShapeDtypeStruct(gt.shape, gt.dtype),
            jax.ShapeDtypeStruct((3 * width,), F32),
            jax.ShapeDtypeStruct((heads, taps), F32),
        ]
        + [row] * 6
        + [jax.ShapeDtypeStruct((share,), F32)],
        compiler_params=pltpu.CompilerParams(vmem_limit_bytes=60 * 2**20),
        name="spread_out",
    )(grads, grads, up, down, few, out, gt)


def body(
    tokens, segment_ids, w_qkv, b_qkv, conv_kernel, w_out, b_out, norm1_gain, norm1_bias,
    w_up, b_up, w_down, b_down, norm2_gain, norm2_bias, cotangent,
):
    width = tokens.shape[1]
    heads, taps = conv_kernel.shape
    dp_size, tensor_size = lax.axis_size("dp"), lax.axis_size("tensor")
    q, k, v, sq, sk, weight, slope, att, inv, ctx, res, up_all, down_all, bias_all = attend(
        tokens, segment_ids, w_qkv, b_qkv, conv_kernel, w_out, b_out, w_up, w_down, b_up, dp_size, tensor_size
    )
    out, dproj, dctx, gwo, pu, pd, small = feed_forward(
        res, cotangent, ctx, w_out, norm1_gain, norm1_bias, norm2_gain, norm2_bias, b_down, bias_all, up_all, down_all
    )
    gt, grads, grad_up, grad_down, few = attend_back(
        dctx, att, inv, q, k, v, sq, sk, weight, slope, tokens, segment_ids, w_qkv, conv_kernel, dproj,
        gwo, pu, pd, small, dp_size, tensor_size,
    )
    first_lane = (HALO - taps // 2 + BLK - 1 + BLK) % (2 * BLK)
    gw, gwo, grad_up, grad_down, out, gt, gb, grad_conv, gg2, gs2, gbd, gg1, gs1, gbo, gbu = spread_out(
        grads, grad_up, grad_down, few, out, gt, width, heads, taps, first_lane, small.shape[0]
    )
    return (out, gt, gw, gb, grad_conv, gwo, gbo, gg1, gs1, grad_up, gbu, grad_down, gbd, gg2, gs2)


def solution(mesh):
    placed = (
        P(("dp", "tensor"), None),
        P(("dp", "tensor"), None),
        P(), P(), P(), P(), P(), P(), P(),
        P(None, "tensor"),
        P("tensor"),
        P("tensor", None),
        P(), P(), P(),
        P(("dp", "tensor"), None),
    )
    return jax.shard_map(
        body,
        mesh=mesh,
        in_specs=placed,
        out_specs=(
            P(("dp", "tensor"), None),
            P(("dp", "tensor"), None),
            P(), P(), P(), P(), P(), P(), P(),
            P(None, "tensor"),
            P("tensor"),
            P("tensor", None),
            P(), P(), P(),
        ),
        check_vma=False,
    )
```

```python
import functools
import math

import jax
import jax.numpy as jnp
from jax import lax
from jax.experimental import pallas as pl
from jax.experimental.pallas import tpu as pltpu
from jax.sharding import PartitionSpec as P

F32 = jnp.float32
BF16 = jnp.bfloat16
EPS_NORM = 1e-5
EPS_UNIT = 1e-6
SHRINK = 0.95
TAU = 8
SLOPE = TAU / math.pi
ARC = (0.49999996, -0.06830509, 0.02825875, -0.01557005, 0.00864352, -0.00363107, 0.00076235)
QUAD = 256
PAIR = 128
HEAD = 64
BLK = 128
HALO = 64


def dot_nn(a, b):
    return lax.dot_general(a, b, (((1,), (0,)), ((), ())), preferred_element_type=F32)


def dot_nt(a, b):
    return lax.dot_general(a, b, (((1,), (1,)), ((), ())), preferred_element_type=F32)


def dot_tn(a, b):
    return lax.dot_general(a, b, (((0,), (0,)), ((), ())), preferred_element_type=F32)


def lanes(shape):
    return lax.broadcasted_iota(jnp.int32, shape, len(shape) - 1)


def rows(shape):
    return lax.broadcasted_iota(jnp.int32, shape, len(shape) - 2)


def head_sum(values):
    width = values.shape[-1]
    ones = (rows((width, width)) // HEAD == lanes((width, width)) // HEAD).astype(BF16)
    high = values.astype(BF16)
    low = (values - high.astype(F32)).astype(BF16)
    return dot_nn(high, ones) + dot_nn(low, ones)


def closeness_terms(cosine):
    size = jnp.abs(cosine)
    room = 1.0 - size
    inverse = lax.rsqrt(room)
    poly = jnp.full_like(size, ARC[-1])
    for coefficient in ARC[-2::-1]:
        poly = poly * size + coefficient
    small = room * inverse * poly
    close = jnp.where(cosine >= 0.0, 1.0 - small, small)
    two = close * close
    four = two * two
    slope = (four * two) * (close * inverse) * lax.rsqrt(1.0 + size)
    return four * four, slope


def head_mask(half, shape):
    return (lanes(shape) // HEAD == half).astype(BF16)


def window_of(block, blocks):
    low = max(0, block * BLK - 256)
    high = min(blocks * BLK, block * BLK + BLK + 256)
    return low, high


def band(taps, count):
    spread = jnp.broadcast_to(taps, (count, taps.shape[1]))
    return pltpu.roll(spread, 0, 1, stride=1, stride_axis=0)


def norm_stats(values):
    centred = values - jnp.mean(values, -1, keepdims=True)
    scaling = lax.rsqrt(jnp.mean(centred * centred, -1, keepdims=True) + EPS_NORM)
    return centred * scaling, scaling


def segment_rows(seg_ref, row):
    ids = seg_ref[pl.ds(row, 1)].astype(F32)
    edge = jnp.full((1, HALO), -1.0, F32)
    return jnp.concatenate([edge, ids, edge], 1), jnp.broadcast_to(ids, (PAIR, ids.shape[1])).T[:, :1]


def build_same(seg_pad, seg_col, same_ref):
    length = seg_col.shape[0]
    for start in range(0, length, BLK):
        own = seg_col[start : start + BLK]
        same_ref[start : start + BLK, :] = jnp.where(
            own == seg_pad[:, HALO : HALO + length], 1.0, 0.0
        ).astype(BF16)


def build_near(seg_pad, seg_col, near_ref):
    length = seg_col.shape[0]
    for start in range(0, length, BLK):
        own = seg_col[start : start + BLK]
        near_ref[start // BLK] = jnp.where(
            own == seg_pad[:, start : start + 2 * BLK], 1.0, 0.0
        ).astype(BF16)


def place_taps(kernel, reverse):
    taps = kernel.shape[1]
    shape = (taps, 2 * BLK)
    tap = taps - 1 - rows(shape) if reverse else rows(shape)
    return dot_nn(kernel.astype(BF16), (lanes(shape) == tap + HALO - taps // 2).astype(BF16))


def attend_kernel(
    x_ref, seg_ref, wq_ref, wk_ref, wv_ref, b_ref, kernel_ref, wo_ref, bo_ref,
    wu_ref, wd_ref, bu_ref,
    q_ref, k_ref, v_ref, sq_ref, sk_ref, w_ref, s_ref, att_ref, inv_ref, ctx_ref, res_ref,
    up_ref, down_ref, bias_ref,
    same_ref, near_ref, vv_ref, tap_ref, mine_ref, send_sem, recv_sem, copy_sem,
    *, dp_size, tensor_size,
):
    row, quad = pl.program_id(0), pl.program_id(1)
    quads, seqs = pl.num_programs(1), pl.num_programs(0)
    ticks = gather_plan(dp_size, tensor_size, (wu_ref, wd_ref, mine_ref), (up_ref, down_ref, bias_ref), (send_sem, recv_sem), copy_sem)
    length = x_ref.shape[0]
    blocks = length // BLK

    @pl.when((row == 0) & (quad == 0))
    def _():
        tap_ref[...] = place_taps(kernel_ref[...], False)
        mine_ref[...] = bu_ref[...].astype(F32)[None, :]

    @pl.when(quad == 0)
    def _():
        seg_pad, seg_col = segment_rows(seg_ref, row)
        build_same(seg_pad, seg_col, same_ref)
        build_near(seg_pad, seg_col, near_ref)
        for half in range(2):
            edge = jnp.zeros((HALO, 2 * PAIR), BF16)
            vv_ref[half, :HALO] = edge
            vv_ref[half, HALO + length :] = edge
            vv_ref[half, HALO : HALO + length, PAIR:] = head_mask(half, (length, PAIR))

    def bias(part):
        start = pl.multiple_of(part * x_ref.shape[1] + quad * QUAD, QUAD)
        return b_ref[pl.ds(start, QUAD)][None, :]

    for start in range(0, length, ROWS):
        here = slice(start, start + ROWS)
        x = x_ref[here]
        for number, (w, unit, scale, factor) in enumerate(
            ((wq_ref, q_ref, sq_ref, SHRINK), (wk_ref, k_ref, sk_ref, 1.0))
        ):
            part = dot_nn(x, w[...]) + bias(number)
            scaling = lax.rsqrt(head_sum(part * part) + EPS_UNIT)
            unit[here] = (part * (scaling * factor)).astype(BF16)
            scale[here] = scaling.astype(BF16)
        v_ref[here] = (dot_nn(x, wv_ref[...]) + bias(2)).astype(BF16)

    def one_pair(pair, carry):
        turn = (row * quads + quad) * (QUAD // PAIR) + pair
        for when, events in ticks.items():

            @pl.when(turn == when)
            def _(events=events):
                for event in events:
                    event()

        at = pl.ds(pl.multiple_of(pair * PAIR, PAIR), PAIR)
        v = v_ref[:, at]
        for half in range(2):
            vv_ref[half, HALO : HALO + length, :PAIR] = v * head_mask(half, (length, PAIR))
        for block in range(blocks):
            here = slice(block * BLK, block * BLK + BLK)
            low, high = window_of(block, blocks)
            q = q_ref[here, at]
            total = jnp.zeros((BLK, 2 * PAIR), F32)
            near = jnp.zeros((BLK, PAIR), F32)
            for half in range(2):
                head = pair * 2 + half
                q_half = q * head_mask(half, (BLK, PAIR))
                for start in range(low, high, KCH):
                    stop = min(start + KCH, high)
                    cosine = dot_nt(q_half, k_ref[start:stop, at])
                    weight, slope = closeness_terms(cosine)
                    same = same_ref[here, start:stop]
                    weight = weight.astype(BF16) * same
                    w_ref[0, head, here, start:stop] = weight
                    s_ref[0, head, here, start:stop] = slope.astype(BF16) * same
                    total += dot_nn(weight, vv_ref[half, HALO + start : HALO + stop])
                if low > 0:
                    w_ref[0, head, here, :low] = jnp.zeros((BLK, low), BF16)
                if high < length:
                    w_ref[0, head, here, high:] = jnp.zeros((BLK, length - high), BF16)
                taps = band(tap_ref[pl.ds(quad * (QUAD // HEAD) + head, 1)], BLK).astype(BF16) * near_ref[block]
                near += dot_nn(taps, vv_ref[half, block * BLK : block * BLK + 2 * BLK, :PAIR])
            inverse = 1.0 / (1.0 + total[:, PAIR:])
            attended = total[:, :PAIR] * inverse
            att_ref[here, at] = attended.astype(BF16)
            inv_ref[here, at] = inverse.astype(BF16)
            ctx_ref[here, at] = (attended + near).astype(BF16)
        return carry

    lax.fori_loop(0, QUAD // PAIR, one_pair, 0)

    @pl.when(quad == 0)
    def _():
        res_ref[...] = x_ref[...].astype(F32) + bo_ref[...][None, :]

    for start in range(0, length, ROWS):
        here = slice(start, start + ROWS)
        res_ref[here] += dot_nn(ctx_ref[here], wo_ref[...])


def gather_plan(dp_size, tensor_size, own, whole, sems, copy_sem):
    axes = slice_axes(dp_size, tensor_size)
    y, x, core = axes["y"], axes["x"], axes["core"]
    mate = core.device(core.ahead(1))
    number = iter(range(1000))

    def mine(place):
        return place * CORES + core.place

    def half_of(ref, piece):
        size = ref.shape[-2] // 2
        return span(piece % 2 * size, size)

    def rows_at(ref, piece, place):
        size = ref.shape[-2] // (2 * x.size)
        return span(piece % 2 * x.size * size + place * size, size)

    def at_y(piece):
        source, target = own[piece // 2], whole[piece // 2]
        out = []
        for j in range(1, y.size):
            if piece < 4:
                block = rows_at(source, piece, x.place)
                pair = (source.at[block], target.at[mine(y.place), block])
            else:
                pair = (source, target.at[mine(y.place)])
            out.append(send(*pair, sems, next(number), y.device(y.ahead(j))))
        return out

    def at_x(piece):
        target = whole[piece // 2]
        out = []
        for j in range(1, y.size):
            block = target.at[mine(y.ahead(j)), rows_at(target, piece, x.place)]
            out += [send(block, block, sems, next(number), x.device(x.ahead(i))) for i in range(1, x.size)]
        return out

    def to_mate(piece):
        target = whole[piece // 2]
        out = []
        for j in range(1, y.size):
            block = target.at[mine(y.ahead(j))]
            block = block.at[half_of(target, piece)] if piece < 4 else block
            out.append(send(block, block, sems, next(number), mate))
        return out

    keep = [pltpu.make_async_copy(own[i], whole[i].at[mine(y.place)], copy_sem.at[i]) for i in range(3)]
    give = [send(own[i], whole[i].at[mine(y.place)], sems, next(number), mate) for i in range(3)]
    ys, xs, mates = [at_y(i) for i in range(5)], [at_x(i) for i in range(4)], [to_mate(i) for i in range(5)]

    def start(copies):
        return [copy.start for copy in copies]

    def wait(copies):
        return [copy.wait for copy in copies]

    steps = [
        [lambda: greet(axes, ("core", "y", "x"))] + start(ys[0] + ys[1] + ys[4] + give + keep),
        wait(ys[0] + ys[4]) + start(xs[0] + ys[2] + mates[4]),
        wait(ys[1]) + start(xs[1] + ys[3]),
        wait(ys[2] + xs[0]) + start(xs[2] + mates[0]),
        wait(ys[3] + xs[1]) + start(xs[3] + mates[1]),
        wait(xs[2] + xs[3]) + start(mates[2] + mates[3]),
    ]
    last = wait([copy for piece in mates for copy in piece] + give + keep)
    return dict(zip(GATHER_TIMES, steps)) | {GATHER_TIMES[len(steps)]: last}


GATHER_TIMES = (0, 4, 5, 7, 8, 10, 11)


KCH = 256
ROWS = 256


def attend(tokens, segment_ids, w_qkv, b_qkv, kernel, w_out, b_out, w_up, w_down, b_up, dp_size, tensor_size):
    count, width = tokens.shape
    seqs, length = segment_ids.shape
    quads = width // QUAD
    heads = width // HEAD
    per = QUAD // HEAD
    blocks = length // BLK
    own = pl.BlockSpec((length, QUAD), lambda r, p: (r, p))
    act = jax.ShapeDtypeStruct((count, width), BF16)
    big = jax.ShapeDtypeStruct((seqs, heads, length, length), BF16)
    big_spec = pl.BlockSpec((1, per, length, length), lambda r, p: (r, p, 0, 0))

    def part(rows_of, k):
        return pl.BlockSpec((rows_of, QUAD), lambda r, p, k=k: (0, p + k * quads))

    def whole(*shape):
        return pl.BlockSpec(shape, lambda r, p: (0,) * len(shape), pipeline_mode=pl.Buffered(1))

    others = tensor_size // CORES - 1
    copies = 3 + 10 * others + 4 * others * (dp_size // DEPTH - 1)
    return pl.pallas_call(
        functools.partial(attend_kernel, dp_size=dp_size, tensor_size=tensor_size),
        grid=(seqs, quads),
        in_specs=[
            pl.BlockSpec((length, width), lambda r, p: (r, 0)),
            whole(*segment_ids.shape),
            part(width, 0), part(width, 1), part(width, 2),
            whole(*b_qkv.shape),
            whole(*kernel.shape),
            pl.BlockSpec((QUAD, width), lambda r, p: (p, 0)),
            whole(*b_out.shape),
        ]
        + [
            whole(*each.shape) for each in (w_up, w_down, b_up)
        ],
        out_specs=[own] * 5 + [big_spec] * 2 + [own] * 3 + [pl.BlockSpec((length, width), lambda r, p: (r, 0))]
        + [pl.BlockSpec(memory_space=pl.ANY)] * 3,
        out_shape=[act] * 5 + [big] * 2 + [act] * 3 + [jax.ShapeDtypeStruct((count, width), F32)]
        + [jax.ShapeDtypeStruct((tensor_size,) + part.shape, BF16) for part in (w_up, w_down)]
        + [jax.ShapeDtypeStruct((tensor_size, 1, b_up.shape[0]), F32)],
        scratch_shapes=[
            pltpu.VMEM((length, length), BF16),
            pltpu.VMEM((blocks, BLK, 2 * BLK), BF16),
            pltpu.VMEM((2, length + 2 * HALO, 2 * PAIR), BF16),
            pltpu.VMEM((heads, 2 * BLK), F32),
            pltpu.VMEM((1, b_up.shape[0]), F32),
            pltpu.SemaphoreType.DMA((copies,)),
            pltpu.SemaphoreType.DMA((copies,)),
            pltpu.SemaphoreType.DMA((3,)),
        ],
        compiler_params=pltpu.CompilerParams(vmem_limit_bytes=56 * 2**20, collective_id=2, has_side_effects=True),
        name="attend_forward",
    )(tokens, segment_ids, w_qkv, w_qkv, w_qkv, b_qkv, kernel, w_out, b_out, w_up, w_down, b_up)


DEPTH = 4
CORES = 2


class Axis:
    def __init__(self, size, place, device):
        self.size, self.place, self.device = size, place, device

    def ahead(self, j):
        return lax.rem(self.place + j, self.size)


def slice_axes(dp_size, tensor_size):
    dp, tensor = lax.axis_index("dp"), lax.axis_index("tensor")
    across = dp_size // DEPTH
    z, x = dp // across, lax.rem(dp, across)
    y, core = tensor // CORES, lax.rem(tensor, CORES)
    return {
        "core": Axis(CORES, core, lambda p: (dp, y * CORES + p)),
        "y": Axis(tensor_size // CORES, y, lambda p: (dp, p * CORES + core)),
        "x": Axis(across, x, lambda p: (z * across + p, tensor)),
        "z": Axis(DEPTH, z, lambda p: (p * across + x, tensor)),
    }


def greet(axes, names=("core", "y", "x", "z")):
    barrier = pltpu.get_barrier_semaphore()
    count = 0
    for axis in (axes[name] for name in names):
        for j in range(1, axis.size):
            pl.semaphore_signal(
                barrier, inc=1, device_id=axis.device(axis.ahead(j)), device_id_type=pl.DeviceIdType.MESH
            )
            count += 1
    pl.semaphore_wait(barrier, count)


def send(source, target, sems, at, device):
    return pltpu.make_async_remote_copy(
        src_ref=source, dst_ref=target, send_sem=sems[0].at[at], recv_sem=sems[1].at[at],
        device_id=device, device_id_type=pl.DeviceIdType.MESH,
    )


def span(start, size):
    if isinstance(start, int):
        return pl.ds(start, size)
    return pl.ds(pl.multiple_of(start, math.gcd(size, 16)), size)


def add_rows(target, target_at, terms, size):
    tile = next(t for t in (64, 48, 32, 24, 16, 12, 8) if size % t == 0)

    def one(i, carry):
        total = None
        for ref, start in terms:
            rows_of = ref[span(start + i * tile, tile)].astype(F32)
            total = rows_of if total is None else total + rows_of
        target[span(target_at + i * tile, tile)] = total.astype(target.dtype)
        return carry

    lax.fori_loop(0, size // tile, one, 0)


class Reduction:
    def __init__(self, axes, order, back, source, source_at, size, final, final_at, landings, sems, first_sem=0):
        self.axes, self.order, self.back = axes, order, back
        self.source, self.source_at, self.size = source, source_at, size
        self.final, self.final_at = final, final_at
        self.landings, self.sems = landings, sems
        self.first_sem = first_sem

    def plan(self):
        size, at, out = self.size, self.final_at, []
        for name in self.order:
            axis = self.axes[name]
            size //= axis.size
            at = at + axis.place * size
            out.append((axis, size, at))
        return out

    def copies(self, stage):
        stages = self.plan()
        sem = self.first_sem
        for axis, _, _ in stages[:stage]:
            sem += axis.size - 1
        axis, size, _ = stages[stage]
        held, held_at = (self.source, self.source_at) if stage == 0 else (self.landings[stage - 1].at[0], 0)
        return [
            send(
                held.at[span(held_at + axis.ahead(j) * size, size)], self.landings[stage].at[j - 1],
                self.sems, sem + j - 1, axis.device(axis.ahead(j)),
            )
            for j in range(1, axis.size)
        ]

    def settle(self, stage):
        for copy in self.copies(stage):
            copy.wait()
        axis, size, final_at = self.plan()[stage]
        held, held_at = (self.source, self.source_at) if stage == 0 else (self.landings[stage - 1].at[0], 0)
        terms = [(held, held_at + axis.place * size)]
        terms += [(self.landings[stage].at[j - 1], 0) for j in range(1, axis.size)]
        if stage == len(self.order) - 1:
            add_rows(self.final, final_at, terms, size)
        else:
            add_rows(self.landings[stage].at[0], 0, terms, size)

    def gathers(self, which):
        stages = self.plan()
        sem = self.first_sem + sum(axis.size - 1 for axis, _, _ in stages)
        for name in self.back[:which]:
            sem += self.axes[name].size - 1
        depth = self.order.index(self.back[which])
        axis, size, at = stages[depth]
        block = self.final.at[span(at, size)]
        return [send(block, block, self.sems, sem + j - 1, axis.device(axis.ahead(j))) for j in range(1, axis.size)]

    def events(self):
        out = []
        count = len(self.order)

        def begin(copies):
            first = len(copies) // 2
            for copy in copies[first:] + copies[:first]:
                copy.start()

        for stage in range(count):
            def event(stage=stage):
                if stage > 0:
                    self.settle(stage - 1)
                begin(self.copies(stage))

            out.append(event)
        for which in range(len(self.back)):
            def event(which=which):
                if which == 0:
                    self.settle(count - 1)
                else:
                    for copy in self.gathers(which - 1):
                        copy.wait()
                begin(self.gathers(which))

            out.append(event)

        def last():
            for copy in self.gathers(len(self.back) - 1):
                copy.wait()

        out.append(last)
        return out


def landing_shapes(order, sizes, size, columns, dtype):
    shapes = []
    for name in order:
        size //= sizes[name]
        shapes.append(pltpu.VMEM((sizes[name] - 1, size, columns), dtype))
    return shapes


def copies_of(order, back, sizes):
    return sum(sizes[name] - 1 for name in order) + sum(sizes[name] - 1 for name in back)

GELU_A = math.sqrt(2.0 / math.pi)
GELU_B = 0.044715
TILE = 256
UNROLL = 4


def gelu_terms(pre):
    square = pre * pre
    swing = jnp.tanh(pre * (GELU_A + GELU_A * GELU_B * square))
    gate = 0.5 + 0.5 * swing
    steep = GELU_A + 3.0 * GELU_A * GELU_B * square
    return pre * gate, gate + 0.5 * pre * (1.0 - swing * swing) * steep


def norm_backward(grad_out, unit, scaling, gain):
    grad_unit = grad_out * gain
    return scaling * (
        grad_unit
        - jnp.mean(grad_unit, -1, keepdims=True)
        - unit * jnp.mean(grad_unit * unit, -1, keepdims=True)
    )


def column_sum(values):
    return jnp.sum(values, 0, keepdims=True)


def ffn_kernel(
    res_ref, cot_hbm, ctx_hbm, wo_hbm, gain1_ref, shift1_ref, gain2_ref, shift2_ref, bd_ref, bu_ref, wu_ref, wd_ref,
    out_ref, dproj_ref, dctx_ref, gwo_ref, pu_ref, pd_ref, small_ref,
    low_ref, acc_ref, hid_ref, slope_ref, dffn_ref, dpre_ref, sendu_ref, sendd_ref, recvu_ref, recvd_ref, pdown_ref, yland_ref,
    send_sem, recv_sem, cot_ref, ctx_ref, wo_ref, load_sem,
):
    parts = pl.num_programs(0) // 2
    step = pl.program_id(0)
    count, width = res_ref.shape
    share = dpre_ref.shape[1]
    tiles = count // TILE
    f = part_order(step, parts)
    late = jnp.maximum(step - parts, 0)
    heights = parts // CORES
    slot = late // CORES
    dp, tensor = lax.axis_index("dp"), lax.axis_index("tensor")
    height, core = tensor // CORES, lax.rem(tensor, CORES)
    mate = (dp, height * CORES + 1 - core)

    def up_to_mate(which):
        return send(sendu_ref.at[which], recvu_ref.at[which], (send_sem.at[0], recv_sem.at[0]), which, mate)

    def down_to_mate(which):
        return send(sendd_ref.at[which], recvd_ref.at[which], (send_sem.at[1], recv_sem.at[1]), which, mate)

    def to_height(which):
        there = (dp, lax.rem(height + 1 + which, heights) * CORES + core)
        return send(pdown_ref.at[which], yland_ref.at[which], (send_sem.at[2], recv_sem.at[2]), which, there)

    def down_part(late):
        part = part_order(parts + late, parts)
        piece = math.gcd(TILE, share)
        for start in range(0, share, piece):
            cut = slice(start, start + piece)
            yield cut, dot_tn(hid_ref[part, :, cut], dffn_ref[...]).astype(BF16)

    def ready(which):
        down_to_mate(which).wait()
        add_rows(pdown_ref.at[which], 0, [(pdown_ref.at[which], 0), (recvd_ref.at[which], 0)], share)
        if which < heights - 1:
            to_height(which).start()

    loads = [
        pltpu.make_async_copy(source, target, load_sem.at[i])
        for i, (source, target) in enumerate(((cot_hbm, cot_ref), (ctx_hbm, ctx_ref), (wo_hbm, wo_ref)))
    ]

    @pl.when(step == 0)
    def _():
        for load in loads:
            load.start()
        barrier = pltpu.get_barrier_semaphore()
        peers = [mate] + [(dp, lax.rem(height + j, heights) * CORES + core) for j in range(1, heights)]
        for peer in peers:
            pl.semaphore_signal(barrier, inc=1, device_id=peer, device_id_type=pl.DeviceIdType.MESH)
        pl.semaphore_wait(barrier, len(peers))

    def put_row(row, values):
        for i in range(values.shape[1] // PAIR):
            small_ref[pl.ds(row + i, 1)] = values[:, i * PAIR : (i + 1) * PAIR]

    def at(t):
        return pl.ds(pl.multiple_of(t * TILE, TILE), TILE)

    @pl.when(step == 0)
    def _():
        def one(t, carry):
            unit, _ = norm_stats(res_ref[at(t)])
            low_ref[at(t)] = (unit * gain1_ref[...][None, :] + shift1_ref[...][None, :]).astype(BF16)
            acc_ref[at(t)] = jnp.zeros((TILE, width), F32)
            return carry

        lax.fori_loop(0, tiles, one, 0, unroll=UNROLL)

    @pl.when(step < parts)
    def _():
        def one(t, carry):
            pre = dot_nn(low_ref[at(t)], wu_ref[0]) + bu_ref[0].astype(F32)
            hidden, slope = gelu_terms(pre)
            hidden = hidden.astype(BF16)
            hid_ref[f, at(t)] = hidden
            slope_ref[f, at(t)] = slope.astype(BF16)
            acc_ref[at(t)] += dot_nn(hidden, wd_ref[0])
            return carry

        lax.fori_loop(0, tiles, one, 0, unroll=UNROLL)

    @pl.when(step == parts)
    def _():
        loads[0].wait()

        def one(t, sums):
            unit, _ = norm_stats(res_ref[at(t)])
            first = unit * gain1_ref[...][None, :] + shift1_ref[...][None, :]
            unit, scaling = norm_stats(first + acc_ref[at(t)] + bd_ref[...][None, :])
            out_ref[at(t)] = (unit * gain2_ref[...][None, :] + shift2_ref[...][None, :]).astype(BF16)
            grad = cot_ref[at(t)].astype(F32)
            d_res = norm_backward(grad, unit, scaling, gain2_ref[...][None, :])
            d_ffn = d_res.astype(BF16)
            acc_ref[at(t)] = d_res
            dffn_ref[at(t)] = d_ffn
            return (
                sums[0] + column_sum(grad * unit),
                sums[1] + column_sum(grad),
                sums[2] + column_sum(d_ffn.astype(F32)),
            )

        zero = jnp.zeros((1, width), F32)
        sums = lax.fori_loop(0, tiles, one, (zero, zero, zero), unroll=UNROLL)
        small_ref[...] = jnp.zeros_like(small_ref)
        for i, values in enumerate(sums):
            put_row(i * (width // PAIR), values)

        def theirs(which, carry):
            for cut, values in down_part(CORES * which):
                sendd_ref[which, cut] = values
            down_to_mate(which).start()
            return carry

        def ours(which, carry):
            for cut, values in down_part(CORES * which + 1):
                pdown_ref[which, cut] = values
            return carry

        for which in range(heights):
            theirs(which, 0)
            if which > 0:
                ready(which - 1)
            ours(which, 0)

    @pl.when(step >= parts)
    def _():
        def one(t, total):
            d_hidden = dot_nt(dffn_ref[at(t)], wd_ref[0])
            d_pre = (d_hidden * slope_ref[f, at(t)].astype(F32)).astype(BF16)
            dpre_ref[at(t)] = d_pre
            acc_ref[at(t)] += dot_nt(d_pre, wu_ref[0])
            return total + column_sum(d_pre.astype(F32))

        bias = lax.fori_loop(0, tiles, one, jnp.zeros((1, share), F32), unroll=UNROLL)
        put_row(6 * (width // PAIR) + f * (share // PAIR), bias)

        @pl.when(late == 0)
        def _():
            ready(heights - 1)

        @pl.when(lax.rem(late, CORES) == 0)
        def _():
            for start in range(0, width, TILE):
                cut = slice(start, start + TILE)
                sendu_ref[slot, cut] = dot_tn(low_ref[:, cut], dpre_ref[...]).astype(BF16)
            up_to_mate(slot).start()

        @pl.when(lax.rem(late, CORES) == 1)
        def _():
            up_to_mate(slot).wait()
            for start in range(0, width, TILE):
                cut = slice(start, start + TILE)
                values = dot_tn(low_ref[:, cut], dpre_ref[...])
                pu_ref[slot, cut] = (values + recvu_ref[slot, cut].astype(F32)).astype(BF16)

    @pl.when(step == 2 * parts - 1)
    def _():
        loads[1].wait()
        loads[2].wait()

        def one(t, sums):
            unit, scaling = norm_stats(res_ref[at(t)])
            grad = acc_ref[at(t)]
            d_proj = norm_backward(grad, unit, scaling, gain1_ref[...][None, :]).astype(BF16)
            dproj_ref[at(t)] = d_proj
            dctx_ref[at(t)] = dot_nt(d_proj, wo_ref[...]).astype(BF16)
            return (
                sums[0] + column_sum(grad * unit),
                sums[1] + column_sum(grad),
                sums[2] + column_sum(d_proj.astype(F32)),
            )

        zero = jnp.zeros((1, width), F32)
        sums = lax.fori_loop(0, tiles, one, (zero, zero, zero), unroll=UNROLL)
        for i, values in enumerate(sums):
            put_row((3 + i) * (width // PAIR), values)
        for start in range(0, width, TILE):
            values = dot_tn(ctx_ref[:, start : start + TILE], dproj_ref[...]).astype(BF16)
            gwo_ref[start : start + TILE] = values[:, : width // 2]
            gwo_ref[width + start : width + start + TILE] = values[:, width // 2 :]
        for which in range(heights - 1):
            to_height(which).wait()
        terms = [(pdown_ref.at[heights - 1], 0)] + [(yland_ref.at[which], 0) for which in range(heights - 1)]
        add_rows(pd_ref, 0, terms, share)


def part_order(step, parts):
    tensor = lax.axis_index("tensor")
    height, core = tensor // CORES, lax.rem(tensor, CORES)
    late = jnp.maximum(step - parts, 0)
    there = lax.rem(height + 1 + late // CORES, parts // CORES)
    whose = jnp.where(lax.rem(late, CORES) == 0, 1 - core, core)
    return jnp.where(step < parts, step, there * CORES + whose)


def feed_forward(res, cot, ctx, w_out, gain1, shift1, gain2, shift2, b_down, b_up, w_up, w_down):
    count, width = res.shape
    parts, _, share = w_up.shape
    heights = parts // 2
    smalls = 6 * width // PAIR + parts * share // PAIR
    smalls = -(-smalls // 8) * 8

    def whole(*shape):
        return pl.BlockSpec(shape, lambda s: (0,) * len(shape), pipeline_mode=pl.Buffered(1))

    def per_part(*shape):
        return pl.BlockSpec((1,) + shape, lambda s: (part_order(s, parts),) + (0,) * len(shape))

    act = jax.ShapeDtypeStruct((count, width), BF16)
    return pl.pallas_call(
        ffn_kernel,
        grid=(2 * parts,),
        in_specs=[whole(count, width)]
        + [pl.BlockSpec(memory_space=pl.ANY)] * 3
        + [whole(width)] * 5
        + [per_part(1, share), per_part(width, share), per_part(share, width)],
        out_specs=[whole(count, width)] * 3
        + [whole(2 * width, width // 2), whole(heights, width, share), whole(share, width), whole(smalls, PAIR)],
        out_shape=[act] * 3
        + [
            jax.ShapeDtypeStruct((2 * width, width // 2), BF16),
            jax.ShapeDtypeStruct((heights, width, share), BF16),
            jax.ShapeDtypeStruct((share, width), BF16),
            jax.ShapeDtypeStruct((smalls, PAIR), F32),
        ],
        scratch_shapes=[
            pltpu.VMEM((count, width), BF16),
            pltpu.VMEM((count, width), F32),
            pltpu.VMEM((parts, count, share), BF16),
            pltpu.VMEM((parts, count, share), BF16),
            pltpu.VMEM((count, width), BF16),
            pltpu.VMEM((count, share), BF16),
            pltpu.VMEM((heights, width, share), BF16),
            pltpu.VMEM((heights, share, width), BF16),
            pltpu.VMEM((heights, width, share), BF16),
            pltpu.VMEM((heights, share, width), BF16),
            pltpu.VMEM((heights, share, width), BF16),
            pltpu.VMEM((heights - 1, share, width), BF16),
            pltpu.SemaphoreType.DMA((3, heights)),
            pltpu.SemaphoreType.DMA((3, heights)),
            pltpu.VMEM((count, width), BF16),
            pltpu.VMEM((count, width), BF16),
            pltpu.VMEM((width, width), BF16),
            pltpu.SemaphoreType.DMA((3,)),
        ],
        compiler_params=pltpu.CompilerParams(vmem_limit_bytes=60 * 2**20, collective_id=0, has_side_effects=True),
        name="feed_forward",
    )(res, cot, ctx, w_out, gain1, shift1, gain2, shift2, b_down, b_up, w_up, w_down)


def attend_back_kernel(
    dctx_ref, att_ref, inv_ref, q_ref, k_ref, v_ref, sq_ref, sk_ref, w_ref, s_ref, x_ref, seg_ref,
    wqkv_hbm, kernel_ref, dproj_ref, gwo_ref, pu_ref, pd_ref, small_ref,
    gt_ref, all_out, up_out, down_out, few_out,
    near_ref, vv_ref, dpad_ref, dcos_ref, dq_ref, dk_ref, dv_ref, joined_ref, gwacc_ref, conv_ref,
    gwlow_ref, gb_ref, flip_ref, mini_ref, all_ref, up_ref, down_ref, few_ref, out_sem, wqkv_ref, load_sem, *links,
    plan, quads, seqs,
):
    quad, row = pl.program_id(0), pl.program_id(1)
    length = x_ref.shape[0]
    blocks = length // BLK
    inside = slice(HALO, HALO + length)

    _, sizes, dp_size, tensor_size = plan
    axes = slice_axes(dp_size, tensor_size)
    ticks = schedule(axes, sizes, quads, seqs, gwo_ref, pu_ref, pd_ref, gwlow_ref, mini_ref, all_ref, up_ref, down_ref, few_ref, links,
        (all_out, up_out, down_out, few_out, out_sem))
    calls = quads * seqs * (QUAD // HEAD)

    build_near(*segment_rows(seg_ref, row), near_ref)
    for half in range(2):
        edge = jnp.zeros((HALO, PAIR), BF16)
        for ref in (vv_ref, dpad_ref):
            ref[half, :HALO, :PAIR] = edge
            ref[half, HALO + length :, :PAIR] = edge
        vv_ref[half, inside, PAIR:] = head_mask(half, (length, PAIR))

    @pl.when(row == 0)
    def _():
        conv_ref[...] = jnp.zeros_like(conv_ref)
        gwacc_ref[...] = jnp.zeros_like(gwacc_ref)

    load = pltpu.make_async_copy(wqkv_hbm, wqkv_ref, load_sem)

    @pl.when((quad == 0) & (row == 0))
    def _():
        load.start()
        gb_ref[...] = jnp.zeros_like(gb_ref)
        flip_ref[...] = place_taps(kernel_ref[...], True)
        mini_ref[...] = jnp.zeros_like(mini_ref)
        mini_ref[: small_ref.shape[0]] = small_ref[...]
        filled = 2 * gwacc_ref.shape[0]
        if gwlow_ref.shape[1] > filled:
            gwlow_ref[:, filled:] = jnp.zeros((quads, gwlow_ref.shape[1] - filled, gwlow_ref.shape[2]), BF16)

    def one_pair(pair, carry):
        at = pl.ds(pl.multiple_of(pair * PAIR, PAIR), PAIR)
        inverse = inv_ref[:, at].astype(F32)
        d_ctx = dctx_ref[:, at]
        d_summed = (d_ctx.astype(F32) * inverse).astype(BF16)
        d_total = (-d_summed.astype(F32) * att_ref[:, at].astype(F32)).astype(BF16)
        both = jnp.concatenate([d_summed, d_total], 1)
        dk = jnp.zeros((PAIR, length), F32)
        dv = jnp.zeros((PAIR, length), F32)
        turn = (quad * seqs + row) * (QUAD // PAIR) + pair
        for half in range(2):
            for when in range(half, calls, 2):
                if ticks.get(when):

                    @pl.when(turn == when // 2)
                    def _(when=when):
                        for event in ticks[when]:
                            event()

            head = pair * 2 + half
            mask = head_mask(half, (length, PAIR))
            vv_ref[half, inside, :PAIR] = v_ref[:, at] * mask
            dpad_ref[half, inside] = d_ctx * mask
            k_half = k_ref[:, at] * mask
            for block in range(blocks):
                here = slice(block * BLK, block * BLK + BLK)
                low, high = window_of(block, blocks)
                d_weight = dot_nt(both[here], vv_ref[half, HALO + low : HALO + high])
                d_cos = d_weight.astype(BF16) * s_ref[0, head, here, low:high]
                dcos_ref[here, low:high] = d_cos
                if low > 0:
                    dcos_ref[here, :low] = jnp.zeros((BLK, low), BF16)
                if high < length:
                    dcos_ref[here, high:] = jnp.zeros((BLK, length - high), BF16)
                grown = dot_nn(d_cos, k_half[low:high])
                if half == 0:
                    dq_ref[here] = grown
                else:
                    dq_ref[here] += grown
                window = slice(block * BLK, block * BLK + 2 * BLK)
                near = near_ref[block]
                taps = band(flip_ref[pl.ds(quad * (QUAD // HEAD) + head, 1)], BLK).astype(BF16) * near
                grown = dot_nn(taps, dpad_ref[half, window])
                if half == 0:
                    dv_ref[here] = grown
                else:
                    dv_ref[here] += grown
                conv_ref[head] += near.astype(F32) * dot_nt(d_ctx[here], vv_ref[half, window, :PAIR])
            dk += dot_tn(q_ref[:, at] * mask, dcos_ref[...])
            dv += dot_tn(d_summed * mask, w_ref[0, head])
        dv_ref[...] += dv.T
        grad = SLOPE * dq_ref[...]
        unit = q_ref[:, at].astype(F32)
        d_query = sq_ref[:, at].astype(F32) * (SHRINK * grad - unit * (head_sum(grad * unit) / SHRINK))
        grad = SLOPE * dk.T
        unit = k_ref[:, at].astype(F32)
        d_key = sk_ref[:, at].astype(F32) * (grad - unit * head_sum(grad * unit))
        for part, values in enumerate((d_query, d_key, dv_ref[...])):
            joined_ref[quad, row, :, pl.ds(pl.multiple_of(part * QUAD + pair * PAIR, PAIR), PAIR)] = values.astype(BF16)
        return carry

    lax.fori_loop(0, QUAD // PAIR, one_pair, 0)

    gb_ref[quad, :1] += column_sum(joined_ref[quad, row].astype(F32))
    width = gwacc_ref.shape[0]
    for start in range(0, width, TILE):
        cut = slice(start, start + TILE)
        gwacc_ref[cut] += dot_tn(x_ref[:, cut], joined_ref[quad, row])

    @pl.when(row == seqs - 1)
    def _():
        half = gwacc_ref.shape[1] // 2
        for start in range(0, width, TILE):
            for side in range(2):
                values = gwacc_ref[start : start + TILE, side * half : (side + 1) * half]
                gwlow_ref[quad, side * width + start : side * width + start + TILE] = values.astype(BF16)
        base = small_ref.shape[0]
        lines = gb_ref.shape[2] // PAIR
        for i in range(lines):
            mini_ref[pl.ds(base + quad * lines + i, 1)] = gb_ref[quad, :1, i * PAIR : (i + 1) * PAIR]
        base += quads * lines
        for head in range(QUAD // HEAD):
            sums = conv_ref[head]
            high = sums.astype(BF16)
            turn = (rows((BLK, BLK)) + lanes((BLK, BLK)) == BLK - 1).astype(BF16)
            turned = dot_nn(turn, high) + dot_nn(turn, (sums - high.astype(F32)).astype(BF16))
            turned = pltpu.roll(turned, BLK, 1, stride=1, stride_axis=0)
            mini_ref[pl.ds(base + quad * (QUAD // HEAD) + head, 1)] = column_sum(turned)[:, :PAIR]

    last = (quad == quads - 1) & (row == seqs - 1)

    @pl.when(last)
    def _():
        for event in ticks.get(calls, ()):
            event()

    @pl.when((quad == quads - 1) & (row == 0))
    def _():
        load.wait()

    @pl.when(quad == quads - 1)
    def _():
        for start in range(0, length, TILE):
            cut = slice(start, start + TILE)
            grown = dproj_ref[cut].astype(F32)
            for q in range(quads):
                for part in range(3):
                    to = part * width + q * QUAD
                    grown += dot_nt(joined_ref[q, row, cut, part * QUAD : (part + 1) * QUAD], wqkv_ref[:, to : to + QUAD])
            gt_ref[cut] = grown.astype(BF16)

    @pl.when(last)
    def _():
        for when in sorted(ticks):
            if when > calls:
                for event in ticks[when]:
                    event()


FFN_PLAN = (
    (
        (("z", "x"), (1, 28, 42, 44, 57)),
        (("x", "z"), (1, 7, 14, 38, 48)),
    ),
    (
        (("x", "z"), (0, 8, 13, 17, 24, 36)),
        (("x", "z"), (6, 16, 23, 42, 48, 55)),
    ),
)
ALL_PLAN = (
    (
        (3, 1, (2, 4, 13, 16, 21, 27, 33, 43, 54)),
    ),
    (
        (3, 0, (13, 18, 24, 29, 31, 41, 43, 51, 53)),
    ),
    (
        (3, 1, (17, 18, 23, 26, 29, 34, 41, 46, 47)),
    ),
    (
        (3, 1, (24, 25, 30, 35, 39, 42, 45, 50, 52)),
    ),
)
MINI_ORDER = 1
MINI_TIMES = (29, 31, 32, 37, 40, 42, 49, 52, 56)
FFN_ROWS = 384
ORDERS = (("core", "x", "y", "z"), ("core", "y", "x", "z"))


def all_parts(index, size, devices):
    parts = ALL_PLAN[index]
    if sum(units for units, _, _ in parts) * 16 * devices != size:
        parts = ((size // (16 * devices), parts[-1][1], parts[-1][2]),)
    out, start = [], 0
    for units, order, times in parts:
        rows_of = units * 16 * devices
        out.append((start, rows_of, ORDERS[order], times))
        start += rows_of
    return out


class FfnReduction(Reduction):
    def copies(self, stage):
        if stage > 0:
            return super().copies(stage)
        axis = self.axes["y"]
        return [
            send(
                self.source.at[j - 1, span(self.source_at, self.size)], self.landings[0].at[j - 1],
                self.sems, self.first_sem + j - 1, axis.device(axis.ahead(j)),
            )
            for j in range(1, axis.size)
        ]

    def plan(self):
        size, at = self.size, self.final_at
        out = [(self.axes["y"], size, at)]
        for name in self.order[1:]:
            axis = self.axes[name]
            size //= axis.size
            at = at + axis.place * size
            out.append((axis, size, at))
        return out

    def settle(self, stage):
        if stage > 0:
            return super().settle(stage)
        axis = self.axes["y"]
        for copy in self.copies(0):
            copy.wait()
        terms = [(self.source.at[axis.size - 1], self.source_at)]
        terms += [(self.landings[0].at[j - 1], 0) for j in range(1, axis.size)]
        add_rows(self.landings[0].at[0], 0, terms, self.size)


def link_plan(sizes, width, share, quads):
    out = []
    devices = math.prod(sizes.values())
    y = sizes["y"]
    for late, (height, columns) in enumerate(((share, width), (width, share))):
        for start in range(0, height, FFN_ROWS):
            order = FFN_PLAN[late][start // FFN_ROWS][0]
            shapes = [pltpu.VMEM((y - 1, FFN_ROWS, columns), BF16)] if late else []
            shapes += landing_shapes(order, sizes, FFN_ROWS, columns, BF16)
            out.append((shapes, copies_of((("y",) if late else ()) + order, order, sizes)))
    size = padded(2 * width, devices)
    for index in range(quads + 1):
        for _, rows_of, order, _ in all_parts(index, size, devices):
            out.append((landing_shapes(order, sizes, rows_of, width // 2, BF16), copies_of(order, order, sizes)))
    order = ORDERS[MINI_ORDER]
    out.append((landing_shapes(order, sizes, 8 * devices, PAIR, F32), copies_of(order, order, sizes)))
    return out


def padded(size, devices):
    return -(-size // (16 * devices)) * 16 * devices


def schedule(axes, sizes, quads, seqs, gwo_ref, pu_ref, pd_ref, gwlow_ref, mini_ref, all_ref, up_ref, down_ref, few_ref, links, outs):
    all_out, up_out, down_out, few_out, out_sem = outs
    calls = quads * seqs * (QUAD // HEAD)
    share, width = pd_ref.shape
    devices = math.prod(sizes.values())
    groups = link_plan(sizes, width, share, quads)
    taken, position = [], 0
    for shapes, _ in groups:
        taken.append((links[position : position + len(shapes)], links[position + len(shapes) : position + len(shapes) + 2]))
        position += len(shapes) + 2
    ticks = {0: [lambda: greet(axes)]}

    stores = []

    def enlist(reduction, times, done, place):
        for time, event in zip(times, reduction.events(), strict=True):
            ticks.setdefault(time, []).append(event)
        store = pltpu.make_async_copy(done, place, out_sem.at[len(stores)])
        ticks[times[-1]].append(store.start)
        stores.append(store)

    number = 0
    for late, (source, final, place) in enumerate(((pd_ref, down_ref, down_out), (pu_ref, up_ref, up_out))):
        for start in range(0, final.shape[0], FFN_ROWS):
            landings, sems = taken[number]
            block = span(start, FFN_ROWS)
            order, times = FFN_PLAN[late][start // FFN_ROWS]
            kind = FfnReduction if late else Reduction
            whole_order = ("y",) + order if late else order
            reduction = kind(axes, whole_order, order[::-1], source, start, FFN_ROWS, final, start, landings, sems)
            enlist(reduction, times, final.at[block], place.at[block])
            number += 1
    size = padded(2 * width, devices)
    for index in range(quads + 1):
        source = gwo_ref if index == 0 else gwlow_ref.at[index - 1]
        for start, rows_of, order, times in all_parts(index, size, devices):
            landings, sems = taken[number]
            final = all_ref.at[index]
            reduction = Reduction(axes, order, order[::-1], source, start, rows_of, final, start, landings, sems)
            enlist(reduction, times, final.at[span(start, rows_of)], all_out.at[index, span(start, rows_of)])
            number += 1
    landings, sems = taken[number]
    order = ORDERS[MINI_ORDER]
    reduction = Reduction(axes, order, order[::-1], mini_ref, 0, 8 * devices, few_ref, 0, landings, sems)
    enlist(reduction, MINI_TIMES, few_ref, few_out)
    ticks[max(ticks) + 1] = [store.wait for store in stores]
    return ticks


def attend_back(dctx, att, inv, q, k, v, sq, sk, weight, slope, tokens, segment_ids, w_qkv, kernel, dproj, gwo, pu, pd, small, dp_size, tensor_size):
    count, width = tokens.shape
    seqs, length = segment_ids.shape
    quads = width // QUAD
    per = QUAD // HEAD
    blocks = length // BLK
    own = pl.BlockSpec((length, QUAD), lambda p, r: (r, p))
    big = pl.BlockSpec((1, per, length, length), lambda p, r: (r, p, 0, 0))
    wide = pl.BlockSpec((length, width), lambda p, r: (r, 0))

    sizes = {"core": CORES, "y": tensor_size // CORES, "x": dp_size // DEPTH, "z": DEPTH}
    devices = dp_size * tensor_size
    share = pd.shape[0]
    grown = padded(2 * width, devices)
    gwo = jnp.pad(gwo, ((0, grown - gwo.shape[0]), (0, 0)))
    minis = 8 * devices
    scratch = []
    for shapes, count_of in link_plan(sizes, width, share, quads):
        scratch += shapes + [pltpu.SemaphoreType.DMA((count_of,)), pltpu.SemaphoreType.DMA((count_of,))]

    def whole(*shape):
        return pl.BlockSpec(shape, lambda p, r: (0,) * len(shape), pipeline_mode=pl.Buffered(1))

    return pl.pallas_call(
        functools.partial(attend_back_kernel, plan=(None, sizes, dp_size, tensor_size), quads=quads, seqs=seqs),
        grid=(quads, seqs),
        in_specs=[own] * 8
        + [big] * 2
        + [
            wide,
            whole(*segment_ids.shape),
            pl.BlockSpec(memory_space=pl.ANY),
            whole(*kernel.shape),
            wide,
            whole(*gwo.shape), whole(*pu.shape), whole(*pd.shape), whole(*small.shape),
        ],
        out_specs=[
            pl.BlockSpec((length, width), lambda p, r: (jnp.where(p == quads - 1, r, 0), 0)),
        ]
        + [pl.BlockSpec(memory_space=pl.ANY)] * 4,
        out_shape=[
            jax.ShapeDtypeStruct((count, width), BF16),
            jax.ShapeDtypeStruct((quads + 1, grown, width // 2), BF16),
            jax.ShapeDtypeStruct((width, share), BF16),
            jax.ShapeDtypeStruct((share, width), BF16),
            jax.ShapeDtypeStruct((minis, PAIR), F32),
        ],
        scratch_shapes=[
            pltpu.VMEM((blocks, BLK, 2 * BLK), BF16),
            pltpu.VMEM((2, length + 2 * HALO, 2 * PAIR), BF16),
            pltpu.VMEM((2, length + 2 * HALO, PAIR), BF16),
            pltpu.VMEM((length, length), BF16),
            pltpu.VMEM((length, PAIR), F32),
            pltpu.VMEM((length, PAIR), F32),
            pltpu.VMEM((length, PAIR), F32),
            pltpu.VMEM((quads, seqs, length, 3 * QUAD), BF16),
            pltpu.VMEM((width, 3 * QUAD), F32),
            pltpu.VMEM((per, BLK, 2 * BLK), F32),
            pltpu.VMEM((quads, grown, width // 2), BF16),
            pltpu.VMEM((quads, 8, 3 * QUAD), F32),
            pltpu.VMEM((width // HEAD, 2 * BLK), F32),
            pltpu.VMEM((minis, PAIR), F32),
            pltpu.VMEM((quads + 1, grown, width // 2), BF16),
            pltpu.VMEM((width, share), BF16),
            pltpu.VMEM((share, width), BF16),
            pltpu.VMEM((minis, PAIR), F32),
            pltpu.SemaphoreType.DMA((len(link_plan(sizes, width, share, quads)),)),
            pltpu.VMEM((width, 3 * width), BF16),
            pltpu.SemaphoreType.DMA,
        ]
        + scratch,
        compiler_params=pltpu.CompilerParams(vmem_limit_bytes=60 * 2**20, collective_id=1, has_side_effects=True),
        name="attend_backward",
    )(dctx, att, inv, q, k, v, sq, sk, weight, slope, tokens, segment_ids, w_qkv, kernel, dproj, gwo, pu, pd, small)


def spread_kernel(low_ref, high_ref, up_ref, down_ref, few_ref, a_ref, b_ref, gw_ref, gwo_ref, gup_ref, gdown_ref, a_out, b_out, *vectors, first_lane, base):
    width = gwo_ref.shape[1]
    half = width // 2
    quads = low_ref.shape[0] - 1
    gwo_ref[:, :half] = low_ref[0].astype(F32)
    gwo_ref[:, half:] = high_ref[0].astype(F32)
    for quad in range(quads):
        for part in range(3):
            for start in range(part * QUAD, (part + 1) * QUAD, PAIR):
                side, lane = (low_ref, start) if start < half else (high_ref, start - half)
                to = part * width + quad * QUAD + start - part * QUAD
                gw_ref[:, to : to + PAIR] = side[1 + quad, :, lane : lane + PAIR].astype(F32)
    a_out[...] = a_ref[...]
    b_out[...] = b_ref[...]
    gup_ref[...] = up_ref[...].astype(F32)
    gdown_ref[...] = down_ref[...].astype(F32)

    @pl.when(pl.program_id(0) == 0)
    def _():
        gb_ref, conv_ref, *six, gbu_ref = vectors
        lines = width // PAIR

        def copy_line(target, to, line):
            target[to * PAIR : (to + 1) * PAIR] = few_ref[line]

        for number, target in enumerate(six):
            for i in range(lines):
                copy_line(target, i, number * lines + i)
        share = gbu_ref.shape[0] // PAIR
        mine = lax.axis_index("tensor") * share
        for i in range(share):
            copy_line(gbu_ref, i, 6 * lines + mine + i)
        per = QUAD // PAIR
        for quad in range(quads):
            for part in range(3):
                for i in range(per):
                    copy_line(gb_ref, (part * width + quad * QUAD) // PAIR + i, base + (quad * 3 + part) * per + i)
        heads, taps = conv_ref.shape
        kept = few_ref[base + 3 * lines : base + 3 * lines + heads]
        conv_ref[...] = pltpu.roll(kept, PAIR - first_lane, 1)[:, :taps]


def spread_out(grads, up, down, few, out, gt, width, heads, taps, first_lane, base):
    chunks = grads.shape[0]
    quads = chunks - 1
    steps = 8
    rows_of = width // steps
    share = up.shape[1]
    down_rows = share // steps

    def whole(*shape):
        return pl.BlockSpec(shape, lambda s: (0,) * len(shape))

    def by_rows(count, columns):
        return pl.BlockSpec((count, columns), lambda s: (s, 0))

    row = jax.ShapeDtypeStruct((width,), F32)
    return pl.pallas_call(
        functools.partial(spread_kernel, first_lane=first_lane, base=base),
        grid=(steps,),
        in_specs=[
            pl.BlockSpec((chunks, rows_of, width // 2), lambda s: (0, s, 0)),
            pl.BlockSpec((chunks, rows_of, width // 2), lambda s: (0, steps + s, 0)),
            by_rows(rows_of, share),
            by_rows(down_rows, width),
            whole(*few.shape),
            by_rows(out.shape[0] // steps, width), by_rows(out.shape[0] // steps, width),
        ],
        out_specs=[
            by_rows(rows_of, 3 * width), by_rows(rows_of, width), by_rows(rows_of, share), by_rows(down_rows, width),
            by_rows(out.shape[0] // steps, width), by_rows(out.shape[0] // steps, width),
            whole(3 * width), whole(heads, taps),
        ]
        + [whole(width)] * 6
        + [whole(share)],
        out_shape=[
            jax.ShapeDtypeStruct((width, 3 * width), F32),
            jax.ShapeDtypeStruct((width, width), F32),
            jax.ShapeDtypeStruct((width, share), F32),
            jax.ShapeDtypeStruct((share, width), F32),
            jax.ShapeDtypeStruct(out.shape, out.dtype),
            jax.ShapeDtypeStruct(gt.shape, gt.dtype),
            jax.ShapeDtypeStruct((3 * width,), F32),
            jax.ShapeDtypeStruct((heads, taps), F32),
        ]
        + [row] * 6
        + [jax.ShapeDtypeStruct((share,), F32)],
        compiler_params=pltpu.CompilerParams(vmem_limit_bytes=60 * 2**20),
        name="spread_out",
    )(grads, grads, up, down, few, out, gt)


def body(
    tokens, segment_ids, w_qkv, b_qkv, conv_kernel, w_out, b_out, norm1_gain, norm1_bias,
    w_up, b_up, w_down, b_down, norm2_gain, norm2_bias, cotangent,
):
    width = tokens.shape[1]
    heads, taps = conv_kernel.shape
    dp_size, tensor_size = lax.axis_size("dp"), lax.axis_size("tensor")
    q, k, v, sq, sk, weight, slope, att, inv, ctx, res, up_all, down_all, bias_all = attend(
        tokens, segment_ids, w_qkv, b_qkv, conv_kernel, w_out, b_out, w_up, w_down, b_up, dp_size, tensor_size
    )
    out, dproj, dctx, gwo, pu, pd, small = feed_forward(
        res, cotangent, ctx, w_out, norm1_gain, norm1_bias, norm2_gain, norm2_bias, b_down, bias_all, up_all, down_all
    )
    gt, grads, grad_up, grad_down, few = attend_back(
        dctx, att, inv, q, k, v, sq, sk, weight, slope, tokens, segment_ids, w_qkv, conv_kernel, dproj,
        gwo, pu, pd, small, dp_size, tensor_size,
    )
    first_lane = (HALO - taps // 2 + BLK - 1 + BLK) % (2 * BLK)
    gw, gwo, grad_up, grad_down, out, gt, gb, grad_conv, gg2, gs2, gbd, gg1, gs1, gbo, gbu = spread_out(
        grads, grad_up, grad_down, few, out, gt, width, heads, taps, first_lane, small.shape[0]
    )
    return (out, gt, gw, gb, grad_conv, gwo, gbo, gg1, gs1, grad_up, gbu, grad_down, gbd, gg2, gs2)


def solution(mesh):
    placed = (
        P(("dp", "tensor"), None),
        P(("dp", "tensor"), None),
        P(), P(), P(), P(), P(), P(), P(),
        P(None, "tensor"),
        P("tensor"),
        P("tensor", None),
        P(), P(), P(),
        P(("dp", "tensor"), None),
    )
    return jax.shard_map(
        body,
        mesh=mesh,
        in_specs=placed,
        out_specs=(
            P(("dp", "tensor"), None),
            P(("dp", "tensor"), None),
            P(), P(), P(), P(), P(), P(), P(),
            P(None, "tensor"),
            P("tensor"),
            P("tensor", None),
            P(), P(), P(),
        ),
        check_vma=False,
    )
```

```python
import functools
import math

import jax
import jax.numpy as jnp
from jax import lax
from jax.experimental import pallas as pl
from jax.experimental.pallas import tpu as pltpu
from jax.sharding import PartitionSpec as P

F32 = jnp.float32
BF16 = jnp.bfloat16
EPS_NORM = 1e-5
EPS_UNIT = 1e-6
SHRINK = 0.95
TAU = 8
SLOPE = TAU / math.pi
ARC = (0.49999996, -0.06830509, 0.02825875, -0.01557005, 0.00864352, -0.00363107, 0.00076235)
QUAD = 256
PAIR = 128
HEAD = 64
BLK = 128
HALO = 64


def dot_nn(a, b):
    return lax.dot_general(a, b, (((1,), (0,)), ((), ())), preferred_element_type=F32)


def dot_nt(a, b):
    return lax.dot_general(a, b, (((1,), (1,)), ((), ())), preferred_element_type=F32)


def dot_tn(a, b):
    return lax.dot_general(a, b, (((0,), (0,)), ((), ())), preferred_element_type=F32)


def lanes(shape):
    return lax.broadcasted_iota(jnp.int32, shape, len(shape) - 1)


def rows(shape):
    return lax.broadcasted_iota(jnp.int32, shape, len(shape) - 2)


def head_sum(values):
    width = values.shape[-1]
    ones = (rows((width, width)) // HEAD == lanes((width, width)) // HEAD).astype(BF16)
    high = values.astype(BF16)
    low = (values - high.astype(F32)).astype(BF16)
    return dot_nn(high, ones) + dot_nn(low, ones)


def closeness_terms(cosine):
    size = jnp.abs(cosine)
    room = 1.0 - size
    inverse = lax.rsqrt(room)
    poly = jnp.full_like(size, ARC[-1])
    for coefficient in ARC[-2::-1]:
        poly = poly * size + coefficient
    small = room * inverse * poly
    close = jnp.where(cosine >= 0.0, 1.0 - small, small)
    two = close * close
    four = two * two
    slope = (four * two) * (close * inverse) * lax.rsqrt(1.0 + size)
    return four * four, slope


def head_mask(half, shape):
    return (lanes(shape) // HEAD == half).astype(BF16)


def window_of(block, blocks):
    low = max(0, block * BLK - 256)
    high = min(blocks * BLK, block * BLK + BLK + 256)
    return low, high


def band(taps, count):
    spread = jnp.broadcast_to(taps, (count, taps.shape[1]))
    return pltpu.roll(spread, 0, 1, stride=1, stride_axis=0)


def norm_stats(values):
    centred = values - jnp.mean(values, -1, keepdims=True)
    scaling = lax.rsqrt(jnp.mean(centred * centred, -1, keepdims=True) + EPS_NORM)
    return centred * scaling, scaling


def segment_rows(seg_ref, row):
    ids = seg_ref[pl.ds(row, 1)].astype(F32)
    edge = jnp.full((1, HALO), -1.0, F32)
    return jnp.concatenate([edge, ids, edge], 1), jnp.broadcast_to(ids, (PAIR, ids.shape[1])).T[:, :1]


def build_same(seg_pad, seg_col, same_ref):
    length = seg_col.shape[0]
    for start in range(0, length, BLK):
        own = seg_col[start : start + BLK]
        same_ref[start : start + BLK, :] = jnp.where(
            own == seg_pad[:, HALO : HALO + length], 1.0, 0.0
        ).astype(BF16)


def build_near(seg_pad, seg_col, near_ref):
    length = seg_col.shape[0]
    for start in range(0, length, BLK):
        own = seg_col[start : start + BLK]
        near_ref[start // BLK] = jnp.where(
            own == seg_pad[:, start : start + 2 * BLK], 1.0, 0.0
        ).astype(BF16)


def place_taps(kernel, reverse):
    taps = kernel.shape[1]
    shape = (taps, 2 * BLK)
    tap = taps - 1 - rows(shape) if reverse else rows(shape)
    return dot_nn(kernel.astype(BF16), (lanes(shape) == tap + HALO - taps // 2).astype(BF16))


def attend_kernel(
    x_ref, seg_ref, wq_ref, wk_ref, wv_ref, b_ref, kernel_ref, wo_ref, bo_ref,
    wu_ref, wd_ref, bu_ref,
    q_ref, k_ref, v_ref, sq_ref, sk_ref, w_ref, s_ref, att_ref, inv_ref, ctx_ref, res_ref,
    up_ref, down_ref, bias_ref,
    same_ref, near_ref, vv_ref, tap_ref, mine_ref, send_sem, recv_sem, copy_sem,
    *, dp_size, tensor_size,
):
    row, quad = pl.program_id(0), pl.program_id(1)
    quads, seqs = pl.num_programs(1), pl.num_programs(0)
    ticks = gather_plan(dp_size, tensor_size, (wu_ref, wd_ref, mine_ref), (up_ref, down_ref, bias_ref), (send_sem, recv_sem), copy_sem)
    length = x_ref.shape[0]
    blocks = length // BLK

    @pl.when((row == 0) & (quad == 0))
    def _():
        tap_ref[...] = place_taps(kernel_ref[...], False)
        mine_ref[...] = bu_ref[...].astype(F32)[None, :]

    @pl.when(quad == 0)
    def _():
        seg_pad, seg_col = segment_rows(seg_ref, row)
        build_same(seg_pad, seg_col, same_ref)
        build_near(seg_pad, seg_col, near_ref)
        for half in range(2):
            edge = jnp.zeros((HALO, 2 * PAIR), BF16)
            vv_ref[half, :HALO] = edge
            vv_ref[half, HALO + length :] = edge
            vv_ref[half, HALO : HALO + length, PAIR:] = head_mask(half, (length, PAIR))

    def bias(part):
        start = pl.multiple_of(part * x_ref.shape[1] + quad * QUAD, QUAD)
        return b_ref[pl.ds(start, QUAD)][None, :]

    for start in range(0, length, ROWS):
        here = slice(start, start + ROWS)
        x = x_ref[here]
        for number, (w, unit, scale, factor) in enumerate(
            ((wq_ref, q_ref, sq_ref, SHRINK), (wk_ref, k_ref, sk_ref, 1.0))
        ):
            part = dot_nn(x, w[...]) + bias(number)
            scaling = lax.rsqrt(head_sum(part * part) + EPS_UNIT)
            unit[here] = (part * (scaling * factor)).astype(BF16)
            scale[here] = scaling.astype(BF16)
        v_ref[here] = (dot_nn(x, wv_ref[...]) + bias(2)).astype(BF16)

    def one_pair(pair, carry):
        turn = (row * quads + quad) * (QUAD // PAIR) + pair
        for when, events in ticks.items():

            @pl.when(turn == when)
            def _(events=events):
                for event in events:
                    event()

        at = pl.ds(pl.multiple_of(pair * PAIR, PAIR), PAIR)
        v = v_ref[:, at]
        for half in range(2):
            vv_ref[half, HALO : HALO + length, :PAIR] = v * head_mask(half, (length, PAIR))
        for block in range(blocks):
            here = slice(block * BLK, block * BLK + BLK)
            low, high = window_of(block, blocks)
            q = q_ref[here, at]
            total = jnp.zeros((BLK, 2 * PAIR), F32)
            near = jnp.zeros((BLK, PAIR), F32)
            for half in range(2):
                head = pair * 2 + half
                q_half = q * head_mask(half, (BLK, PAIR))
                for start in range(low, high, KCH):
                    stop = min(start + KCH, high)
                    cosine = dot_nt(q_half, k_ref[start:stop, at])
                    weight, slope = closeness_terms(cosine)
                    same = same_ref[here, start:stop]
                    weight = weight.astype(BF16) * same
                    w_ref[0, head, here, start:stop] = weight
                    s_ref[0, head, here, start:stop] = slope.astype(BF16) * same
                    total += dot_nn(weight, vv_ref[half, HALO + start : HALO + stop])
                if low > 0:
                    w_ref[0, head, here, :low] = jnp.zeros((BLK, low), BF16)
                if high < length:
                    w_ref[0, head, here, high:] = jnp.zeros((BLK, length - high), BF16)
                taps = band(tap_ref[pl.ds(quad * (QUAD // HEAD) + head, 1)], BLK).astype(BF16) * near_ref[block]
                near += dot_nn(taps, vv_ref[half, block * BLK : block * BLK + 2 * BLK, :PAIR])
            inverse = 1.0 / (1.0 + total[:, PAIR:])
            attended = total[:, :PAIR] * inverse
            att_ref[here, at] = attended.astype(BF16)
            inv_ref[here, at] = inverse.astype(BF16)
            ctx_ref[here, at] = (attended + near).astype(BF16)
        return carry

    lax.fori_loop(0, QUAD // PAIR, one_pair, 0)

    @pl.when(quad == 0)
    def _():
        res_ref[...] = x_ref[...].astype(F32) + bo_ref[...][None, :]

    for start in range(0, length, ROWS):
        here = slice(start, start + ROWS)
        res_ref[here] += dot_nn(ctx_ref[here], wo_ref[...])


def gather_plan(dp_size, tensor_size, own, whole, sems, copy_sem):
    axes = slice_axes(dp_size, tensor_size)
    y, x, core = axes["y"], axes["x"], axes["core"]
    mate = core.device(core.ahead(1))
    number = iter(range(1000))

    def mine(place):
        return place * CORES + core.place

    def half_of(ref, piece):
        size = ref.shape[-2] // 2
        return span(piece % 2 * size, size)

    def rows_at(ref, piece, place):
        size = ref.shape[-2] // (2 * x.size)
        return span(piece % 2 * x.size * size + place * size, size)

    def at_y(piece):
        source, target = own[piece // 2], whole[piece // 2]
        out = []
        for j in range(1, y.size):
            if piece < 4:
                block = rows_at(source, piece, x.place)
                pair = (source.at[block], target.at[mine(y.place), block])
            else:
                pair = (source, target.at[mine(y.place)])
            out.append(send(*pair, sems, next(number), y.device(y.ahead(j))))
        return out

    def at_x(piece):
        target = whole[piece // 2]
        out = []
        for j in range(1, y.size):
            block = target.at[mine(y.ahead(j)), rows_at(target, piece, x.place)]
            out += [send(block, block, sems, next(number), x.device(x.ahead(i))) for i in range(1, x.size)]
        return out

    def to_mate(piece):
        target = whole[piece // 2]
        out = []
        for j in range(1, y.size):
            block = target.at[mine(y.ahead(j))]
            block = block.at[half_of(target, piece)] if piece < 4 else block
            out.append(send(block, block, sems, next(number), mate))
        return out

    keep = [pltpu.make_async_copy(own[i], whole[i].at[mine(y.place)], copy_sem.at[i]) for i in range(3)]
    give = [send(own[i], whole[i].at[mine(y.place)], sems, next(number), mate) for i in range(3)]
    ys, xs, mates = [at_y(i) for i in range(5)], [at_x(i) for i in range(4)], [to_mate(i) for i in range(5)]

    def start(copies):
        return [copy.start for copy in copies]

    def wait(copies):
        return [copy.wait for copy in copies]

    steps = [
        [lambda: greet(axes, ("core", "y", "x"))] + start(ys[0] + ys[1] + ys[4] + give + keep),
        wait(ys[0] + ys[4]) + start(xs[0] + ys[2] + mates[4]),
        wait(ys[1]) + start(xs[1] + ys[3]),
        wait(ys[2] + xs[0]) + start(xs[2] + mates[0]),
        wait(ys[3] + xs[1]) + start(xs[3] + mates[1]),
        wait(xs[2] + xs[3]) + start(mates[2] + mates[3]),
    ]
    last = wait([copy for piece in mates for copy in piece] + give + keep)
    return dict(zip(GATHER_TIMES, steps)) | {GATHER_TIMES[len(steps)]: last}


GATHER_TIMES = (0, 4, 5, 7, 8, 10, 11)


KCH = 256
ROWS = 256


def attend(tokens, segment_ids, w_qkv, b_qkv, kernel, w_out, b_out, w_up, w_down, b_up, dp_size, tensor_size):
    count, width = tokens.shape
    seqs, length = segment_ids.shape
    quads = width // QUAD
    heads = width // HEAD
    per = QUAD // HEAD
    blocks = length // BLK
    own = pl.BlockSpec((length, QUAD), lambda r, p: (r, p))
    act = jax.ShapeDtypeStruct((count, width), BF16)
    big = jax.ShapeDtypeStruct((seqs, heads, length, length), BF16)
    big_spec = pl.BlockSpec((1, per, length, length), lambda r, p: (r, p, 0, 0))

    def part(rows_of, k):
        return pl.BlockSpec((rows_of, QUAD), lambda r, p, k=k: (0, p + k * quads))

    def whole(*shape):
        return pl.BlockSpec(shape, lambda r, p: (0,) * len(shape), pipeline_mode=pl.Buffered(1))

    others = tensor_size // CORES - 1
    copies = 3 + 10 * others + 4 * others * (dp_size // DEPTH - 1)
    return pl.pallas_call(
        functools.partial(attend_kernel, dp_size=dp_size, tensor_size=tensor_size),
        grid=(seqs, quads),
        in_specs=[
            pl.BlockSpec((length, width), lambda r, p: (r, 0)),
            whole(*segment_ids.shape),
            part(width, 0), part(width, 1), part(width, 2),
            whole(*b_qkv.shape),
            whole(*kernel.shape),
            pl.BlockSpec((QUAD, width), lambda r, p: (p, 0)),
            whole(*b_out.shape),
        ]
        + [
            whole(*each.shape) for each in (w_up, w_down, b_up)
        ],
        out_specs=[own] * 5 + [big_spec] * 2 + [own] * 3 + [pl.BlockSpec((length, width), lambda r, p: (r, 0))]
        + [pl.BlockSpec(memory_space=pl.ANY)] * 3,
        out_shape=[act] * 5 + [big] * 2 + [act] * 3 + [jax.ShapeDtypeStruct((count, width), F32)]
        + [jax.ShapeDtypeStruct((tensor_size,) + part.shape, BF16) for part in (w_up, w_down)]
        + [jax.ShapeDtypeStruct((tensor_size, 1, b_up.shape[0]), F32)],
        scratch_shapes=[
            pltpu.VMEM((length, length), BF16),
            pltpu.VMEM((blocks, BLK, 2 * BLK), BF16),
            pltpu.VMEM((2, length + 2 * HALO, 2 * PAIR), BF16),
            pltpu.VMEM((heads, 2 * BLK), F32),
            pltpu.VMEM((1, b_up.shape[0]), F32),
            pltpu.SemaphoreType.DMA((copies,)),
            pltpu.SemaphoreType.DMA((copies,)),
            pltpu.SemaphoreType.DMA((3,)),
        ],
        compiler_params=pltpu.CompilerParams(vmem_limit_bytes=56 * 2**20, collective_id=2, has_side_effects=True),
        name="attend_forward",
    )(tokens, segment_ids, w_qkv, w_qkv, w_qkv, b_qkv, kernel, w_out, b_out, w_up, w_down, b_up)


DEPTH = 4
CORES = 2


class Axis:
    def __init__(self, size, place, device):
        self.size, self.place, self.device = size, place, device

    def ahead(self, j):
        return lax.rem(self.place + j, self.size)


def slice_axes(dp_size, tensor_size):
    dp, tensor = lax.axis_index("dp"), lax.axis_index("tensor")
    across = dp_size // DEPTH
    z, x = dp // across, lax.rem(dp, across)
    y, core = tensor // CORES, lax.rem(tensor, CORES)
    return {
        "core": Axis(CORES, core, lambda p: (dp, y * CORES + p)),
        "y": Axis(tensor_size // CORES, y, lambda p: (dp, p * CORES + core)),
        "x": Axis(across, x, lambda p: (z * across + p, tensor)),
        "z": Axis(DEPTH, z, lambda p: (p * across + x, tensor)),
    }


def greet(axes, names=("core", "y", "x", "z")):
    barrier = pltpu.get_barrier_semaphore()
    count = 0
    for axis in (axes[name] for name in names):
        for j in range(1, axis.size):
            pl.semaphore_signal(
                barrier, inc=1, device_id=axis.device(axis.ahead(j)), device_id_type=pl.DeviceIdType.MESH
            )
            count += 1
    pl.semaphore_wait(barrier, count)


def send(source, target, sems, at, device):
    return pltpu.make_async_remote_copy(
        src_ref=source, dst_ref=target, send_sem=sems[0].at[at], recv_sem=sems[1].at[at],
        device_id=device, device_id_type=pl.DeviceIdType.MESH,
    )


def span(start, size):
    if isinstance(start, int):
        return pl.ds(start, size)
    return pl.ds(pl.multiple_of(start, math.gcd(size, 16)), size)


def add_rows(target, target_at, terms, size):
    tile = next(t for t in (64, 48, 32, 24, 16, 12, 8) if size % t == 0)

    def one(i, carry):
        total = None
        for ref, start in terms:
            rows_of = ref[span(start + i * tile, tile)].astype(F32)
            total = rows_of if total is None else total + rows_of
        target[span(target_at + i * tile, tile)] = total.astype(target.dtype)
        return carry

    lax.fori_loop(0, size // tile, one, 0)


class Reduction:
    def __init__(self, axes, order, back, source, source_at, size, final, final_at, landings, sems, first_sem=0):
        self.axes, self.order, self.back = axes, order, back
        self.source, self.source_at, self.size = source, source_at, size
        self.final, self.final_at = final, final_at
        self.landings, self.sems = landings, sems
        self.first_sem = first_sem

    def plan(self):
        size, at, out = self.size, self.final_at, []
        for name in self.order:
            axis = self.axes[name]
            size //= axis.size
            at = at + axis.place * size
            out.append((axis, size, at))
        return out

    def copies(self, stage):
        stages = self.plan()
        sem = self.first_sem
        for axis, _, _ in stages[:stage]:
            sem += axis.size - 1
        axis, size, _ = stages[stage]
        held, held_at = (self.source, self.source_at) if stage == 0 else (self.landings[stage - 1].at[0], 0)
        return [
            send(
                held.at[span(held_at + axis.ahead(j) * size, size)], self.landings[stage].at[j - 1],
                self.sems, sem + j - 1, axis.device(axis.ahead(j)),
            )
            for j in range(1, axis.size)
        ]

    def settle(self, stage):
        for copy in self.copies(stage):
            copy.wait()
        axis, size, final_at = self.plan()[stage]
        held, held_at = (self.source, self.source_at) if stage == 0 else (self.landings[stage - 1].at[0], 0)
        terms = [(held, held_at + axis.place * size)]
        terms += [(self.landings[stage].at[j - 1], 0) for j in range(1, axis.size)]
        if stage == len(self.order) - 1:
            add_rows(self.final, final_at, terms, size)
        else:
            add_rows(self.landings[stage].at[0], 0, terms, size)

    def gathers(self, which):
        stages = self.plan()
        sem = self.first_sem + sum(axis.size - 1 for axis, _, _ in stages)
        for name in self.back[:which]:
            sem += self.axes[name].size - 1
        depth = self.order.index(self.back[which])
        axis, size, at = stages[depth]
        block = self.final.at[span(at, size)]
        return [send(block, block, self.sems, sem + j - 1, axis.device(axis.ahead(j))) for j in range(1, axis.size)]

    def events(self):
        out = []
        count = len(self.order)

        def begin(copies):
            first = len(copies) // 2
            for copy in copies[first:] + copies[:first]:
                copy.start()

        for stage in range(count):
            def event(stage=stage):
                if stage > 0:
                    self.settle(stage - 1)
                begin(self.copies(stage))

            out.append(event)
        for which in range(len(self.back)):
            def event(which=which):
                if which == 0:
                    self.settle(count - 1)
                else:
                    for copy in self.gathers(which - 1):
                        copy.wait()
                begin(self.gathers(which))

            out.append(event)

        def last():
            for copy in self.gathers(len(self.back) - 1):
                copy.wait()

        out.append(last)
        return out


def landing_shapes(order, sizes, size, columns, dtype):
    shapes = []
    for name in order:
        size //= sizes[name]
        shapes.append(pltpu.VMEM((sizes[name] - 1, size, columns), dtype))
    return shapes


def copies_of(order, back, sizes):
    return sum(sizes[name] - 1 for name in order) + sum(sizes[name] - 1 for name in back)

GELU_A = math.sqrt(2.0 / math.pi)
GELU_B = 0.044715
TILE = 256
UNROLL = 4


def gelu_terms(pre):
    square = pre * pre
    swing = jnp.tanh(pre * (GELU_A + GELU_A * GELU_B * square))
    gate = 0.5 + 0.5 * swing
    steep = GELU_A + 3.0 * GELU_A * GELU_B * square
    return pre * gate, gate + 0.5 * pre * (1.0 - swing * swing) * steep


def norm_backward(grad_out, unit, scaling, gain):
    grad_unit = grad_out * gain
    return scaling * (
        grad_unit
        - jnp.mean(grad_unit, -1, keepdims=True)
        - unit * jnp.mean(grad_unit * unit, -1, keepdims=True)
    )


def column_sum(values):
    return jnp.sum(values, 0, keepdims=True)


def ffn_kernel(
    res_ref, cot_hbm, ctx_hbm, wo_hbm, gain1_ref, shift1_ref, gain2_ref, shift2_ref, bd_ref, bu_ref, wu_ref, wd_ref,
    out_ref, dproj_ref, dctx_ref, gwo_ref, pu_ref, pd_ref, small_ref,
    low_ref, acc_ref, hid_ref, slope_ref, dffn_ref, dpre_ref, sendu_ref, sendd_ref, recvu_ref, recvd_ref, pdown_ref, yland_ref,
    send_sem, recv_sem, cot_ref, ctx_ref, wo_ref, load_sem,
):
    parts = pl.num_programs(0) // 2
    step = pl.program_id(0)
    count, width = res_ref.shape
    share = dpre_ref.shape[1]
    tiles = count // TILE
    f = part_order(step, parts)
    late = jnp.maximum(step - parts, 0)
    heights = parts // CORES
    slot = late // CORES
    dp, tensor = lax.axis_index("dp"), lax.axis_index("tensor")
    height, core = tensor // CORES, lax.rem(tensor, CORES)
    mate = (dp, height * CORES + 1 - core)

    def up_to_mate(which):
        return send(sendu_ref.at[which], recvu_ref.at[which], (send_sem.at[0], recv_sem.at[0]), which, mate)

    def down_to_mate(which):
        return send(sendd_ref.at[which], recvd_ref.at[which], (send_sem.at[1], recv_sem.at[1]), which, mate)

    def to_height(which):
        there = (dp, lax.rem(height + 1 + which, heights) * CORES + core)
        return send(pdown_ref.at[which], yland_ref.at[which], (send_sem.at[2], recv_sem.at[2]), which, there)

    def down_part(late):
        part = part_order(parts + late, parts)
        piece = math.gcd(TILE, share)
        for start in range(0, share, piece):
            cut = slice(start, start + piece)
            yield cut, dot_tn(hid_ref[part, :, cut], dffn_ref[...]).astype(BF16)

    def ready(which):
        down_to_mate(which).wait()
        add_rows(pdown_ref.at[which], 0, [(pdown_ref.at[which], 0), (recvd_ref.at[which], 0)], share)
        if which < heights - 1:
            to_height(which).start()

    loads = [
        pltpu.make_async_copy(source, target, load_sem.at[i])
        for i, (source, target) in enumerate(((cot_hbm, cot_ref), (ctx_hbm, ctx_ref), (wo_hbm, wo_ref)))
    ]

    @pl.when(step == 0)
    def _():
        for load in loads:
            load.start()
        barrier = pltpu.get_barrier_semaphore()
        peers = [mate] + [(dp, lax.rem(height + j, heights) * CORES + core) for j in range(1, heights)]
        for peer in peers:
            pl.semaphore_signal(barrier, inc=1, device_id=peer, device_id_type=pl.DeviceIdType.MESH)
        pl.semaphore_wait(barrier, len(peers))

    def put_row(row, values):
        for i in range(values.shape[1] // PAIR):
            small_ref[pl.ds(row + i, 1)] = values[:, i * PAIR : (i + 1) * PAIR]

    def at(t):
        return pl.ds(pl.multiple_of(t * TILE, TILE), TILE)

    @pl.when(step == 0)
    def _():
        def one(t, carry):
            unit, _ = norm_stats(res_ref[at(t)])
            low_ref[at(t)] = (unit * gain1_ref[...][None, :] + shift1_ref[...][None, :]).astype(BF16)
            acc_ref[at(t)] = jnp.zeros((TILE, width), F32)
            return carry

        lax.fori_loop(0, tiles, one, 0, unroll=UNROLL)

    @pl.when(step < parts)
    def _():
        def one(t, carry):
            pre = dot_nn(low_ref[at(t)], wu_ref[0]) + bu_ref[0].astype(F32)
            hidden, slope = gelu_terms(pre)
            hidden = hidden.astype(BF16)
            hid_ref[f, at(t)] = hidden
            slope_ref[f, at(t)] = slope.astype(BF16)
            acc_ref[at(t)] += dot_nn(hidden, wd_ref[0])
            return carry

        lax.fori_loop(0, tiles, one, 0, unroll=UNROLL)

    @pl.when(step == parts)
    def _():
        loads[0].wait()

        def one(t, sums):
            unit, _ = norm_stats(res_ref[at(t)])
            first = unit * gain1_ref[...][None, :] + shift1_ref[...][None, :]
            unit, scaling = norm_stats(first + acc_ref[at(t)] + bd_ref[...][None, :])
            out_ref[at(t)] = (unit * gain2_ref[...][None, :] + shift2_ref[...][None, :]).astype(BF16)
            grad = cot_ref[at(t)].astype(F32)
            d_res = norm_backward(grad, unit, scaling, gain2_ref[...][None, :])
            d_ffn = d_res.astype(BF16)
            acc_ref[at(t)] = d_res
            dffn_ref[at(t)] = d_ffn
            return (
                sums[0] + column_sum(grad * unit),
                sums[1] + column_sum(grad),
                sums[2] + column_sum(d_ffn.astype(F32)),
            )

        zero = jnp.zeros((1, width), F32)
        sums = lax.fori_loop(0, tiles, one, (zero, zero, zero), unroll=UNROLL)
        small_ref[...] = jnp.zeros_like(small_ref)
        for i, values in enumerate(sums):
            put_row(i * (width // PAIR), values)

        def theirs(which, carry):
            for cut, values in down_part(CORES * which):
                sendd_ref[which, cut] = values
            down_to_mate(which).start()
            return carry

        def ours(which, carry):
            for cut, values in down_part(CORES * which + 1):
                pdown_ref[which, cut] = values
            return carry

        for which in range(heights):
            theirs(which, 0)
            if which > 0:
                ready(which - 1)
            ours(which, 0)

    @pl.when(step >= parts)
    def _():
        def one(t, total):
            d_hidden = dot_nt(dffn_ref[at(t)], wd_ref[0])
            d_pre = (d_hidden * slope_ref[f, at(t)].astype(F32)).astype(BF16)
            dpre_ref[at(t)] = d_pre
            acc_ref[at(t)] += dot_nt(d_pre, wu_ref[0])
            return total + column_sum(d_pre.astype(F32))

        bias = lax.fori_loop(0, tiles, one, jnp.zeros((1, share), F32), unroll=UNROLL)
        put_row(6 * (width // PAIR) + f * (share // PAIR), bias)

        @pl.when(late == 0)
        def _():
            ready(heights - 1)

        @pl.when(lax.rem(late, CORES) == 0)
        def _():
            for start in range(0, width, TILE):
                cut = slice(start, start + TILE)
                sendu_ref[slot, cut] = dot_tn(low_ref[:, cut], dpre_ref[...]).astype(BF16)
            up_to_mate(slot).start()

        @pl.when(lax.rem(late, CORES) == 1)
        def _():
            up_to_mate(slot).wait()
            for start in range(0, width, TILE):
                cut = slice(start, start + TILE)
                values = dot_tn(low_ref[:, cut], dpre_ref[...])
                pu_ref[slot, cut] = (values + recvu_ref[slot, cut].astype(F32)).astype(BF16)

    @pl.when(step == 2 * parts - 1)
    def _():
        loads[1].wait()
        loads[2].wait()

        def one(t, sums):
            unit, scaling = norm_stats(res_ref[at(t)])
            grad = acc_ref[at(t)]
            d_proj = norm_backward(grad, unit, scaling, gain1_ref[...][None, :]).astype(BF16)
            dproj_ref[at(t)] = d_proj
            dctx_ref[at(t)] = dot_nt(d_proj, wo_ref[...]).astype(BF16)
            return (
                sums[0] + column_sum(grad * unit),
                sums[1] + column_sum(grad),
                sums[2] + column_sum(d_proj.astype(F32)),
            )

        zero = jnp.zeros((1, width), F32)
        sums = lax.fori_loop(0, tiles, one, (zero, zero, zero), unroll=UNROLL)
        for i, values in enumerate(sums):
            put_row((3 + i) * (width // PAIR), values)
        for start in range(0, width, TILE):
            values = dot_tn(ctx_ref[:, start : start + TILE], dproj_ref[...]).astype(BF16)
            gwo_ref[start : start + TILE] = values[:, : width // 2]
            gwo_ref[width + start : width + start + TILE] = values[:, width // 2 :]
        for which in range(heights - 1):
            to_height(which).wait()
        terms = [(pdown_ref.at[heights - 1], 0)] + [(yland_ref.at[which], 0) for which in range(heights - 1)]
        add_rows(pd_ref, 0, terms, share)


def part_order(step, parts):
    tensor = lax.axis_index("tensor")
    height, core = tensor // CORES, lax.rem(tensor, CORES)
    late = jnp.maximum(step - parts, 0)
    there = lax.rem(height + 1 + late // CORES, parts // CORES)
    whose = jnp.where(lax.rem(late, CORES) == 0, 1 - core, core)
    return jnp.where(step < parts, step, there * CORES + whose)


def feed_forward(res, cot, ctx, w_out, gain1, shift1, gain2, shift2, b_down, b_up, w_up, w_down):
    count, width = res.shape
    parts, _, share = w_up.shape
    heights = parts // 2
    smalls = 6 * width // PAIR + parts * share // PAIR
    smalls = -(-smalls // 8) * 8

    def whole(*shape):
        return pl.BlockSpec(shape, lambda s: (0,) * len(shape), pipeline_mode=pl.Buffered(1))

    def per_part(*shape):
        return pl.BlockSpec((1,) + shape, lambda s: (part_order(s, parts),) + (0,) * len(shape))

    act = jax.ShapeDtypeStruct((count, width), BF16)
    return pl.pallas_call(
        ffn_kernel,
        grid=(2 * parts,),
        in_specs=[whole(count, width)]
        + [pl.BlockSpec(memory_space=pl.ANY)] * 3
        + [whole(width)] * 5
        + [per_part(1, share), per_part(width, share), per_part(share, width)],
        out_specs=[whole(count, width)] * 3
        + [whole(2 * width, width // 2), whole(heights, width, share), whole(share, width), whole(smalls, PAIR)],
        out_shape=[act] * 3
        + [
            jax.ShapeDtypeStruct((2 * width, width // 2), BF16),
            jax.ShapeDtypeStruct((heights, width, share), BF16),
            jax.ShapeDtypeStruct((share, width), BF16),
            jax.ShapeDtypeStruct((smalls, PAIR), F32),
        ],
        scratch_shapes=[
            pltpu.VMEM((count, width), BF16),
            pltpu.VMEM((count, width), F32),
            pltpu.VMEM((parts, count, share), BF16),
            pltpu.VMEM((parts, count, share), BF16),
            pltpu.VMEM((count, width), BF16),
            pltpu.VMEM((count, share), BF16),
            pltpu.VMEM((heights, width, share), BF16),
            pltpu.VMEM((heights, share, width), BF16),
            pltpu.VMEM((heights, width, share), BF16),
            pltpu.VMEM((heights, share, width), BF16),
            pltpu.VMEM((heights, share, width), BF16),
            pltpu.VMEM((heights - 1, share, width), BF16),
            pltpu.SemaphoreType.DMA((3, heights)),
            pltpu.SemaphoreType.DMA((3, heights)),
            pltpu.VMEM((count, width), BF16),
            pltpu.VMEM((count, width), BF16),
            pltpu.VMEM((width, width), BF16),
            pltpu.SemaphoreType.DMA((3,)),
        ],
        compiler_params=pltpu.CompilerParams(vmem_limit_bytes=60 * 2**20, collective_id=0, has_side_effects=True),
        name="feed_forward",
    )(res, cot, ctx, w_out, gain1, shift1, gain2, shift2, b_down, b_up, w_up, w_down)


def attend_back_kernel(
    dctx_ref, att_ref, inv_ref, q_ref, k_ref, v_ref, sq_ref, sk_ref, w_ref, s_ref, x_ref, seg_ref,
    wqkv_hbm, kernel_ref, dproj_ref, gwo_ref, pu_ref, pd_ref, small_ref,
    gt_ref, all_out, up_out, down_out, few_out,
    near_ref, vv_ref, dpad_ref, dcos_ref, dq_ref, dk_ref, dv_ref, joined_ref, gwacc_ref, conv_ref,
    gwlow_ref, gb_ref, flip_ref, mini_ref, all_ref, up_ref, down_ref, few_ref, out_sem, wqkv_ref, load_sem, *links,
    plan, quads, seqs,
):
    quad, row = pl.program_id(0), pl.program_id(1)
    length = x_ref.shape[0]
    blocks = length // BLK
    inside = slice(HALO, HALO + length)

    _, sizes, dp_size, tensor_size = plan
    axes = slice_axes(dp_size, tensor_size)
    ticks = schedule(axes, sizes, quads, seqs, gwo_ref, pu_ref, pd_ref, gwlow_ref, mini_ref, all_ref, up_ref, down_ref, few_ref, links,
        (all_out, up_out, down_out, few_out, out_sem))
    calls = quads * seqs * (QUAD // HEAD)

    build_near(*segment_rows(seg_ref, row), near_ref)
    for half in range(2):
        edge = jnp.zeros((HALO, PAIR), BF16)
        for ref in (vv_ref, dpad_ref):
            ref[half, :HALO, :PAIR] = edge
            ref[half, HALO + length :, :PAIR] = edge
        vv_ref[half, inside, PAIR:] = head_mask(half, (length, PAIR))

    @pl.when(row == 0)
    def _():
        conv_ref[...] = jnp.zeros_like(conv_ref)
        gwacc_ref[...] = jnp.zeros_like(gwacc_ref)

    load = pltpu.make_async_copy(wqkv_hbm, wqkv_ref, load_sem)

    @pl.when((quad == 0) & (row == 0))
    def _():
        load.start()
        gb_ref[...] = jnp.zeros_like(gb_ref)
        flip_ref[...] = place_taps(kernel_ref[...], True)
        mini_ref[...] = jnp.zeros_like(mini_ref)
        mini_ref[: small_ref.shape[0]] = small_ref[...]
        filled = 2 * gwacc_ref.shape[0]
        if gwlow_ref.shape[1] > filled:
            gwlow_ref[:, filled:] = jnp.zeros((quads, gwlow_ref.shape[1] - filled, gwlow_ref.shape[2]), BF16)

    def one_pair(pair, carry):
        at = pl.ds(pl.multiple_of(pair * PAIR, PAIR), PAIR)
        inverse = inv_ref[:, at].astype(F32)
        d_ctx = dctx_ref[:, at]
        d_summed = (d_ctx.astype(F32) * inverse).astype(BF16)
        d_total = (-d_summed.astype(F32) * att_ref[:, at].astype(F32)).astype(BF16)
        both = jnp.concatenate([d_summed, d_total], 1)
        dk = jnp.zeros((PAIR, length), F32)
        dv = jnp.zeros((PAIR, length), F32)
        turn = (quad * seqs + row) * (QUAD // PAIR) + pair
        for half in range(2):
            for when in range(half, calls, 2):
                if ticks.get(when):

                    @pl.when(turn == when // 2)
                    def _(when=when):
                        for event in ticks[when]:
                            event()

            head = pair * 2 + half
            mask = head_mask(half, (length, PAIR))
            vv_ref[half, inside, :PAIR] = v_ref[:, at] * mask
            dpad_ref[half, inside] = d_ctx * mask
            k_half = k_ref[:, at] * mask
            for block in range(blocks):
                here = slice(block * BLK, block * BLK + BLK)
                low, high = window_of(block, blocks)
                d_weight = dot_nt(both[here], vv_ref[half, HALO + low : HALO + high])
                d_cos = d_weight.astype(BF16) * s_ref[0, head, here, low:high]
                dcos_ref[here, low:high] = d_cos
                if low > 0:
                    dcos_ref[here, :low] = jnp.zeros((BLK, low), BF16)
                if high < length:
                    dcos_ref[here, high:] = jnp.zeros((BLK, length - high), BF16)
                grown = dot_nn(d_cos, k_half[low:high])
                if half == 0:
                    dq_ref[here] = grown
                else:
                    dq_ref[here] += grown
                window = slice(block * BLK, block * BLK + 2 * BLK)
                near = near_ref[block]
                taps = band(flip_ref[pl.ds(quad * (QUAD // HEAD) + head, 1)], BLK).astype(BF16) * near
                grown = dot_nn(taps, dpad_ref[half, window])
                if half == 0:
                    dv_ref[here] = grown
                else:
                    dv_ref[here] += grown
                conv_ref[head] += near.astype(F32) * dot_nt(d_ctx[here], vv_ref[half, window, :PAIR])
            dk += dot_tn(q_ref[:, at] * mask, dcos_ref[...])
            dv += dot_tn(d_summed * mask, w_ref[0, head])
        dv_ref[...] += dv.T
        grad = SLOPE * dq_ref[...]
        unit = q_ref[:, at].astype(F32)
        d_query = sq_ref[:, at].astype(F32) * (SHRINK * grad - unit * (head_sum(grad * unit) / SHRINK))
        grad = SLOPE * dk.T
        unit = k_ref[:, at].astype(F32)
        d_key = sk_ref[:, at].astype(F32) * (grad - unit * head_sum(grad * unit))
        for part, values in enumerate((d_query, d_key, dv_ref[...])):
            joined_ref[quad, row, :, pl.ds(pl.multiple_of(part * QUAD + pair * PAIR, PAIR), PAIR)] = values.astype(BF16)
        return carry

    lax.fori_loop(0, QUAD // PAIR, one_pair, 0)

    gb_ref[quad, :1] += column_sum(joined_ref[quad, row].astype(F32))
    width = gwacc_ref.shape[0]
    for start in range(0, width, TILE):
        cut = slice(start, start + TILE)
        gwacc_ref[cut] += dot_tn(x_ref[:, cut], joined_ref[quad, row])

    @pl.when(row == seqs - 1)
    def _():
        half = gwacc_ref.shape[1] // 2
        for start in range(0, width, TILE):
            for side in range(2):
                values = gwacc_ref[start : start + TILE, side * half : (side + 1) * half]
                gwlow_ref[quad, side * width + start : side * width + start + TILE] = values.astype(BF16)
        base = small_ref.shape[0]
        lines = gb_ref.shape[2] // PAIR
        for i in range(lines):
            mini_ref[pl.ds(base + quad * lines + i, 1)] = gb_ref[quad, :1, i * PAIR : (i + 1) * PAIR]
        base += quads * lines
        for head in range(QUAD // HEAD):
            sums = conv_ref[head]
            high = sums.astype(BF16)
            turn = (rows((BLK, BLK)) + lanes((BLK, BLK)) == BLK - 1).astype(BF16)
            turned = dot_nn(turn, high) + dot_nn(turn, (sums - high.astype(F32)).astype(BF16))
            turned = pltpu.roll(turned, BLK, 1, stride=1, stride_axis=0)
            mini_ref[pl.ds(base + quad * (QUAD // HEAD) + head, 1)] = column_sum(turned)[:, :PAIR]

    last = (quad == quads - 1) & (row == seqs - 1)

    @pl.when(last)
    def _():
        for event in ticks.get(calls, ()):
            event()

    @pl.when((quad == quads - 1) & (row == 0))
    def _():
        load.wait()

    @pl.when(quad == quads - 1)
    def _():
        for start in range(0, length, TILE):
            cut = slice(start, start + TILE)
            grown = dproj_ref[cut].astype(F32)
            for q in range(quads):
                for part in range(3):
                    to = part * width + q * QUAD
                    grown += dot_nt(joined_ref[q, row, cut, part * QUAD : (part + 1) * QUAD], wqkv_ref[:, to : to + QUAD])
            gt_ref[cut] = grown.astype(BF16)

    @pl.when(last)
    def _():
        for when in sorted(ticks):
            if when > calls:
                for event in ticks[when]:
                    event()


FFN_PLAN = (
    (
        (("z", "x"), (1, 28, 42, 44, 57)),
        (("x", "z"), (1, 7, 14, 38, 48)),
    ),
    (
        (("x", "z"), (0, 8, 13, 17, 24, 36)),
        (("x", "z"), (6, 16, 23, 42, 48, 55)),
    ),
)
ALL_PLAN = (
    (
        (3, 1, (2, 4, 13, 16, 21, 27, 33, 43, 54)),
    ),
    (
        (3, 0, (13, 18, 24, 29, 31, 41, 43, 51, 53)),
    ),
    (
        (3, 1, (17, 18, 23, 26, 29, 34, 41, 46, 47)),
    ),
    (
        (3, 1, (24, 25, 30, 35, 39, 42, 45, 50, 52)),
    ),
)
MINI_ORDER = 1
MINI_TIMES = (29, 31, 32, 37, 40, 42, 49, 52, 56)
FFN_ROWS = 384
ORDERS = (("core", "x", "y", "z"), ("core", "y", "x", "z"))


def all_parts(index, size, devices):
    parts = ALL_PLAN[index]
    if sum(units for units, _, _ in parts) * 16 * devices != size:
        parts = ((size // (16 * devices), parts[-1][1], parts[-1][2]),)
    out, start = [], 0
    for units, order, times in parts:
        rows_of = units * 16 * devices
        out.append((start, rows_of, ORDERS[order], times))
        start += rows_of
    return out


class FfnReduction(Reduction):
    def copies(self, stage):
        if stage > 0:
            return super().copies(stage)
        axis = self.axes["y"]
        return [
            send(
                self.source.at[j - 1, span(self.source_at, self.size)], self.landings[0].at[j - 1],
                self.sems, self.first_sem + j - 1, axis.device(axis.ahead(j)),
            )
            for j in range(1, axis.size)
        ]

    def plan(self):
        size, at = self.size, self.final_at
        out = [(self.axes["y"], size, at)]
        for name in self.order[1:]:
            axis = self.axes[name]
            size //= axis.size
            at = at + axis.place * size
            out.append((axis, size, at))
        return out

    def settle(self, stage):
        if stage > 0:
            return super().settle(stage)
        axis = self.axes["y"]
        for copy in self.copies(0):
            copy.wait()
        terms = [(self.source.at[axis.size - 1], self.source_at)]
        terms += [(self.landings[0].at[j - 1], 0) for j in range(1, axis.size)]
        add_rows(self.landings[0].at[0], 0, terms, self.size)


def link_plan(sizes, width, share, quads):
    out = []
    devices = math.prod(sizes.values())
    y = sizes["y"]
    for late, (height, columns) in enumerate(((share, width), (width, share))):
        for start in range(0, height, FFN_ROWS):
            order = FFN_PLAN[late][start // FFN_ROWS][0]
            shapes = [pltpu.VMEM((y - 1, FFN_ROWS, columns), BF16)] if late else []
            shapes += landing_shapes(order, sizes, FFN_ROWS, columns, BF16)
            out.append((shapes, copies_of((("y",) if late else ()) + order, order, sizes)))
    size = padded(2 * width, devices)
    for index in range(quads + 1):
        for _, rows_of, order, _ in all_parts(index, size, devices):
            out.append((landing_shapes(order, sizes, rows_of, width // 2, BF16), copies_of(order, order, sizes)))
    order = ORDERS[MINI_ORDER]
    out.append((landing_shapes(order, sizes, 8 * devices, PAIR, F32), copies_of(order, order, sizes)))
    return out


def padded(size, devices):
    return -(-size // (16 * devices)) * 16 * devices


def schedule(axes, sizes, quads, seqs, gwo_ref, pu_ref, pd_ref, gwlow_ref, mini_ref, all_ref, up_ref, down_ref, few_ref, links, outs):
    all_out, up_out, down_out, few_out, out_sem = outs
    calls = quads * seqs * (QUAD // HEAD)
    share, width = pd_ref.shape
    devices = math.prod(sizes.values())
    groups = link_plan(sizes, width, share, quads)
    taken, position = [], 0
    for shapes, _ in groups:
        taken.append((links[position : position + len(shapes)], links[position + len(shapes) : position + len(shapes) + 2]))
        position += len(shapes) + 2
    ticks = {0: [lambda: greet(axes)]}

    stores = []

    def enlist(reduction, times, done, place):
        for time, event in zip(times, reduction.events(), strict=True):
            ticks.setdefault(time, []).append(event)
        store = pltpu.make_async_copy(done, place, out_sem.at[len(stores)])
        ticks[times[-1]].append(store.start)
        stores.append(store)

    number = 0
    for late, (source, final, place) in enumerate(((pd_ref, down_ref, down_out), (pu_ref, up_ref, up_out))):
        for start in range(0, final.shape[0], FFN_ROWS):
            landings, sems = taken[number]
            block = span(start, FFN_ROWS)
            order, times = FFN_PLAN[late][start // FFN_ROWS]
            kind = FfnReduction if late else Reduction
            whole_order = ("y",) + order if late else order
            reduction = kind(axes, whole_order, order[::-1], source, start, FFN_ROWS, final, start, landings, sems)
            enlist(reduction, times, final.at[block], place.at[block])
            number += 1
    size = padded(2 * width, devices)
    for index in range(quads + 1):
        source = gwo_ref if index == 0 else gwlow_ref.at[index - 1]
        for start, rows_of, order, times in all_parts(index, size, devices):
            landings, sems = taken[number]
            final = all_ref.at[index]
            reduction = Reduction(axes, order, order[::-1], source, start, rows_of, final, start, landings, sems)
            enlist(reduction, times, final.at[span(start, rows_of)], all_out.at[index, span(start, rows_of)])
            number += 1
    landings, sems = taken[number]
    order = ORDERS[MINI_ORDER]
    reduction = Reduction(axes, order, order[::-1], mini_ref, 0, 8 * devices, few_ref, 0, landings, sems)
    enlist(reduction, MINI_TIMES, few_ref, few_out)
    ticks[max(ticks) + 1] = [store.wait for store in stores]
    return ticks


def attend_back(dctx, att, inv, q, k, v, sq, sk, weight, slope, tokens, segment_ids, w_qkv, kernel, dproj, gwo, pu, pd, small, dp_size, tensor_size):
    count, width = tokens.shape
    seqs, length = segment_ids.shape
    quads = width // QUAD
    per = QUAD // HEAD
    blocks = length // BLK
    own = pl.BlockSpec((length, QUAD), lambda p, r: (r, p))
    big = pl.BlockSpec((1, per, length, length), lambda p, r: (r, p, 0, 0))
    wide = pl.BlockSpec((length, width), lambda p, r: (r, 0))

    sizes = {"core": CORES, "y": tensor_size // CORES, "x": dp_size // DEPTH, "z": DEPTH}
    devices = dp_size * tensor_size
    share = pd.shape[0]
    grown = padded(2 * width, devices)
    gwo = jnp.pad(gwo, ((0, grown - gwo.shape[0]), (0, 0)))
    minis = 8 * devices
    scratch = []
    for shapes, count_of in link_plan(sizes, width, share, quads):
        scratch += shapes + [pltpu.SemaphoreType.DMA((count_of,)), pltpu.SemaphoreType.DMA((count_of,))]

    def whole(*shape):
        return pl.BlockSpec(shape, lambda p, r: (0,) * len(shape), pipeline_mode=pl.Buffered(1))

    return pl.pallas_call(
        functools.partial(attend_back_kernel, plan=(None, sizes, dp_size, tensor_size), quads=quads, seqs=seqs),
        grid=(quads, seqs),
        in_specs=[own] * 8
        + [big] * 2
        + [
            wide,
            whole(*segment_ids.shape),
            pl.BlockSpec(memory_space=pl.ANY),
            whole(*kernel.shape),
            wide,
            whole(*gwo.shape), whole(*pu.shape), whole(*pd.shape), whole(*small.shape),
        ],
        out_specs=[
            pl.BlockSpec((length, width), lambda p, r: (jnp.where(p == quads - 1, r, 0), 0)),
        ]
        + [pl.BlockSpec(memory_space=pl.ANY)] * 4,
        out_shape=[
            jax.ShapeDtypeStruct((count, width), BF16),
            jax.ShapeDtypeStruct((quads + 1, grown, width // 2), BF16),
            jax.ShapeDtypeStruct((width, share), BF16),
            jax.ShapeDtypeStruct((share, width), BF16),
            jax.ShapeDtypeStruct((minis, PAIR), F32),
        ],
        scratch_shapes=[
            pltpu.VMEM((blocks, BLK, 2 * BLK), BF16),
            pltpu.VMEM((2, length + 2 * HALO, 2 * PAIR), BF16),
            pltpu.VMEM((2, length + 2 * HALO, PAIR), BF16),
            pltpu.VMEM((length, length), BF16),
            pltpu.VMEM((length, PAIR), F32),
            pltpu.VMEM((length, PAIR), F32),
            pltpu.VMEM((length, PAIR), F32),
            pltpu.VMEM((quads, seqs, length, 3 * QUAD), BF16),
            pltpu.VMEM((width, 3 * QUAD), F32),
            pltpu.VMEM((per, BLK, 2 * BLK), F32),
            pltpu.VMEM((quads, grown, width // 2), BF16),
            pltpu.VMEM((quads, 8, 3 * QUAD), F32),
            pltpu.VMEM((width // HEAD, 2 * BLK), F32),
            pltpu.VMEM((minis, PAIR), F32),
            pltpu.VMEM((quads + 1, grown, width // 2), BF16),
            pltpu.VMEM((width, share), BF16),
            pltpu.VMEM((share, width), BF16),
            pltpu.VMEM((minis, PAIR), F32),
            pltpu.SemaphoreType.DMA((len(link_plan(sizes, width, share, quads)),)),
            pltpu.VMEM((width, 3 * width), BF16),
            pltpu.SemaphoreType.DMA,
        ]
        + scratch,
        compiler_params=pltpu.CompilerParams(vmem_limit_bytes=60 * 2**20, collective_id=1, has_side_effects=True),
        name="attend_backward",
    )(dctx, att, inv, q, k, v, sq, sk, weight, slope, tokens, segment_ids, w_qkv, kernel, dproj, gwo, pu, pd, small)


def spread_kernel(low_ref, high_ref, up_ref, down_ref, few_ref, a_ref, b_ref, gw_ref, gwo_ref, gup_ref, gdown_ref, a_out, b_out, *vectors, first_lane, base):
    width = gwo_ref.shape[1]
    half = width // 2
    quads = low_ref.shape[0] - 1
    gwo_ref[:, :half] = low_ref[0].astype(F32)
    gwo_ref[:, half:] = high_ref[0].astype(F32)
    for quad in range(quads):
        for part in range(3):
            for start in range(part * QUAD, (part + 1) * QUAD, PAIR):
                side, lane = (low_ref, start) if start < half else (high_ref, start - half)
                to = part * width + quad * QUAD + start - part * QUAD
                gw_ref[:, to : to + PAIR] = side[1 + quad, :, lane : lane + PAIR].astype(F32)
    a_out[...] = a_ref[...]
    b_out[...] = b_ref[...]
    gup_ref[...] = up_ref[...].astype(F32)
    gdown_ref[...] = down_ref[...].astype(F32)

    @pl.when(pl.program_id(0) == 0)
    def _():
        gb_ref, conv_ref, *six, gbu_ref = vectors
        lines = width // PAIR

        def copy_line(target, to, line):
            target[to * PAIR : (to + 1) * PAIR] = few_ref[line]

        for number, target in enumerate(six):
            for i in range(lines):
                copy_line(target, i, number * lines + i)
        share = gbu_ref.shape[0] // PAIR
        mine = lax.axis_index("tensor") * share
        for i in range(share):
            copy_line(gbu_ref, i, 6 * lines + mine + i)
        per = QUAD // PAIR
        for quad in range(quads):
            for part in range(3):
                for i in range(per):
                    copy_line(gb_ref, (part * width + quad * QUAD) // PAIR + i, base + (quad * 3 + part) * per + i)
        heads, taps = conv_ref.shape
        kept = few_ref[base + 3 * lines : base + 3 * lines + heads]
        conv_ref[...] = pltpu.roll(kept, PAIR - first_lane, 1)[:, :taps]


def spread_out(grads, up, down, few, out, gt, width, heads, taps, first_lane, base):
    chunks = grads.shape[0]
    quads = chunks - 1
    steps = 16
    rows_of = width // steps
    share = up.shape[1]
    down_rows = share // steps

    def whole(*shape):
        return pl.BlockSpec(shape, lambda s: (0,) * len(shape))

    def by_rows(count, columns):
        return pl.BlockSpec((count, columns), lambda s: (s, 0))

    row = jax.ShapeDtypeStruct((width,), F32)
    return pl.pallas_call(
        functools.partial(spread_kernel, first_lane=first_lane, base=base),
        grid=(steps,),
        in_specs=[
            pl.BlockSpec((chunks, rows_of, width // 2), lambda s: (0, s, 0)),
            pl.BlockSpec((chunks, rows_of, width // 2), lambda s: (0, steps + s, 0)),
            by_rows(rows_of, share),
            by_rows(down_rows, width),
            whole(*few.shape),
            by_rows(out.shape[0] // steps, width), by_rows(out.shape[0] // steps, width),
        ],
        out_specs=[
            by_rows(rows_of, 3 * width), by_rows(rows_of, width), by_rows(rows_of, share), by_rows(down_rows, width),
            by_rows(out.shape[0] // steps, width), by_rows(out.shape[0] // steps, width),
            whole(3 * width), whole(heads, taps),
        ]
        + [whole(width)] * 6
        + [whole(share)],
        out_shape=[
            jax.ShapeDtypeStruct((width, 3 * width), F32),
            jax.ShapeDtypeStruct((width, width), F32),
            jax.ShapeDtypeStruct((width, share), F32),
            jax.ShapeDtypeStruct((share, width), F32),
            jax.ShapeDtypeStruct(out.shape, out.dtype),
            jax.ShapeDtypeStruct(gt.shape, gt.dtype),
            jax.ShapeDtypeStruct((3 * width,), F32),
            jax.ShapeDtypeStruct((heads, taps), F32),
        ]
        + [row] * 6
        + [jax.ShapeDtypeStruct((share,), F32)],
        compiler_params=pltpu.CompilerParams(vmem_limit_bytes=60 * 2**20),
        name="spread_out",
    )(grads, grads, up, down, few, out, gt)


def body(
    tokens, segment_ids, w_qkv, b_qkv, conv_kernel, w_out, b_out, norm1_gain, norm1_bias,
    w_up, b_up, w_down, b_down, norm2_gain, norm2_bias, cotangent,
):
    width = tokens.shape[1]
    heads, taps = conv_kernel.shape
    dp_size, tensor_size = lax.axis_size("dp"), lax.axis_size("tensor")
    q, k, v, sq, sk, weight, slope, att, inv, ctx, res, up_all, down_all, bias_all = attend(
        tokens, segment_ids, w_qkv, b_qkv, conv_kernel, w_out, b_out, w_up, w_down, b_up, dp_size, tensor_size
    )
    out, dproj, dctx, gwo, pu, pd, small = feed_forward(
        res, cotangent, ctx, w_out, norm1_gain, norm1_bias, norm2_gain, norm2_bias, b_down, bias_all, up_all, down_all
    )
    gt, grads, grad_up, grad_down, few = attend_back(
        dctx, att, inv, q, k, v, sq, sk, weight, slope, tokens, segment_ids, w_qkv, conv_kernel, dproj,
        gwo, pu, pd, small, dp_size, tensor_size,
    )
    first_lane = (HALO - taps // 2 + BLK - 1 + BLK) % (2 * BLK)
    gw, gwo, grad_up, grad_down, out, gt, gb, grad_conv, gg2, gs2, gbd, gg1, gs1, gbo, gbu = spread_out(
        grads, grad_up, grad_down, few, out, gt, width, heads, taps, first_lane, small.shape[0]
    )
    return (out, gt, gw, gb, grad_conv, gwo, gbo, gg1, gs1, grad_up, gbu, grad_down, gbd, gg2, gs2)


def solution(mesh):
    placed = (
        P(("dp", "tensor"), None),
        P(("dp", "tensor"), None),
        P(), P(), P(), P(), P(), P(), P(),
        P(None, "tensor"),
        P("tensor"),
        P("tensor", None),
        P(), P(), P(),
        P(("dp", "tensor"), None),
    )
    return jax.shard_map(
        body,
        mesh=mesh,
        in_specs=placed,
        out_specs=(
            P(("dp", "tensor"), None),
            P(("dp", "tensor"), None),
            P(), P(), P(), P(), P(), P(), P(),
            P(None, "tensor"),
            P("tensor"),
            P("tensor", None),
            P(), P(), P(),
        ),
        check_vma=False,
    )
```
